128 devices in a mesh: grp: 4 (over y), dev: 32 (over z, x, core).
Axes of the slice: x: 4, y: 4, z: 4, core: 2. Of those that a mesh axis runs over, the one named last changes fastest.
Arguments:
- points: float32 [64, 196608], P(None, 'dev'), may hold values from -6 to 6
- weights: float32 [196608, 128], P('dev'), may hold values from -4 to 4
- proj: float32 [256, 196608], P(None, 'dev'), may hold values from -0.078125 to 0.078125
- fetch_table: int32 [3, 32, 32, 2], P(None, 'dev'), may hold values from 0 to 11, as said below
- near_list: int32 [384, 16], P('dev'), may hold values from 0 to 63, as said below
- far_list: int32 [384, 8], P('dev'), may hold values from 0 to 31, as said below
- skel_idx: int32 [32, 256], P('dev'), may hold values from 0 to 6143, as said below
Outputs:
- potential: float32 [196608, 128], P('dev')
The draws below stay inside these ranges and needn't reach their ends.
Inputs may be any that keep to these rules, and one draw needn't show every extreme that they name: Entries of fetch_table[r, d, e] are distinct local leaf numbers of column e. `near_list`: the 16 slots of one target leaf are distinct. `far_list`: the 8 nodes of one target leaf are distinct, and one of them is node (c + 1) mod 32 for the leaf's column c. `skel_idx`: the 256 skeleton points of one node are distinct.
All inputs are finite; a program needn't handle non-finite values.
Results may differ from the reference program's by a relative error of at most 0.0003.
Values sent between devices are 32-bit elements; how exact they have to be, the bound alone decides.
A program may use at most 192 MiB of HBM per device.

```python
import jax
import jax.numpy as jnp
from jax import lax

DIM = 64
WCOL = 128
LEAF = 512
SKEL = 256
Q = 4
NEAR = 16
FAR = 8
CAP = 2
TGT_DEV = 12
NLEAF = 384
COLPTS = 6144
NPTS = 196608
N_GRP = 4
N_DEV = 32


def distinct_pick(key, leading, count, chosen):
    scores = jax.random.randint(key, leading + (count,), 0, 1 << 16) * count
    scores = scores + jnp.arange(count, dtype=jnp.int32)
    return jnp.argsort(scores, axis=-1)[..., :chosen].astype(jnp.int32)


def draw_fetch_table(key, part):
    return distinct_pick(jax.random.fold_in(key, 11), (N_GRP - 1, N_DEV, N_DEV), TGT_DEV, CAP)


def draw_near_list(key, part):
    return distinct_pick(jax.random.fold_in(key, 12), (NLEAF,), N_DEV * CAP, NEAR)


def draw_far_list(key, part):
    column = (jnp.arange(NLEAF, dtype=jnp.int32) // TGT_DEV)[:, None]
    others = distinct_pick(jax.random.fold_in(key, 13), (NLEAF,), N_DEV - 1, FAR - 1)
    others = (column + 2 + others) % N_DEV
    following = (column + 1) % N_DEV
    return jnp.concatenate([following, others], axis=1).astype(jnp.int32)


def draw_skel_idx(key, part):
    return distinct_pick(jax.random.fold_in(key, 14), (N_DEV,), TGT_DEV * LEAF, SKEL)


def level_of(own_key, extent, shards, least, top_value):
    loudness, own = 1.0, jax.random.fold_in(own_key, 6)
    for dim, parts in shards:
        steps = jnp.exp(jax.random.uniform(jax.random.fold_in(own, dim), (parts,), jnp.float32, least / len(shards), top_value / len(shards)))
        loudness = loudness * jnp.repeat(steps, extent[dim] // parts).reshape([-1 if axis == dim else 1 for axis in range(len(extent))])
    return loudness


def noise(key, extent, spread, limit, shards=(), held_as=jnp.bfloat16):
    factor_of = level_of(key, extent, shards, -0.22, 0.18) if shards else 1.0
    array = jax.random.normal(key, extent, jnp.float32) * spread * factor_of
    return jnp.minimum(jnp.maximum(array, -limit), limit).astype(held_as)


def setup_inputs(seed: int = 0) -> dict:
    keys = jax.random.split(jax.random.key(seed), 8)
    return {
        "points": noise(keys[0], (DIM, NPTS), 1.0, 6.0, ((1, 32),), jnp.float32),
        "weights": noise(keys[1], (NPTS, WCOL), 0.5, 4.0, ((0, 32),), jnp.float32),
        "proj": noise(keys[2], (SKEL, NPTS), (TGT_DEV * LEAF) ** -0.5, 0.078125, ((1, 32),), jnp.float32),
        "fetch_table": draw_fetch_table(jax.random.fold_in(keys[7], 71), 0),
        "near_list": draw_near_list(jax.random.fold_in(keys[7], 71), 0),
        "far_list": draw_far_list(jax.random.fold_in(keys[7], 71), 0),
        "skel_idx": draw_skel_idx(jax.random.fold_in(keys[7], 71), 0),
    }


def kernel_sum(target, sources, values):
    high = lax.Precision.HIGHEST
    target_f = target.astype(jnp.float32)
    source_f = sources.astype(jnp.float32)
    inner = jnp.einsum('dt,jds->tjs', target_f, source_f, precision=high)
    target_norm = jnp.sum(target_f * target_f, axis=0)
    source_norm = jnp.sum(source_f * source_f, axis=1)
    distance = target_norm[:, None, None] + source_norm[None] - 2.0 * inner
    kernel = jnp.exp(-distance * (2.0 / DIM))
    return jnp.einsum('tjs,jsw->tw', kernel, values.astype(jnp.float32), precision=high)


def reference(points, weights, proj, fetch_table, near_list, far_list, skel_idx):
    leaf_coords = points.reshape(DIM, NLEAF, LEAF)
    leaf_weights = weights.reshape(NLEAF, LEAF, WCOL)
    leaf_ids = jnp.arange(NLEAF, dtype=jnp.int32)
    column = leaf_ids // TGT_DEV
    near_row = (leaf_ids % TGT_DEV) // Q
    owner = near_list // CAP
    place = near_list % CAP
    local = fetch_table[near_row[:, None], column[:, None], owner, place]
    sources = (owner * TGT_DEV + local).astype(jnp.int32)

    def near_leaf(items):
        leaf_id, source_ids = items
        target = jnp.take(leaf_coords, leaf_id, axis=1)
        source_coords = jnp.moveaxis(jnp.take(leaf_coords, source_ids, axis=1), 0, 1)
        source_values = jnp.take(leaf_weights, source_ids, axis=0)
        return kernel_sum(target, source_coords, source_values)

    near = lax.map(near_leaf, (leaf_ids, sources))

    def node_tables(node):
        start = (node * COLPTS).astype(jnp.int32)
        node_points = lax.dynamic_slice_in_dim(points, start, COLPTS, 1)
        node_proj = lax.dynamic_slice_in_dim(proj, start, COLPTS, 1)
        node_weights = lax.dynamic_slice_in_dim(weights, start, COLPTS, 0)
        coords = jnp.take(node_points, skel_idx[node], axis=1)
        summed = jnp.dot(node_proj, node_weights, preferred_element_type=jnp.float32, precision=lax.Precision.HIGHEST)
        return coords, summed

    skel_coords, skel_weights = lax.map(node_tables, jnp.arange(N_DEV, dtype=jnp.int32))

    def far_leaf(items):
        leaf_id, node_ids = items
        target = jnp.take(leaf_coords, leaf_id, axis=1)
        return kernel_sum(target, jnp.take(skel_coords, node_ids, axis=0), jnp.take(skel_weights, node_ids, axis=0))

    far = lax.map(far_leaf, (leaf_ids, far_list))
    return (near + far).reshape(NPTS, WCOL)
```

```python
import functools
import math

import jax
import jax.numpy as jnp
from jax import lax
from jax.experimental import pallas as pl
from jax.experimental.pallas import tpu as pltpu
from jax.sharding import PartitionSpec as P

F32, BF16 = jnp.float32, jnp.bfloat16
MESH = pl.DeviceIdType.MESH
VMEM = pltpu.VMEM
LOG2E = math.log2(math.e)
SIDE = 4
SPOTS = SIDE * SIDE
LEAF, DIM, WCOL, SKEL = 512, 64, 128, 256
LEAVES = 12
MINE = 3
COLPTS = LEAVES * LEAF
HALF = LEAF // 2
PAYLOAD = MINE * HALF + 8
TARGETS = SPOTS * MINE
SOURCES = 2 * COLPTS + 2 * SKEL
CHUNK = 1024
CUTS = (0, 192, 384, 576, PAYLOAD)


def mm(a, b):
    return jnp.dot(a, b, preferred_element_type=F32)


def split2(v):
    high = v.astype(BF16)
    return high, (v - high.astype(F32)).astype(BF16)


def prepare_kernel(y_ref, points, weights, proj, index, own, table, payload, coords, values):
    step = pl.program_id(0)
    wh, wl = split2(weights[...])
    ph, plow = split2(proj[...])
    value = mm(ph, wh) + mm(ph, wl) + mm(plow, wh)
    rows = lax.broadcasted_iota(jnp.int32, (CHUNK, SKEL), 0) + step * CHUNK
    pick = jnp.where(rows == index[...], 1.0, 0.0).astype(BF16)
    first = points[...].astype(BF16)
    rest = points[...] - first.astype(F32)
    second, third = split2(rest)
    coord = mm(first, pick) + mm(second, pick) + mm(third, pick)

    @pl.when(step == 0)
    def _():
        values[...] = value
        coords[...] = coord
        payload[pl.ds(MINE * HALF, 8), :] = table[...]
        for leaf in range(MINE):
            block = own[:, leaf * LEAF : (leaf + 1) * LEAF]
            packed = jnp.concatenate([block[:, :HALF], block[:, HALF:]], axis=0)
            payload[pl.ds(leaf * HALF, HALF), :] = packed.T

    @pl.when(step > 0)
    def _():
        values[...] += value
        coords[...] += coord


def prepare(y, points, weights, proj, index, table):
    steps = COLPTS // CHUNK
    return pl.pallas_call(
        prepare_kernel,
        out_shape=(
            jax.ShapeDtypeStruct((PAYLOAD, 128), F32),
            jax.ShapeDtypeStruct((DIM, SKEL), F32),
            jax.ShapeDtypeStruct((SKEL, WCOL), F32),
        ),
        grid_spec=pltpu.PrefetchScalarGridSpec(
            num_scalar_prefetch=1,
            grid=(steps,),
            in_specs=[
                pl.BlockSpec((DIM, CHUNK), lambda i, y: (0, i)),
                pl.BlockSpec((CHUNK, WCOL), lambda i, y: (i, 0)),
                pl.BlockSpec((SKEL, CHUNK), lambda i, y: (0, i)),
                pl.BlockSpec((1, SKEL), lambda i, y: (0, 0)),
                pl.BlockSpec((DIM, MINE * LEAF), lambda i, y: (0, y[0])),
                pl.BlockSpec((8, 128), lambda i, y: (0, 0)),
            ],
            out_specs=[
                pl.BlockSpec((PAYLOAD, 128), lambda i, y: (0, 0)),
                pl.BlockSpec((DIM, SKEL), lambda i, y: (0, 0)),
                pl.BlockSpec((SKEL, WCOL), lambda i, y: (0, 0)),
            ],
        ),
        compiler_params=pltpu.CompilerParams(vmem_limit_bytes=32 << 20),
    )(y, points, weights, proj, index, points, table)


def place():
    y, dev = lax.axis_index("grp"), lax.axis_index("dev")
    return y, dev // 8, (dev // 2) % SIDE, dev % 2


def device(y, z, x, core):
    return (y, (z * SIDE + x) * 2 + core)


def stream_axes(k):
    return k < 2, 1 if k % 2 == 0 else SIDE - 1


def moved(k, z, x, first, second):
    x_first, sign = stream_axes(k)
    along_x, along_z = (first, second) if x_first else (second, first)
    return (z + sign * along_z) % SIDE, (x + sign * along_x) % SIDE


def greet(peers):
    barrier = pltpu.get_barrier_semaphore()
    for peer in peers:
        pl.semaphore_signal(barrier, inc=1, device_id=peer, device_id_type=MESH)
    pl.semaphore_wait(barrier, len(peers))


def gather_kernel(
    payload, points, weights, coords, values,
    gathered, points2, weights2, coords2, values2,
    send, recv, pair_send, pair_recv, own_sem,
):
    y, z, x, core = place()
    near = [(1, 0), (SIDE - 1, 0), (0, 1), (0, SIDE - 1)]
    peers = [device(y, (z + a) % SIDE, (x + b) % SIDE, core) for a, b in near]
    sibling = device(y, z, x, 1 - core)
    greet(peers + [sibling])

    def copy(k, i, j, first):
        az, ax = moved(k, z, x, -i, -j)
        spot = az * SIDE + ax
        rows = pl.ds(CUTS[k], CUTS[k + 1] - CUTS[k])
        tz, tx = moved(k, z, x, 1 if first else 0, 0 if first else 1)
        arrival = (i + 1) * SIDE + j if first else i * SIDE + j + 1
        number = i if first else SIDE - 1 + i * (SIDE - 1) + j
        source = payload.at[rows] if i == 0 and j == 0 else gathered.at[spot, rows]
        return pltpu.make_async_remote_copy(
            src_ref=source,
            dst_ref=gathered.at[spot, rows],
            send_sem=send.at[k, number],
            recv_sem=recv.at[k, arrival],
            device_id=device(y, tz, tx, core),
            device_id_type=MESH,
        )

    def wait_arrival(k, i, j):
        az, ax = moved(k, z, x, -i, -j)
        spot = az * SIDE + ax
        rows = pl.ds(CUTS[k], CUTS[k + 1] - CUTS[k])
        pltpu.make_async_copy(gathered.at[spot, rows], gathered.at[spot, rows], recv.at[k, i * SIDE + j]).wait()

    own = pltpu.make_async_copy(payload, gathered.at[z * SIDE + x], own_sem)
    own.start()
    started = []
    for level in range(2 * SIDE - 1):
        for i in range(SIDE):
            j = level - i
            if not 0 <= j < SIDE:
                continue
            for k in range(4):
                if level > 0:
                    wait_arrival(k, i, j)
                if j == 0 and i < SIDE - 1:
                    c = copy(k, i, j, True)
                    c.start()
                    started.append(c)
                if j < SIDE - 1:
                    c = copy(k, i, j, False)
                    c.start()
                    started.append(c)
        if level == 0:
            swaps = []
            for n, (a, b) in enumerate(
                ((points, points2), (weights, weights2), (coords, coords2), (values, values2))
            ):
                c = pltpu.make_async_remote_copy(
                    src_ref=a, dst_ref=b, send_sem=pair_send.at[n], recv_sem=pair_recv.at[n],
                    device_id=sibling, device_id_type=MESH,
                )
                c.start()
                swaps.append(c)
    for c in started:
        c.wait_send()
    for c in swaps:
        c.wait()
    own.wait()


def gather(payload, points, weights, coords, values):
    anywhere = pl.BlockSpec(memory_space=pl.ANY)
    return pl.pallas_call(
        gather_kernel,
        out_shape=(
            jax.ShapeDtypeStruct((SPOTS, PAYLOAD, 128), F32),
            jax.ShapeDtypeStruct(points.shape, F32),
            jax.ShapeDtypeStruct(weights.shape, F32),
            jax.ShapeDtypeStruct(coords.shape, F32),
            jax.ShapeDtypeStruct(values.shape, F32),
        ),
        in_specs=[anywhere] * 5,
        out_specs=[anywhere] * 5,
        scratch_shapes=[
            pltpu.SemaphoreType.DMA((4, 15)),
            pltpu.SemaphoreType.DMA((4, 16)),
            pltpu.SemaphoreType.DMA((4,)),
            pltpu.SemaphoreType.DMA((4,)),
            pltpu.SemaphoreType.DMA,
        ],
        compiler_params=pltpu.CompilerParams(
            collective_id=0, has_side_effects=True, vmem_limit_bytes=32 << 20
        ),
    )(payload, points, weights, coords, values)


def pair_kernel(
    spot_ref, table, gathered, points, points2, weights, weights2, coords, coords2, values, values2,
    out, left, right, norm, wcat, near_pairs, far_pairs,
):
    scale = LOG2E / 32.0

    def put_source(block, start, width):
        scaled = block * (2.0 * scale)
        high, low = split2(scaled)
        right[0:DIM, pl.ds(start, width)] = high
        right[DIM : 2 * DIM, pl.ds(start, width)] = high
        right[2 * DIM : 3 * DIM, pl.ds(start, width)] = low
        right[3 * DIM : 4 * DIM, pl.ds(start, width)] = jnp.full((DIM, width), -1.0, BF16)
        norm[:, pl.ds(start, width)] = -scale * jnp.sum(block * block, axis=0, keepdims=True)

    def put_weights(block, start, rows):
        high, low = split2(block)
        wcat[pl.ds(start, rows), 0:WCOL] = high
        wcat[pl.ds(start, rows), WCOL : 2 * WCOL] = low

    def sources(n, _):
        at = pl.multiple_of(n * LEAF, LEAF)
        put_source(points[:, pl.ds(at, LEAF)], at, LEAF)
        put_source(points2[:, pl.ds(at, LEAF)], pl.multiple_of(COLPTS + at, LEAF), LEAF)
        put_weights(weights[pl.ds(at, LEAF), :], at, LEAF)
        put_weights(weights2[pl.ds(at, LEAF), :], pl.multiple_of(COLPTS + at, LEAF), LEAF)
        return _

    lax.fori_loop(0, LEAVES, sources, 0)
    put_source(coords[...], 2 * COLPTS, SKEL)
    put_source(coords2[...], 2 * COLPTS + SKEL, SKEL)
    put_weights(values[...], 2 * COLPTS, SKEL)
    put_weights(values2[...], 2 * COLPTS + SKEL, SKEL)

    lane = lax.broadcasted_iota(jnp.int32, (HALF, 128), 1)
    first_half = lane < DIM
    first_quarter = lane % DIM < DIM // 2

    def target(t, _):
        spot, leaf = t // MINE, t % MINE
        both = gathered[spot, pl.ds(pl.multiple_of(leaf * HALF, HALF), HALF), :]
        high = both.astype(BF16).astype(F32)
        low = both - high
        high_r, low_r = pltpu.roll(high, DIM, 1), pltpu.roll(low, DIM, 1)
        square = both * both * scale
        down = square + pltpu.roll(square, 32, 1)
        up = square + pltpu.roll(square, 96, 1)
        up_high = up.astype(BF16).astype(F32)
        down_low = down - down.astype(BF16).astype(F32)
        sums = jnp.where(first_quarter, up_high, down_low)
        at = pl.multiple_of(t * LEAF, LEAF)
        left[pl.ds(at, HALF), 0:128] = jnp.where(first_half, high, low_r).astype(BF16)
        left[pl.ds(at, HALF), 128:256] = jnp.where(first_half, high, pltpu.roll(sums, DIM, 1)).astype(BF16)
        at = pl.multiple_of(at + HALF, HALF)
        left[pl.ds(at, HALF), 0:128] = jnp.where(first_half, high_r, low).astype(BF16)
        left[pl.ds(at, HALF), 128:256] = jnp.where(first_half, high_r, sums).astype(BF16)
        out[pl.ds(pl.multiple_of(t * LEAF, LEAF), LEAF), :] = jnp.zeros((LEAF, WCOL), F32)
        return _

    lax.fori_loop(0, TARGETS, target, 0)

    spot = spot_ref[0]

    def note(t, counts):
        near, far = counts
        for slot in range(4):
            source = table[t, 4 * spot + slot]
            near_pairs[near] = t * 64 + source
            near = near + jnp.where(source >= 0, 1, 0)
        for slot in range(2):
            node = table[t, 64 + 2 * spot + slot]
            far_pairs[far] = t * 64 + node
            far = far + jnp.where(node >= 0, 1, 0)
        return near, far

    near_count, far_count = lax.fori_loop(0, TARGETS, note, (0, 0))

    def interact(t, start, width):
        at = pl.multiple_of(t * LEAF, LEAF)
        columns = pl.ds(start, width)
        power = mm(left[pl.ds(at, LEAF), :], right[:, columns]) + norm[:, columns]
        high, low = split2(jnp.exp2(power))
        total = mm(high, wcat[columns, :])
        rest = mm(low, wcat[columns, 0:WCOL])
        out[pl.ds(at, LEAF), :] += total[:, :WCOL] + total[:, WCOL:] + rest

    def near_pair(n, _):
        code = near_pairs[n]
        interact(code // 64, pl.multiple_of((code % 64) * LEAF, LEAF), LEAF)
        return _

    def far_pair(n, _):
        code = far_pairs[n]
        interact(code // 64, pl.multiple_of(2 * COLPTS + (code % 64) * SKEL, SKEL), SKEL)
        return _

    lax.fori_loop(0, near_count, near_pair, 0)
    lax.fori_loop(0, far_count, far_pair, 0)


def pairs(spot, table, gathered, *sources):
    smem = pl.BlockSpec(memory_space=pltpu.SMEM)
    vmem = pl.BlockSpec(memory_space=VMEM)
    return pl.pallas_call(
        pair_kernel,
        out_shape=jax.ShapeDtypeStruct((TARGETS * LEAF, WCOL), F32),
        in_specs=[smem, smem] + [vmem] * 9,
        out_specs=vmem,
        scratch_shapes=[
            VMEM((TARGETS * LEAF, 256), BF16),
            VMEM((4 * DIM, SOURCES), BF16),
            VMEM((1, SOURCES), F32),
            VMEM((SOURCES, 2 * WCOL), BF16),
            pltpu.SMEM((TARGETS * 4 + 1,), jnp.int32),
            pltpu.SMEM((TARGETS * 2 + 1,), jnp.int32),
        ],
        compiler_params=pltpu.CompilerParams(vmem_limit_bytes=62 << 20),
    )(spot, table, gathered, *sources)


QUARTER = LEAF // 4


def scatter_kernel(partial, out, slots, turn, send, recv, turn_send, turn_recv, y_send, y_recv):
    y, z, x, core = place()
    near = [(1, 0), (SIDE - 1, 0), (0, 1), (0, SIDE - 1)]
    peers = [device(y, (z + a) % SIDE, (x + b) % SIDE, core) for a, b in near]
    above, below = device((y + 1) % SIDE, z, x, core), device((y + SIDE - 1) % SIDE, z, x, core)
    greet(peers + [above, below])
    started = []

    def own(k, leaf, first, second):
        az, ax = moved(k, z, x, first, second)
        start = ((az * SIDE + ax) * MINE + leaf) * LEAF + k * QUARTER
        return pl.ds(pl.multiple_of(start, QUARTER), QUARTER)

    def begin(c):
        c.start()
        started.append(c)

    def step_first(k, leaf, step, j, source):
        tz, tx = moved(k, z, x, 1, 0)
        n = (leaf * 3 + step) * SIDE + j
        begin(pltpu.make_async_remote_copy(
            src_ref=source, dst_ref=slots.at[k, n], send_sem=send.at[k, n], recv_sem=recv.at[k, n],
            device_id=device(y, tz, tx, core), device_id_type=MESH,
        ))

    def arrived_first(k, leaf, step, j):
        n = (leaf * 3 + step) * SIDE + j
        pltpu.make_async_copy(slots.at[k, n], slots.at[k, n], recv.at[k, n]).wait()
        slots[k, n] += partial[own(k, leaf, 2 - step, 3 - j), :]
        return n

    def step_second(k, leaf, step, source):
        tz, tx = moved(k, z, x, 0, 1)
        n = leaf * 3 + step
        begin(pltpu.make_async_remote_copy(
            src_ref=source, dst_ref=turn.at[k, n], send_sem=turn_send.at[k, n], recv_sem=turn_recv.at[k, n],
            device_id=device(y, tz, tx, core), device_id_type=MESH,
        ))

    def rows_of(plane, leaf, k):
        return pl.ds(pl.multiple_of((plane * MINE + leaf) * LEAF + k * QUARTER, QUARTER), QUARTER)

    def to_y(leaf, k, number, plane, up):
        rows = rows_of(plane, leaf, k)
        n = (leaf * 4 + k) * 3 + number
        begin(pltpu.make_async_remote_copy(
            src_ref=out.at[rows], dst_ref=out.at[rows], send_sem=y_send.at[n], recv_sem=y_recv.at[n],
            device_id=above if up else below, device_id_type=MESH,
        ))

    def y_wait(leaf, k, number, plane):
        rows = rows_of(plane, leaf, k)
        n = (leaf * 4 + k) * 3 + number
        pltpu.make_async_copy(out.at[rows], out.at[rows], y_recv.at[n]).wait()

    def second_axis(k, leaf, j):
        n = arrived_first(k, leaf, 2, j)
        if j > 0:
            m = leaf * 3 + j - 1
            pltpu.make_async_copy(turn.at[k, m], turn.at[k, m], turn_recv.at[k, m]).wait()
        if j == 0:
            step_second(k, leaf, 0, slots.at[k, n])
        elif j < 3:
            turn[k, m] += slots[k, n]
            step_second(k, leaf, j, turn.at[k, m])
        else:
            out[rows_of(y, leaf, k), :] = turn[k, m] + slots[k, n]
            to_y(leaf, k, 0, y, True)
            to_y(leaf, k, 1, y, False)

    def second_hop(leaf, k):
        lower, upper = (y + SIDE - 1) % SIDE, (y + 1) % SIDE
        if k % 2 == 0:
            y_wait(leaf, k, 0, lower)
            to_y(leaf, k, 2, lower, True)
        else:
            y_wait(leaf, k, 1, upper)
            to_y(leaf, k, 2, upper, False)

    def last_arrivals(leaf, k):
        lower, upper, across = (y + SIDE - 1) % SIDE, (y + 1) % SIDE, (y + 2) % SIDE
        if k % 2 == 0:
            y_wait(leaf, k, 1, upper)
        else:
            y_wait(leaf, k, 0, lower)
        y_wait(leaf, k, 2, across)

    for leaf in range(MINE + 1):
        if leaf < MINE:
            for j in range(SIDE):
                for k in range(4):
                    step_first(k, leaf, 0, j, partial.at[own(k, leaf, 3, 3 - j)])
        for j in range(SIDE):
            for k in range(4):
                if leaf < MINE:
                    n = arrived_first(k, leaf, 0, j)
                    step_first(k, leaf, 1, j, slots.at[k, n])
                if leaf > 0:
                    second_axis(k, leaf - 1, j)
        if leaf < MINE:
            for j in range(SIDE):
                for k in range(4):
                    n = arrived_first(k, leaf, 1, j)
                    step_first(k, leaf, 2, j, slots.at[k, n])
        if leaf > 0:
            for k in range(4):
                second_hop(leaf - 1, k)
    for leaf in range(MINE):
        for k in range(4):
            last_arrivals(leaf, k)
    for c in started:
        c.wait_send()


def scatter(partial):
    vmem = pl.BlockSpec(memory_space=VMEM)
    return pl.pallas_call(
        scatter_kernel,
        out_shape=jax.ShapeDtypeStruct((COLPTS, WCOL), F32),
        in_specs=[vmem],
        out_specs=vmem,
        scratch_shapes=[
            VMEM((4, MINE * 3 * SIDE, QUARTER, WCOL), F32),
            VMEM((4, MINE * 3, QUARTER, WCOL), F32),
            pltpu.SemaphoreType.DMA((4, MINE * 3 * SIDE)),
            pltpu.SemaphoreType.DMA((4, MINE * 3 * SIDE)),
            pltpu.SemaphoreType.DMA((4, MINE * 3)),
            pltpu.SemaphoreType.DMA((4, MINE * 3)),
            pltpu.SemaphoreType.DMA((MINE * 4 * 3,)),
            pltpu.SemaphoreType.DMA((MINE * 4 * 3,)),
        ],
        compiler_params=pltpu.CompilerParams(
            collective_id=1, has_side_effects=True, vmem_limit_bytes=60 << 20
        ),
    )(partial)


def lists(y, core, fetch_table, near_list, far_list):
    near = lax.dynamic_slice_in_dim(near_list, y * MINE, MINE, 0)
    far = lax.dynamic_slice_in_dim(far_list, y * MINE, MINE, 0)
    slots = jnp.arange(64, dtype=jnp.int32)
    nodes = jnp.arange(32, dtype=jnp.int32)
    near_used = jnp.any(near[:, :, None] == slots, axis=1)
    far_used = jnp.any(far[:, :, None] == nodes, axis=1)
    rows = (y * MINE + jnp.arange(MINE, dtype=jnp.int32)) // 4
    requests = fetch_table[:, 0].reshape(3, 64)
    local = jnp.sum(jnp.where(rows[:, None, None] == jnp.arange(3)[None, :, None], requests[None], 0), axis=1)
    side = (slots // 2 + core) % 2
    near_value = jnp.where(near_used, side * LEAVES + local, -1)
    far_value = jnp.where(far_used, (nodes + core) % 2, -1)
    table = jnp.concatenate([near_value, far_value, jnp.full((MINE, 32), -1, jnp.int32)], axis=1)
    return jnp.pad(table, ((0, 8 - MINE), (0, 0))).astype(F32)


def on_device(points, weights, proj, fetch_table, near_list, far_list, skel_idx):
    y, z, x, core = place()
    table = lists(y, core, fetch_table, near_list, far_list)
    payload, coords, values = prepare(
        y.reshape(1).astype(jnp.int32), points, weights, proj, skel_idx, table
    )
    gathered, points2, weights2, coords2, values2 = gather(payload, points, weights, coords, values)
    found = gathered[:, MINE * HALF : MINE * HALF + MINE, :].astype(jnp.int32).reshape(TARGETS, 128)
    spot = (z * SIDE + x).reshape(1).astype(jnp.int32)
    partial = pairs(
        spot, found, gathered, points, points2, weights, weights2, coords, coords2, values, values2
    )
    return scatter(partial)


def solution(mesh):
    placed = (
        P(None, "dev"),
        P("dev", None),
        P(None, "dev"),
        P(None, "dev", None, None),
        P("dev", None),
        P("dev", None),
        P("dev", None),
    )
    return jax.shard_map(
        on_device, mesh=mesh, in_specs=placed, out_specs=P("dev", None), check_vma=False
    )
```

```python
import functools
import math

import jax
import jax.numpy as jnp
from jax import lax
from jax.experimental import pallas as pl
from jax.experimental.pallas import tpu as pltpu
from jax.sharding import PartitionSpec as P

F32, BF16 = jnp.float32, jnp.bfloat16
MESH = pl.DeviceIdType.MESH
VMEM = pltpu.VMEM
LOG2E = math.log2(math.e)
SIDE = 4
SPOTS = SIDE * SIDE
LEAF, DIM, WCOL, SKEL = 512, 64, 128, 256
LEAVES = 12
MINE = 3
COLPTS = LEAVES * LEAF
HALF = LEAF // 2
PAYLOAD = MINE * HALF + 8
TARGETS = SPOTS * MINE
SOURCES = 2 * COLPTS + 2 * SKEL
CHUNK = 1024
SCALE = LOG2E / 32.0
K1_VMEM, K2_VMEM, K3_VMEM = 30 << 20, 8 << 20, 30 << 20
CUTS = (0, 192, 384, 576, PAYLOAD)


def mm(a, b):
    return jnp.dot(a, b, preferred_element_type=F32)


def split2(v):
    high = v.astype(BF16)
    return high, (v - high.astype(F32)).astype(BF16)


def place():
    y, dev = lax.axis_index("grp"), lax.axis_index("dev")
    return y, dev // 8, (dev // 2) % SIDE, dev % 2


def device(y, z, x, core):
    return (y, (z * SIDE + x) * 2 + core)


def stream_axes(k):
    return k < 2, 1 if k % 2 == 0 else SIDE - 1


def moved(k, z, x, first, second):
    x_first, sign = stream_axes(k)
    along_x, along_z = (first, second) if x_first else (second, first)
    return (z + sign * along_z) % SIDE, (x + sign * along_x) % SIDE


def greet(peers):
    barrier = pltpu.get_barrier_semaphore()
    for peer in peers:
        pl.semaphore_signal(barrier, inc=1, device_id=peer, device_id_type=MESH)
    pl.semaphore_wait(barrier, len(peers))


def put_source(block, right, norm, start):
    width = block.shape[1]
    high, low = split2(block * (2.0 * SCALE))
    right[0:DIM, pl.ds(start, width)] = high
    right[DIM : 2 * DIM, pl.ds(start, width)] = high
    right[2 * DIM : 3 * DIM, pl.ds(start, width)] = low
    right[3 * DIM : 4 * DIM, pl.ds(start, width)] = jnp.full((DIM, width), -1.0, BF16)
    norm[:, pl.ds(start, width)] = -SCALE * jnp.sum(block * block, axis=0, keepdims=True)


def put_weights(block, wcat, start):
    high, low = split2(block)
    wcat[pl.ds(start, block.shape[0]), 0:WCOL] = high
    wcat[pl.ds(start, block.shape[0]), WCOL : 2 * WCOL] = low


def put_target(both, left, at):
    lane = lax.broadcasted_iota(jnp.int32, both.shape, 1)
    first_half = lane < DIM
    first_quarter = lane % DIM < DIM // 2
    high = both.astype(BF16).astype(F32)
    low = both - high
    high_r, low_r = pltpu.roll(high, DIM, 1), pltpu.roll(low, DIM, 1)
    square = both * both * SCALE
    down = square + pltpu.roll(square, 32, 1)
    up = square + pltpu.roll(square, 96, 1)
    up_high = up.astype(BF16).astype(F32)
    down_low = down - down.astype(BF16).astype(F32)
    sums = jnp.where(first_quarter, up_high, down_low)
    left[pl.ds(at, HALF), 0:128] = jnp.where(first_half, high, low_r).astype(BF16)
    left[pl.ds(at, HALF), 128:256] = jnp.where(first_half, high, pltpu.roll(sums, DIM, 1)).astype(BF16)
    left[pl.ds(at + HALF, HALF), 0:128] = jnp.where(first_half, high_r, low).astype(BF16)
    left[pl.ds(at + HALF, HALF), 128:256] = jnp.where(first_half, high_r, sums).astype(BF16)


def gather_kernel(
    points_hbm, weights_hbm, proj_hbm, index, table,
    left, right, norm, wcat, found,
    payload, gathered, own, points, points2, weights, weights2, proj, coords, coords2, values, values2,
    send, recv, pair_send, pair_recv, load_sem,
):
    y, z, x, core = place()
    loads = [
        pltpu.make_async_copy(
            points_hbm.at[:, pl.ds(pl.multiple_of(y * (MINE * LEAF), LEAF), MINE * LEAF)], own, load_sem.at[0]
        ),
        pltpu.make_async_copy(points_hbm, points, load_sem.at[1]),
        pltpu.make_async_copy(weights_hbm, weights, load_sem.at[2]),
        pltpu.make_async_copy(proj_hbm, proj, load_sem.at[3]),
    ]
    for c in loads:
        c.start()
    near = [(1, 0), (SIDE - 1, 0), (0, 1), (0, SIDE - 1)]
    peers = [device(y, (z + a) % SIDE, (x + b) % SIDE, core) for a, b in near]
    sibling = device(y, z, x, 1 - core)
    greet(peers + [sibling])

    loads[0].wait()
    for leaf in range(MINE):
        block = own[:, leaf * LEAF : (leaf + 1) * LEAF]
        packed = jnp.concatenate([block[:, :HALF], block[:, HALF:]], axis=0)
        payload[leaf * HALF : (leaf + 1) * HALF, :] = packed.T
    payload[MINE * HALF :, :] = table[...]

    started, swaps = [], []

    def spot_of(k, i, j):
        az, ax = moved(k, z, x, -i, -j)
        return az * SIDE + ax

    def copy(k, i, j, first):
        rows = pl.ds(CUTS[k], CUTS[k + 1] - CUTS[k])
        tz, tx = moved(k, z, x, 1 if first else 0, 0 if first else 1)
        arrival = (i + 1) * SIDE + j if first else i * SIDE + j + 1
        number = i if first else SIDE - 1 + i * (SIDE - 1) + j
        target = gathered.at[spot_of(k, i, j), rows]
        c = pltpu.make_async_remote_copy(
            src_ref=payload.at[rows] if i == 0 and j == 0 else target,
            dst_ref=target,
            send_sem=send.at[k, number],
            recv_sem=recv.at[k, arrival],
            device_id=device(y, tz, tx, core),
            device_id_type=MESH,
        )
        c.start()
        started.append(c)

    def forward(level):
        for i in range(SIDE):
            j = level - i
            if not 0 <= j < SIDE:
                continue
            for k in range(4):
                if level > 0:
                    rows = pl.ds(CUTS[k], CUTS[k + 1] - CUTS[k])
                    here = gathered.at[spot_of(k, i, j), rows]
                    pltpu.make_async_copy(here, here, recv.at[k, i * SIDE + j]).wait()
                if j == 0 and i < SIDE - 1:
                    copy(k, i, j, True)
                if j < SIDE - 1:
                    copy(k, i, j, False)

    def swap(n, a, b):
        c = pltpu.make_async_remote_copy(
            src_ref=a, dst_ref=b, send_sem=pair_send.at[n], recv_sem=pair_recv.at[n],
            device_id=sibling, device_id_type=MESH,
        )
        c.start()
        swaps.append(c)

    def targets_at(dz, dx):
        spot = (z + dz) % SIDE * SIDE + (x + dx) % SIDE

        def leaf_rows(leaf, _):
            rows = pl.ds(pl.multiple_of(leaf * HALF, HALF), HALF)
            both = payload[rows, :] if dz == dx == 0 else gathered[spot, rows, :]
            put_target(both, left, pl.multiple_of((spot * MINE + leaf) * LEAF, LEAF))
            return _

        lax.fori_loop(0, MINE, leaf_rows, 0)
        lists_here = payload[MINE * HALF :, :] if dz == dx == 0 else gathered[spot, MINE * HALF :, :]
        found[spot] = lists_here.astype(jnp.int32)

    def column(points_ref, weights_ref, base):
        def one(n, _):
            at = pl.multiple_of(n * LEAF, LEAF)
            put_source(points_ref[:, pl.ds(at, LEAF)], right, norm, pl.multiple_of(base + at, LEAF))
            put_weights(weights_ref[pl.ds(at, LEAF), :], wcat, pl.multiple_of(base + at, LEAF))
            return _

        lax.fori_loop(0, LEAVES, one, 0)

    def spots_of(level):
        steps = (0, 1, 2, 3)

        def done(dz, dx):
            far = lambda d: max(d, (SIDE - d) % SIDE)
            return far(dz) + far(dx)

        return [(dz, dx) for dz in steps for dx in steps if done(dz, dx) == level]

    forward(0)
    loads[1].wait()
    loads[2].wait()
    swap(0, points, points2)
    swap(1, weights, weights2)
    targets_at(0, 0)
    column(points, weights, 0)
    forward(1)
    loads[3].wait()
    values[...] = jnp.zeros_like(values)
    coords[...] = jnp.zeros_like(coords)

    def skeleton(n, _):
        at = pl.multiple_of(n * CHUNK, CHUNK)
        wh, wl = wcat[pl.ds(at, CHUNK), 0:WCOL], wcat[pl.ds(at, CHUNK), WCOL : 2 * WCOL]
        ph, plow = split2(proj[:, pl.ds(at, CHUNK)])
        values[...] += mm(ph, wh) + mm(ph, wl) + mm(plow, wh)
        rows = lax.broadcasted_iota(jnp.int32, (CHUNK, SKEL), 0) + at
        pick = jnp.where(rows == index[...], 1.0, 0.0).astype(BF16)
        block = points[:, pl.ds(at, CHUNK)]
        first = block.astype(BF16)
        second, third = split2(block - first.astype(F32))
        coords[...] += mm(first, pick) + mm(second, pick) + mm(third, pick)
        return _

    lax.fori_loop(0, COLPTS // CHUNK, skeleton, 0)
    swap(2, coords, coords2)
    swap(3, values, values2)
    forward(2)
    put_source(coords[...], right, norm, 2 * COLPTS)
    put_weights(values[...], wcat, 2 * COLPTS)
    swaps[0].wait_recv()
    swaps[1].wait_recv()
    column(points2, weights2, COLPTS)
    forward(3)
    swaps[2].wait_recv()
    swaps[3].wait_recv()
    put_source(coords2[...], right, norm, 2 * COLPTS + SKEL)
    put_weights(values2[...], wcat, 2 * COLPTS + SKEL)
    for level in (2, 3):
        for dz, dx in spots_of(level):
            targets_at(dz, dx)
    for level in (4, 5, 6):
        forward(level)
        for dz, dx in spots_of(level):
            targets_at(dz, dx)
    for c in started + swaps:
        c.wait_send()


def gather(points, weights, proj, index, table):
    anywhere = pl.BlockSpec(memory_space=pl.ANY)
    vmem = pl.BlockSpec(memory_space=VMEM)
    return pl.pallas_call(
        gather_kernel,
        out_shape=(
            pltpu.VMEM((TARGETS * LEAF, 256), BF16),
            pltpu.VMEM((4 * DIM, SOURCES), BF16),
            pltpu.VMEM((1, SOURCES), F32),
            pltpu.VMEM((SOURCES, 2 * WCOL), BF16),
            jax.ShapeDtypeStruct((SPOTS, 8, 128), jnp.int32),
        ),
        in_specs=[anywhere] * 3 + [vmem] * 2,
        out_specs=[vmem] * 5,
        scratch_shapes=[
            VMEM((PAYLOAD, 128), F32),
            VMEM((SPOTS, PAYLOAD, 128), F32),
            VMEM((DIM, MINE * LEAF), F32),
            VMEM((DIM, COLPTS), F32),
            VMEM((DIM, COLPTS), F32),
            VMEM((COLPTS, WCOL), F32),
            VMEM((COLPTS, WCOL), F32),
            VMEM((SKEL, COLPTS), F32),
            VMEM((DIM, SKEL), F32),
            VMEM((DIM, SKEL), F32),
            VMEM((SKEL, WCOL), F32),
            VMEM((SKEL, WCOL), F32),
            pltpu.SemaphoreType.DMA((4, 15)),
            pltpu.SemaphoreType.DMA((4, 16)),
            pltpu.SemaphoreType.DMA((4,)),
            pltpu.SemaphoreType.DMA((4,)),
            pltpu.SemaphoreType.DMA((4,)),
        ],
        compiler_params=pltpu.CompilerParams(
            collective_id=0, has_side_effects=True, vmem_limit_bytes=K1_VMEM
        ),
    )(points, weights, proj, index, table)


def pair_kernel(spot_ref, table, left, right, norm, wcat, out, even, even_low, odd, odd_low, near_pairs, far_pairs):
    def zero(t, _):
        out[pl.ds(pl.multiple_of(t * LEAF, LEAF), LEAF), :] = jnp.zeros((LEAF, WCOL), F32)
        return _

    lax.fori_loop(0, TARGETS + 1, zero, 0)
    spot = spot_ref[0]

    def note(t, counts):
        near, far = counts
        for slot in range(4):
            source = table[t // MINE, t % MINE, 4 * spot + slot]
            near_pairs[near] = t * 64 + source
            near = near + jnp.where(source >= 0, 1, 0)
        for slot in range(2):
            node = table[t // MINE, t % MINE, 64 + 2 * spot + slot]
            far_pairs[far] = t * 64 + node
            far = far + jnp.where(node >= 0, 1, 0)
        return near, far

    near_count, far_count = lax.fori_loop(0, TARGETS, note, (0, 0))
    for extra in range(3):
        near_pairs[near_count + extra] = TARGETS * 64
        far_pairs[far_count + extra] = TARGETS * 64

    def run(pair_list, count, base, width):
        def columns(code):
            return pl.ds(pl.multiple_of(base + (code % 64) * width, width), width)

        def produce(n, high_ref, low_ref):
            code = pair_list[n]
            t, where = code // 64, columns(code)
            at = pl.multiple_of(jnp.where(t < TARGETS, t, 0) * LEAF, LEAF)
            power = mm(left[pl.ds(at, LEAF), :], right[:, where]) + norm[:, where]
            high_ref[:, :width], low_ref[:, :width] = split2(jnp.exp2(power))

        def consume(n, high_ref, low_ref):
            code = pair_list[n]
            t, where = code // 64, columns(code)
            total = mm(high_ref[:, :width], wcat[where, :])
            rest = mm(low_ref[:, :width], wcat[where, 0:WCOL])
            at = pl.multiple_of(t * LEAF, LEAF)
            out[pl.ds(at, LEAF), :] += total[:, :WCOL] + total[:, WCOL:] + rest

        produce(0, even, even_low)

        def two(m, _):
            produce(2 * m + 1, odd, odd_low)
            consume(2 * m, even, even_low)
            produce(2 * m + 2, even, even_low)
            consume(2 * m + 1, odd, odd_low)
            return _

        lax.fori_loop(0, (count + 1) // 2, two, 0)

    run(near_pairs, near_count, 0, LEAF)
    run(far_pairs, far_count, 2 * COLPTS, SKEL)


def pairs(spot, table, left, right, norm, wcat):
    smem = pl.BlockSpec(memory_space=pltpu.SMEM)
    vmem = pl.BlockSpec(memory_space=VMEM)
    return pl.pallas_call(
        pair_kernel,
        out_shape=pltpu.VMEM(((TARGETS + 1) * LEAF, WCOL), F32),
        in_specs=[smem, smem] + [vmem] * 4,
        out_specs=vmem,
        scratch_shapes=[VMEM((LEAF, LEAF), BF16)] * 4
        + [
            pltpu.SMEM((TARGETS * 4 + 3,), jnp.int32),
            pltpu.SMEM((TARGETS * 2 + 3,), jnp.int32),
        ],
        compiler_params=pltpu.CompilerParams(vmem_limit_bytes=K2_VMEM),
    )(spot, table, left, right, norm, wcat)


QUARTER = LEAF // 4


def scatter_kernel(partial, out, slots, turn, send, recv, turn_send, turn_recv, y_send, y_recv):
    y, z, x, core = place()
    near = [(1, 0), (SIDE - 1, 0), (0, 1), (0, SIDE - 1)]
    peers = [device(y, (z + a) % SIDE, (x + b) % SIDE, core) for a, b in near]
    above, below = device((y + 1) % SIDE, z, x, core), device((y + SIDE - 1) % SIDE, z, x, core)
    greet(peers + [above, below])
    started = []

    def own(k, leaf, first, second):
        az, ax = moved(k, z, x, first, second)
        start = ((az * SIDE + ax) * MINE + leaf) * LEAF + k * QUARTER
        return pl.ds(pl.multiple_of(start, QUARTER), QUARTER)

    def begin(c):
        c.start()
        started.append(c)

    def step_first(k, leaf, step, j, source):
        tz, tx = moved(k, z, x, 1, 0)
        n = (leaf * 3 + step) * SIDE + j
        begin(pltpu.make_async_remote_copy(
            src_ref=source, dst_ref=slots.at[k, n], send_sem=send.at[k, n], recv_sem=recv.at[k, n],
            device_id=device(y, tz, tx, core), device_id_type=MESH,
        ))

    def arrived_first(k, leaf, step, j):
        n = (leaf * 3 + step) * SIDE + j
        pltpu.make_async_copy(slots.at[k, n], slots.at[k, n], recv.at[k, n]).wait()
        slots[k, n] += partial[own(k, leaf, 2 - step, 3 - j), :]
        return n

    def step_second(k, leaf, step, source):
        tz, tx = moved(k, z, x, 0, 1)
        n = leaf * 3 + step
        begin(pltpu.make_async_remote_copy(
            src_ref=source, dst_ref=turn.at[k, n], send_sem=turn_send.at[k, n], recv_sem=turn_recv.at[k, n],
            device_id=device(y, tz, tx, core), device_id_type=MESH,
        ))

    def rows_of(plane, leaf, k):
        return pl.ds(pl.multiple_of((plane * MINE + leaf) * LEAF + k * QUARTER, QUARTER), QUARTER)

    def to_y(leaf, k, number, plane, up):
        rows = rows_of(plane, leaf, k)
        n = (leaf * 4 + k) * 3 + number
        begin(pltpu.make_async_remote_copy(
            src_ref=out.at[rows], dst_ref=out.at[rows], send_sem=y_send.at[n], recv_sem=y_recv.at[n],
            device_id=above if up else below, device_id_type=MESH,
        ))

    def y_wait(leaf, k, number, plane):
        rows = rows_of(plane, leaf, k)
        n = (leaf * 4 + k) * 3 + number
        pltpu.make_async_copy(out.at[rows], out.at[rows], y_recv.at[n]).wait()

    def second_axis(k, leaf, j):
        n = arrived_first(k, leaf, 2, j)
        if j > 0:
            m = leaf * 3 + j - 1
            pltpu.make_async_copy(turn.at[k, m], turn.at[k, m], turn_recv.at[k, m]).wait()
        if j == 0:
            step_second(k, leaf, 0, slots.at[k, n])
        elif j < 3:
            turn[k, m] += slots[k, n]
            step_second(k, leaf, j, turn.at[k, m])
        else:
            out[rows_of(y, leaf, k), :] = turn[k, m] + slots[k, n]
            to_y(leaf, k, 0, y, True)
            to_y(leaf, k, 1, y, False)

    def second_hop(leaf, k):
        lower, upper = (y + SIDE - 1) % SIDE, (y + 1) % SIDE
        if k % 2 == 0:
            y_wait(leaf, k, 0, lower)
            to_y(leaf, k, 2, lower, True)
        else:
            y_wait(leaf, k, 1, upper)
            to_y(leaf, k, 2, upper, False)

    def last_arrivals(leaf, k):
        lower, upper, across = (y + SIDE - 1) % SIDE, (y + 1) % SIDE, (y + 2) % SIDE
        if k % 2 == 0:
            y_wait(leaf, k, 1, upper)
        else:
            y_wait(leaf, k, 0, lower)
        y_wait(leaf, k, 2, across)

    for leaf in range(MINE + 1):
        if leaf < MINE:
            for j in range(SIDE):
                for k in range(4):
                    step_first(k, leaf, 0, j, partial.at[own(k, leaf, 3, 3 - j)])
        for j in range(SIDE):
            for k in range(4):
                if leaf < MINE:
                    n = arrived_first(k, leaf, 0, j)
                    step_first(k, leaf, 1, j, slots.at[k, n])
                if leaf > 0:
                    second_axis(k, leaf - 1, j)
        if leaf < MINE:
            for j in range(SIDE):
                for k in range(4):
                    n = arrived_first(k, leaf, 1, j)
                    step_first(k, leaf, 2, j, slots.at[k, n])
        if leaf > 0:
            for k in range(4):
                second_hop(leaf - 1, k)
    for leaf in range(MINE):
        for k in range(4):
            last_arrivals(leaf, k)
    for c in started:
        c.wait_send()


def scatter(partial):
    vmem = pl.BlockSpec(memory_space=VMEM)
    return pl.pallas_call(
        scatter_kernel,
        out_shape=jax.ShapeDtypeStruct((COLPTS, WCOL), F32),
        in_specs=[vmem],
        out_specs=vmem,
        scratch_shapes=[
            VMEM((4, MINE * 3 * SIDE, QUARTER, WCOL), F32),
            VMEM((4, MINE * 3, QUARTER, WCOL), F32),
            pltpu.SemaphoreType.DMA((4, MINE * 3 * SIDE)),
            pltpu.SemaphoreType.DMA((4, MINE * 3 * SIDE)),
            pltpu.SemaphoreType.DMA((4, MINE * 3)),
            pltpu.SemaphoreType.DMA((4, MINE * 3)),
            pltpu.SemaphoreType.DMA((MINE * 4 * 3,)),
            pltpu.SemaphoreType.DMA((MINE * 4 * 3,)),
        ],
        compiler_params=pltpu.CompilerParams(
            collective_id=1, has_side_effects=True, vmem_limit_bytes=K3_VMEM
        ),
    )(partial)


def lists(y, core, fetch_table, near_list, far_list):
    near = lax.dynamic_slice_in_dim(near_list, y * MINE, MINE, 0)
    far = lax.dynamic_slice_in_dim(far_list, y * MINE, MINE, 0)
    slots = jnp.arange(64, dtype=jnp.int32)
    nodes = jnp.arange(32, dtype=jnp.int32)
    near_used = jnp.any(near[:, :, None] == slots, axis=1)
    far_used = jnp.any(far[:, :, None] == nodes, axis=1)
    rows = (y * MINE + jnp.arange(MINE, dtype=jnp.int32)) // 4
    requests = fetch_table[:, 0].reshape(3, 64)
    local = jnp.sum(jnp.where(rows[:, None, None] == jnp.arange(3)[None, :, None], requests[None], 0), axis=1)
    side = (slots // 2 + core) % 2
    near_value = jnp.where(near_used, side * LEAVES + local, -1)
    far_value = jnp.where(far_used, (nodes + core) % 2, -1)
    table = jnp.concatenate([near_value, far_value, jnp.full((MINE, 32), -1, jnp.int32)], axis=1)
    return jnp.pad(table, ((0, 8 - MINE), (0, 0))).astype(F32)


def on_device(points, weights, proj, fetch_table, near_list, far_list, skel_idx):
    y, z, x, core = place()
    table = lists(y, core, fetch_table, near_list, far_list)
    left, right, norm, wcat, found = gather(points, weights, proj, skel_idx, table)
    spot = (z * SIDE + x).reshape(1).astype(jnp.int32)
    partial = pairs(spot, found, left, right, norm, wcat)
    return scatter(partial)


def solution(mesh):
    placed = (
        P(None, "dev"),
        P("dev", None),
        P(None, "dev"),
        P(None, "dev", None, None),
        P("dev", None),
        P("dev", None),
        P("dev", None),
    )
    return jax.shard_map(
        on_device, mesh=mesh, in_specs=placed, out_specs=P("dev", None), check_vma=False
    )
```

```python
import functools
import math

import jax
import jax.numpy as jnp
from jax import lax
from jax.experimental import pallas as pl
from jax.experimental.pallas import tpu as pltpu
from jax.sharding import PartitionSpec as P

F32, BF16 = jnp.float32, jnp.bfloat16
MESH = pl.DeviceIdType.MESH
VMEM = pltpu.VMEM
LOG2E = math.log2(math.e)
SIDE = 4
SPOTS = SIDE * SIDE
LEAF, DIM, WCOL, SKEL = 512, 64, 128, 256
LEAVES = 12
MINE = 3
COLPTS = LEAVES * LEAF
HALF = LEAF // 2
PAYLOAD = MINE * HALF + 8
TARGETS = SPOTS * MINE
SOURCES = 2 * COLPTS + 2 * SKEL
CHUNK = 1024
SCALE = LOG2E / 32.0
K1_VMEM, K2_VMEM, K3_VMEM = 44 << 20, 24 << 20, 26 << 20
CUTS = (0, 192, 384, 576, PAYLOAD)


def mm(a, b):
    return jnp.dot(a, b, preferred_element_type=F32)


def split2(v):
    high = v.astype(BF16)
    return high, (v - high.astype(F32)).astype(BF16)


def place():
    y, dev = lax.axis_index("grp"), lax.axis_index("dev")
    return y, dev // 8, (dev // 2) % SIDE, dev % 2


def device(y, z, x, core):
    return (y, (z * SIDE + x) * 2 + core)


def stream_axes(k):
    return k < 2, 1 if k % 2 == 0 else SIDE - 1


def moved(k, z, x, first, second):
    x_first, sign = stream_axes(k)
    along_x, along_z = (first, second) if x_first else (second, first)
    return (z + sign * along_z) % SIDE, (x + sign * along_x) % SIDE


def greet(peers):
    barrier = pltpu.get_barrier_semaphore()
    for peer in peers:
        pl.semaphore_signal(barrier, inc=1, device_id=peer, device_id_type=MESH)
    pl.semaphore_wait(barrier, len(peers))


def put_source(block, right, norm, start):
    width = block.shape[1]
    high, low = split2(block * (2.0 * SCALE))
    right[0:DIM, pl.ds(start, width)] = high
    right[DIM : 2 * DIM, pl.ds(start, width)] = high
    right[2 * DIM : 3 * DIM, pl.ds(start, width)] = low
    right[3 * DIM : 4 * DIM, pl.ds(start, width)] = jnp.full((DIM, width), -1.0, BF16)
    norm[:, pl.ds(start, width)] = -SCALE * jnp.sum(block * block, axis=0, keepdims=True)


def put_weights(block, wcat, start):
    high, low = split2(block)
    wcat[pl.ds(start, block.shape[0]), 0:WCOL] = high
    wcat[pl.ds(start, block.shape[0]), WCOL : 2 * WCOL] = low


def put_target(both, left, at):
    lane = lax.broadcasted_iota(jnp.int32, both.shape, 1)
    first_half = lane < DIM
    first_quarter = lane % DIM < DIM // 2
    high = both.astype(BF16).astype(F32)
    low = both - high
    high_r, low_r = pltpu.roll(high, DIM, 1), pltpu.roll(low, DIM, 1)
    square = both * both * SCALE
    down = square + pltpu.roll(square, 32, 1)
    up = square + pltpu.roll(square, 96, 1)
    up_high = up.astype(BF16).astype(F32)
    down_low = down - down.astype(BF16).astype(F32)
    sums = jnp.where(first_quarter, up_high, down_low)
    left[pl.ds(at, HALF), 0:128] = jnp.where(first_half, high, low_r).astype(BF16)
    left[pl.ds(at, HALF), 128:256] = jnp.where(first_half, high, pltpu.roll(sums, DIM, 1)).astype(BF16)
    left[pl.ds(at + HALF, HALF), 0:128] = jnp.where(first_half, high_r, low).astype(BF16)
    left[pl.ds(at + HALF, HALF), 128:256] = jnp.where(first_half, high_r, sums).astype(BF16)


def gather_kernel(
    points_hbm, weights_hbm, proj_hbm, index, table,
    left_hbm, right, norm, wcat_hbm, found,
    left, wcat, payload, gathered, own, points, points2, weights, weights2, proj, coords, coords2, values, values2,
    send, recv, pair_send, pair_recv, load_sem, left_sem,
):
    y, z, x, core = place()
    loads = [
        pltpu.make_async_copy(
            points_hbm.at[:, pl.ds(pl.multiple_of(y * (MINE * LEAF), LEAF), MINE * LEAF)], own, load_sem.at[0]
        ),
        pltpu.make_async_copy(points_hbm, points, load_sem.at[1]),
        pltpu.make_async_copy(weights_hbm, weights, load_sem.at[2]),
    ]

    def proj_load(n):
        at = pl.multiple_of(n * CHUNK, CHUNK)
        return pltpu.make_async_copy(proj_hbm.at[:, pl.ds(at, CHUNK)], proj.at[n % 2], load_sem.at[3 + n % 2])

    for c in loads:
        c.start()
    proj_load(0).start()
    near = [(1, 0), (SIDE - 1, 0), (0, 1), (0, SIDE - 1)]
    peers = [device(y, (z + a) % SIDE, (x + b) % SIDE, core) for a, b in near]
    sibling = device(y, z, x, 1 - core)
    greet(peers + [sibling])

    loads[0].wait()
    for leaf in range(MINE):
        block = own[:, leaf * LEAF : (leaf + 1) * LEAF]
        packed = jnp.concatenate([block[:, :HALF], block[:, HALF:]], axis=0)
        payload[leaf * HALF : (leaf + 1) * HALF, :] = packed.T
    payload[MINE * HALF :, :] = table[...]

    started, swaps, handed = [], [], []

    def spot_of(k, i, j):
        az, ax = moved(k, z, x, -i, -j)
        return az * SIDE + ax

    def copy(k, i, j, first):
        rows = pl.ds(CUTS[k], CUTS[k + 1] - CUTS[k])
        tz, tx = moved(k, z, x, 1 if first else 0, 0 if first else 1)
        arrival = (i + 1) * SIDE + j if first else i * SIDE + j + 1
        number = i if first else SIDE - 1 + i * (SIDE - 1) + j
        target = gathered.at[spot_of(k, i, j), rows]
        c = pltpu.make_async_remote_copy(
            src_ref=payload.at[rows] if i == 0 and j == 0 else target,
            dst_ref=target,
            send_sem=send.at[k, number],
            recv_sem=recv.at[k, arrival],
            device_id=device(y, tz, tx, core),
            device_id_type=MESH,
        )
        c.start()
        started.append(c)

    def forward(level):
        for i in range(SIDE):
            j = level - i
            if not 0 <= j < SIDE:
                continue
            for k in range(4):
                if level > 0:
                    rows = pl.ds(CUTS[k], CUTS[k + 1] - CUTS[k])
                    here = gathered.at[spot_of(k, i, j), rows]
                    pltpu.make_async_copy(here, here, recv.at[k, i * SIDE + j]).wait()
                if j == 0 and i < SIDE - 1:
                    copy(k, i, j, True)
                if j < SIDE - 1:
                    copy(k, i, j, False)

    def swap(n, a, b):
        c = pltpu.make_async_remote_copy(
            src_ref=a, dst_ref=b, send_sem=pair_send.at[n], recv_sem=pair_recv.at[n],
            device_id=sibling, device_id_type=MESH,
        )
        c.start()
        swaps.append(c)

    def targets_at(dz, dx):
        spot = (z + dz) % SIDE * SIDE + (x + dx) % SIDE

        def leaf_rows(leaf, _):
            rows = pl.ds(pl.multiple_of(leaf * HALF, HALF), HALF)
            both = payload[rows, :] if dz == dx == 0 else gathered[spot, rows, :]
            put_target(both, left, pl.multiple_of((spot * MINE + leaf) * LEAF, LEAF))
            return _

        lax.fori_loop(0, MINE, leaf_rows, 0)
        lists_here = payload[MINE * HALF :, :] if dz == dx == 0 else gathered[spot, MINE * HALF :, :]
        found[spot] = lists_here.astype(jnp.int32)
        rows = pl.ds(pl.multiple_of(spot * (MINE * LEAF), LEAF), MINE * LEAF)
        c = pltpu.make_async_copy(left.at[rows], left_hbm.at[rows], left_sem.at[dz * SIDE + dx])
        c.start()
        handed.append(c)

    def column(points_ref, weights_ref, base):
        def one(n, _):
            at = pl.multiple_of(n * LEAF, LEAF)
            put_source(points_ref[:, pl.ds(at, LEAF)], right, norm, pl.multiple_of(base + at, LEAF))
            put_weights(weights_ref[pl.ds(at, LEAF), :], wcat, pl.multiple_of(base + at, LEAF))
            return _

        lax.fori_loop(0, LEAVES, one, 0)

    def spots_of(level):
        steps = (0, 1, 2, 3)

        def done(dz, dx):
            far = lambda d: max(d, (SIDE - d) % SIDE)
            return far(dz) + far(dx)

        return [(dz, dx) for dz in steps for dx in steps if done(dz, dx) == level]

    forward(0)
    loads[1].wait()
    loads[2].wait()
    swap(0, points, points2)
    swap(1, weights, weights2)
    targets_at(0, 0)
    column(points, weights, 0)
    forward(1)
    values[...] = jnp.zeros_like(values)
    coords[...] = jnp.zeros_like(coords)

    def skeleton(n, _):
        proj_load(n).wait()

        @pl.when(n + 1 < COLPTS // CHUNK)
        def next_load():
            proj_load(n + 1).start()

        at = pl.multiple_of(n * CHUNK, CHUNK)
        wh, wl = wcat[pl.ds(at, CHUNK), 0:WCOL], wcat[pl.ds(at, CHUNK), WCOL : 2 * WCOL]
        ph, plow = split2(proj[n % 2])
        values[...] += mm(ph, wh) + mm(ph, wl) + mm(plow, wh)
        rows = lax.broadcasted_iota(jnp.int32, (CHUNK, SKEL), 0) + at
        pick = jnp.where(rows == index[...], 1.0, 0.0).astype(BF16)
        block = points[:, pl.ds(at, CHUNK)]
        first = block.astype(BF16)
        second, third = split2(block - first.astype(F32))
        coords[...] += mm(first, pick) + mm(second, pick) + mm(third, pick)
        return _

    lax.fori_loop(0, COLPTS // CHUNK, skeleton, 0)
    swap(2, coords, coords2)
    swap(3, values, values2)
    forward(2)
    put_source(coords[...], right, norm, 2 * COLPTS)
    put_weights(values[...], wcat, 2 * COLPTS)
    swaps[0].wait_recv()
    swaps[1].wait_recv()
    column(points2, weights2, COLPTS)
    forward(3)
    swaps[2].wait_recv()
    swaps[3].wait_recv()
    put_source(coords2[...], right, norm, 2 * COLPTS + SKEL)
    put_weights(values2[...], wcat, 2 * COLPTS + SKEL)
    handed.append(pltpu.make_async_copy(wcat, wcat_hbm, load_sem.at[5]))
    handed[-1].start()
    for level in (2, 3):
        for dz, dx in spots_of(level):
            targets_at(dz, dx)
    for level in (4, 5, 6):
        forward(level)
        for dz, dx in spots_of(level):
            targets_at(dz, dx)
    for c in started + swaps:
        c.wait_send()
    for c in handed:
        c.wait()


def gather(points, weights, proj, index, table):
    hbm = pl.BlockSpec(memory_space=pltpu.HBM)
    vmem = pl.BlockSpec(memory_space=VMEM)
    return pl.pallas_call(
        gather_kernel,
        out_shape=(
            pltpu.HBM((TARGETS * LEAF, 256), BF16),
            pltpu.VMEM((4 * DIM, SOURCES), BF16),
            pltpu.VMEM((1, SOURCES), F32),
            pltpu.HBM((SOURCES, 2 * WCOL), BF16),
            jax.ShapeDtypeStruct((SPOTS, 8, 128), jnp.int32),
        ),
        in_specs=[hbm] * 3 + [vmem] * 2,
        out_specs=[hbm, vmem, vmem, hbm, vmem],
        scratch_shapes=[
            VMEM((TARGETS * LEAF, 256), BF16),
            VMEM((SOURCES, 2 * WCOL), BF16),
            VMEM((PAYLOAD, 128), F32),
            VMEM((SPOTS, PAYLOAD, 128), F32),
            VMEM((DIM, MINE * LEAF), F32),
            VMEM((DIM, COLPTS), F32),
            VMEM((DIM, COLPTS), F32),
            VMEM((COLPTS, WCOL), F32),
            VMEM((COLPTS, WCOL), F32),
            VMEM((2, SKEL, CHUNK), F32),
            VMEM((DIM, SKEL), F32),
            VMEM((DIM, SKEL), F32),
            VMEM((SKEL, WCOL), F32),
            VMEM((SKEL, WCOL), F32),
            pltpu.SemaphoreType.DMA((4, 15)),
            pltpu.SemaphoreType.DMA((4, 16)),
            pltpu.SemaphoreType.DMA((4,)),
            pltpu.SemaphoreType.DMA((4,)),
            pltpu.SemaphoreType.DMA((6,)),
            pltpu.SemaphoreType.DMA((SPOTS,)),
        ],
        compiler_params=pltpu.CompilerParams(
            collective_id=0, has_side_effects=True, vmem_limit_bytes=K1_VMEM
        ),
    )(points, weights, proj, index, table)


def pair_kernel(
    spot_ref, table, left_hbm, right, norm, wcat_hbm, out,
    even, even_low, odd, odd_low, left, wcat, near_pairs, far_pairs, sem,
):
    loads = [
        pltpu.make_async_copy(wcat_hbm, wcat, sem.at[0]),
        pltpu.make_async_copy(left_hbm, left, sem.at[1]),
    ]
    for c in loads:
        c.start()

    def zero(t, _):
        out[pl.ds(pl.multiple_of(t * LEAF, LEAF), LEAF), :] = jnp.zeros((LEAF, WCOL), F32)
        return _

    lax.fori_loop(0, TARGETS + 1, zero, 0)
    spot = spot_ref[0]

    def note(t, counts):
        near, far = counts
        for slot in range(4):
            source = table[t // MINE, t % MINE, 4 * spot + slot]
            near_pairs[near] = t * 64 + source
            near = near + jnp.where(source >= 0, 1, 0)
        for slot in range(2):
            node = table[t // MINE, t % MINE, 64 + 2 * spot + slot]
            far_pairs[far] = t * 64 + node
            far = far + jnp.where(node >= 0, 1, 0)
        return near, far

    near_count, far_count = lax.fori_loop(0, TARGETS, note, (0, 0))
    for c in loads:
        c.wait()
    for extra in range(3):
        near_pairs[near_count + extra] = TARGETS * 64
        far_pairs[far_count + extra] = TARGETS * 64

    def run(pair_list, count, base, width):
        def columns(code):
            return pl.ds(pl.multiple_of(base + (code % 64) * width, width), width)

        def produce(n, high_ref, low_ref):
            code = pair_list[n]
            t, where = code // 64, columns(code)
            at = pl.multiple_of(jnp.where(t < TARGETS, t, 0) * LEAF, LEAF)
            power = mm(left[pl.ds(at, LEAF), :], right[:, where]) + norm[:, where]
            high_ref[:, :width], low_ref[:, :width] = split2(jnp.exp2(power))

        def consume(n, high_ref, low_ref):
            code = pair_list[n]
            t, where = code // 64, columns(code)
            total = mm(high_ref[:, :width], wcat[where, :])
            rest = mm(low_ref[:, :width], wcat[where, 0:WCOL])
            at = pl.multiple_of(t * LEAF, LEAF)
            out[pl.ds(at, LEAF), :] += total[:, :WCOL] + total[:, WCOL:] + rest

        produce(0, even, even_low)

        def two(m, _):
            produce(2 * m + 1, odd, odd_low)
            consume(2 * m, even, even_low)
            produce(2 * m + 2, even, even_low)
            consume(2 * m + 1, odd, odd_low)
            return _

        lax.fori_loop(0, (count + 1) // 2, two, 0)

    run(near_pairs, near_count, 0, LEAF)
    run(far_pairs, far_count, 2 * COLPTS, SKEL)


def pairs(spot, table, left, right, norm, wcat):
    smem = pl.BlockSpec(memory_space=pltpu.SMEM)
    vmem = pl.BlockSpec(memory_space=VMEM)
    hbm = pl.BlockSpec(memory_space=pltpu.HBM)
    return pl.pallas_call(
        pair_kernel,
        out_shape=pltpu.VMEM(((TARGETS + 1) * LEAF, WCOL), F32),
        in_specs=[smem, smem, hbm, vmem, vmem, hbm],
        out_specs=vmem,
        scratch_shapes=[VMEM((LEAF, LEAF), BF16)] * 4
        + [
            VMEM((TARGETS * LEAF, 256), BF16),
            VMEM((SOURCES, 2 * WCOL), BF16),
            pltpu.SMEM((TARGETS * 4 + 3,), jnp.int32),
            pltpu.SMEM((TARGETS * 2 + 3,), jnp.int32),
            pltpu.SemaphoreType.DMA((2,)),
        ],
        compiler_params=pltpu.CompilerParams(vmem_limit_bytes=K2_VMEM),
    )(spot, table, left, right, norm, wcat)


QUARTER = LEAF // 4


def scatter_kernel(partial, out, slots, turn, send, recv, turn_send, turn_recv, y_send, y_recv):
    y, z, x, core = place()
    near = [(1, 0), (SIDE - 1, 0), (0, 1), (0, SIDE - 1)]
    peers = [device(y, (z + a) % SIDE, (x + b) % SIDE, core) for a, b in near]
    above, below = device((y + 1) % SIDE, z, x, core), device((y + SIDE - 1) % SIDE, z, x, core)
    greet(peers + [above, below])
    started = []

    def own(k, leaf, first, second):
        az, ax = moved(k, z, x, first, second)
        start = ((az * SIDE + ax) * MINE + leaf) * LEAF + k * QUARTER
        return pl.ds(pl.multiple_of(start, QUARTER), QUARTER)

    def begin(c):
        c.start()
        started.append(c)

    def step_first(k, leaf, step, j, source):
        tz, tx = moved(k, z, x, 1, 0)
        n = (leaf * 3 + step) * SIDE + j
        begin(pltpu.make_async_remote_copy(
            src_ref=source, dst_ref=slots.at[k, n], send_sem=send.at[k, n], recv_sem=recv.at[k, n],
            device_id=device(y, tz, tx, core), device_id_type=MESH,
        ))

    def arrived_first(k, leaf, step, j):
        n = (leaf * 3 + step) * SIDE + j
        pltpu.make_async_copy(slots.at[k, n], slots.at[k, n], recv.at[k, n]).wait()
        slots[k, n] += partial[own(k, leaf, 2 - step, 3 - j), :]
        return n

    def step_second(k, leaf, step, source):
        tz, tx = moved(k, z, x, 0, 1)
        n = leaf * 3 + step
        begin(pltpu.make_async_remote_copy(
            src_ref=source, dst_ref=turn.at[k, n], send_sem=turn_send.at[k, n], recv_sem=turn_recv.at[k, n],
            device_id=device(y, tz, tx, core), device_id_type=MESH,
        ))

    def rows_of(plane, leaf, k):
        return pl.ds(pl.multiple_of((plane * MINE + leaf) * LEAF + k * QUARTER, QUARTER), QUARTER)

    def to_y(leaf, k, number, plane, up):
        rows = rows_of(plane, leaf, k)
        n = (leaf * 4 + k) * 3 + number
        begin(pltpu.make_async_remote_copy(
            src_ref=out.at[rows], dst_ref=out.at[rows], send_sem=y_send.at[n], recv_sem=y_recv.at[n],
            device_id=above if up else below, device_id_type=MESH,
        ))

    def y_wait(leaf, k, number, plane):
        rows = rows_of(plane, leaf, k)
        n = (leaf * 4 + k) * 3 + number
        pltpu.make_async_copy(out.at[rows], out.at[rows], y_recv.at[n]).wait()

    def second_axis(k, leaf, j):
        n = arrived_first(k, leaf, 2, j)
        if j > 0:
            m = leaf * 3 + j - 1
            pltpu.make_async_copy(turn.at[k, m], turn.at[k, m], turn_recv.at[k, m]).wait()
        if j == 0:
            step_second(k, leaf, 0, slots.at[k, n])
        elif j < 3:
            turn[k, m] += slots[k, n]
            step_second(k, leaf, j, turn.at[k, m])
        else:
            out[rows_of(y, leaf, k), :] = turn[k, m] + slots[k, n]
            to_y(leaf, k, 0, y, True)
            to_y(leaf, k, 1, y, False)

    def second_hop(leaf, k):
        lower, upper = (y + SIDE - 1) % SIDE, (y + 1) % SIDE
        if k % 2 == 0:
            y_wait(leaf, k, 0, lower)
            to_y(leaf, k, 2, lower, True)
        else:
            y_wait(leaf, k, 1, upper)
            to_y(leaf, k, 2, upper, False)

    def last_arrivals(leaf, k):
        lower, upper, across = (y + SIDE - 1) % SIDE, (y + 1) % SIDE, (y + 2) % SIDE
        if k % 2 == 0:
            y_wait(leaf, k, 1, upper)
        else:
            y_wait(leaf, k, 0, lower)
        y_wait(leaf, k, 2, across)

    for leaf in range(MINE + 1):
        if leaf < MINE:
            for j in range(SIDE):
                for k in range(4):
                    step_first(k, leaf, 0, j, partial.at[own(k, leaf, 3, 3 - j)])
        for j in range(SIDE):
            for k in range(4):
                if leaf < MINE:
                    n = arrived_first(k, leaf, 0, j)
                    step_first(k, leaf, 1, j, slots.at[k, n])
                if leaf > 0:
                    second_axis(k, leaf - 1, j)
        if leaf < MINE:
            for j in range(SIDE):
                for k in range(4):
                    n = arrived_first(k, leaf, 1, j)
                    step_first(k, leaf, 2, j, slots.at[k, n])
        if leaf > 0:
            for k in range(4):
                second_hop(leaf - 1, k)
    for leaf in range(MINE):
        for k in range(4):
            last_arrivals(leaf, k)
    for c in started:
        c.wait_send()


def scatter(partial):
    vmem = pl.BlockSpec(memory_space=VMEM)
    return pl.pallas_call(
        scatter_kernel,
        out_shape=jax.ShapeDtypeStruct((COLPTS, WCOL), F32),
        in_specs=[vmem],
        out_specs=vmem,
        scratch_shapes=[
            VMEM((4, MINE * 3 * SIDE, QUARTER, WCOL), F32),
            VMEM((4, MINE * 3, QUARTER, WCOL), F32),
            pltpu.SemaphoreType.DMA((4, MINE * 3 * SIDE)),
            pltpu.SemaphoreType.DMA((4, MINE * 3 * SIDE)),
            pltpu.SemaphoreType.DMA((4, MINE * 3)),
            pltpu.SemaphoreType.DMA((4, MINE * 3)),
            pltpu.SemaphoreType.DMA((MINE * 4 * 3,)),
            pltpu.SemaphoreType.DMA((MINE * 4 * 3,)),
        ],
        compiler_params=pltpu.CompilerParams(
            collective_id=1, has_side_effects=True, vmem_limit_bytes=K3_VMEM
        ),
    )(partial)


def lists(y, core, fetch_table, near_list, far_list):
    near = lax.dynamic_slice_in_dim(near_list, y * MINE, MINE, 0)
    far = lax.dynamic_slice_in_dim(far_list, y * MINE, MINE, 0)
    slots = jnp.arange(64, dtype=jnp.int32)
    nodes = jnp.arange(32, dtype=jnp.int32)
    near_used = jnp.any(near[:, :, None] == slots, axis=1)
    far_used = jnp.any(far[:, :, None] == nodes, axis=1)
    rows = (y * MINE + jnp.arange(MINE, dtype=jnp.int32)) // 4
    requests = fetch_table[:, 0].reshape(3, 64)
    local = jnp.sum(jnp.where(rows[:, None, None] == jnp.arange(3)[None, :, None], requests[None], 0), axis=1)
    side = (slots // 2 + core) % 2
    near_value = jnp.where(near_used, side * LEAVES + local, -1)
    far_value = jnp.where(far_used, (nodes + core) % 2, -1)
    table = jnp.concatenate([near_value, far_value, jnp.full((MINE, 32), -1, jnp.int32)], axis=1)
    return jnp.pad(table, ((0, 8 - MINE), (0, 0))).astype(F32)


def on_device(points, weights, proj, fetch_table, near_list, far_list, skel_idx):
    y, z, x, core = place()
    table = lists(y, core, fetch_table, near_list, far_list)
    fixed = pltpu.with_memory_space_constraint
    points, weights, proj = (fixed(a, pltpu.HBM) for a in (points, weights, proj))
    left, right, norm, wcat, found = gather(points, weights, proj, skel_idx, table)
    spot = (z * SIDE + x).reshape(1).astype(jnp.int32)
    partial = pairs(
        spot, found, fixed(left, pltpu.HBM), fixed(right, VMEM), fixed(norm, VMEM), fixed(wcat, pltpu.HBM)
    )
    partial = fixed(partial, VMEM)
    return scatter(partial)


def solution(mesh):
    placed = (
        P(None, "dev"),
        P("dev", None),
        P(None, "dev"),
        P(None, "dev", None, None),
        P("dev", None),
        P("dev", None),
        P("dev", None),
    )
    return jax.shard_map(
        on_device, mesh=mesh, in_specs=placed, out_specs=P("dev", None), check_vma=False
    )
```

```python
import functools
import math

import jax
import jax.numpy as jnp
from jax import lax
from jax.experimental import pallas as pl
from jax.experimental.pallas import tpu as pltpu
from jax.sharding import PartitionSpec as P

F32, BF16 = jnp.float32, jnp.bfloat16
MESH = pl.DeviceIdType.MESH
VMEM = pltpu.VMEM
LOG2E = math.log2(math.e)
SIDE = 4
SPOTS = SIDE * SIDE
LEAF, DIM, WCOL, SKEL = 512, 64, 128, 256
LEAVES = 12
MINE = 3
COLPTS = LEAVES * LEAF
HALF = LEAF // 2
PAYLOAD = MINE * HALF + 8
TARGETS = SPOTS * MINE
IDLE = 2 * COLPTS + 2 * SKEL
SOURCES = IDLE + LEAF
BLOCK = 256
BLOCKS = SOURCES // BLOCK
LATER = (MINE - 1) * SPOTS
CHUNK = 1024
SCALE = LOG2E / 32.0
K1_VMEM, K2_VMEM, K3_VMEM = 44 << 20, 33 << 20, 42 << 20
CUTS = (0, 192, 384, 576, PAYLOAD)


def mm(a, b):
    return jnp.dot(a, b, preferred_element_type=F32)


def split2(v):
    high = v.astype(BF16)
    return high, (v - high.astype(F32)).astype(BF16)


def place():
    y, dev = lax.axis_index("grp"), lax.axis_index("dev")
    return y, dev // 8, (dev // 2) % SIDE, dev % 2


def device(y, z, x, core):
    return (y, (z * SIDE + x) * 2 + core)


def stream_axes(k):
    return k < 2, 1 if k % 2 == 0 else SIDE - 1


def moved(k, z, x, first, second):
    x_first, sign = stream_axes(k)
    along_x, along_z = (first, second) if x_first else (second, first)
    return (z + sign * along_z) % SIDE, (x + sign * along_x) % SIDE


def greet(peers):
    barrier = pltpu.get_barrier_semaphore()
    for peer in peers:
        pl.semaphore_signal(barrier, inc=1, device_id=peer, device_id_type=MESH)
    pl.semaphore_wait(barrier, len(peers))


def put_source(block, right, norm, first):
    high, low = split2(block * (2.0 * SCALE))
    total = -SCALE * jnp.sum(block * block, axis=0, keepdims=True)
    for n in range(block.shape[1] // BLOCK):
        cols = slice(n * BLOCK, (n + 1) * BLOCK)
        right[first + n, 0:DIM, :] = high[:, cols]
        right[first + n, DIM : 2 * DIM, :] = high[:, cols]
        right[first + n, 2 * DIM : 3 * DIM, :] = low[:, cols]
        right[first + n, 3 * DIM : 4 * DIM, :] = jnp.full((DIM, BLOCK), -1.0, BF16)
        norm[first + n] = total[:, cols]


def put_weights(block, wcat, first):
    high, low = split2(block)
    for n in range(block.shape[0] // BLOCK):
        rows = slice(n * BLOCK, (n + 1) * BLOCK)
        wcat[first + n, :, 0:WCOL] = high[rows]
        wcat[first + n, :, WCOL : 2 * WCOL] = low[rows]


def put_target(both, left, at):
    lane = lax.broadcasted_iota(jnp.int32, both.shape, 1)
    first_half = lane < DIM
    first_quarter = lane % DIM < DIM // 2
    high = both.astype(BF16).astype(F32)
    low = both - high
    high_r, low_r = pltpu.roll(high, DIM, 1), pltpu.roll(low, DIM, 1)
    square = both * both * SCALE
    down = square + pltpu.roll(square, 32, 1)
    up = square + pltpu.roll(square, 96, 1)
    up_high = up.astype(BF16).astype(F32)
    down_low = down - down.astype(BF16).astype(F32)
    sums = jnp.where(first_quarter, up_high, down_low)
    left[pl.ds(at, HALF), 0:128] = jnp.where(first_half, high, low_r).astype(BF16)
    left[pl.ds(at, HALF), 128:256] = jnp.where(first_half, high, pltpu.roll(sums, DIM, 1)).astype(BF16)
    left[pl.ds(at + HALF, HALF), 0:128] = jnp.where(first_half, high_r, low).astype(BF16)
    left[pl.ds(at + HALF, HALF), 128:256] = jnp.where(first_half, high_r, sums).astype(BF16)


def gather_kernel(
    points_hbm, weights_hbm, proj_hbm, index, table,
    left_hbm, right, norm, wcat_hbm, found,
    left, wcat, payload, gathered, own, points, points2, weights, weights2, proj, coords, coords2, values, values2,
    send, recv, pair_send, pair_recv, load_sem, left_sem,
):
    y, z, x, core = place()
    loads = [
        pltpu.make_async_copy(
            points_hbm.at[:, pl.ds(pl.multiple_of(y * (MINE * LEAF), LEAF), MINE * LEAF)], own, load_sem.at[0]
        ),
        pltpu.make_async_copy(points_hbm, points, load_sem.at[1]),
        pltpu.make_async_copy(weights_hbm, weights, load_sem.at[2]),
    ]

    def proj_load(n):
        at = pl.multiple_of(n * CHUNK, CHUNK)
        return pltpu.make_async_copy(proj_hbm.at[:, pl.ds(at, CHUNK)], proj.at[n % 2], load_sem.at[3 + n % 2])

    for c in loads:
        c.start()
    proj_load(0).start()
    near = [(1, 0), (SIDE - 1, 0), (0, 1), (0, SIDE - 1)]
    peers = [device(y, (z + a) % SIDE, (x + b) % SIDE, core) for a, b in near]
    sibling = device(y, z, x, 1 - core)
    greet(peers + [sibling])

    loads[0].wait()
    for leaf in range(MINE):
        block = own[:, leaf * LEAF : (leaf + 1) * LEAF]
        packed = jnp.concatenate([block[:, :HALF], block[:, HALF:]], axis=0)
        payload[leaf * HALF : (leaf + 1) * HALF, :] = packed.T
    payload[MINE * HALF :, :] = table[...]

    started, swaps, handed = [], [], []

    def spot_of(k, i, j):
        az, ax = moved(k, z, x, -i, -j)
        return az * SIDE + ax

    def copy(k, i, j, first):
        rows = pl.ds(CUTS[k], CUTS[k + 1] - CUTS[k])
        tz, tx = moved(k, z, x, 1 if first else 0, 0 if first else 1)
        arrival = (i + 1) * SIDE + j if first else i * SIDE + j + 1
        number = i if first else SIDE - 1 + i * (SIDE - 1) + j
        target = gathered.at[spot_of(k, i, j), rows]
        c = pltpu.make_async_remote_copy(
            src_ref=payload.at[rows] if i == 0 and j == 0 else target,
            dst_ref=target,
            send_sem=send.at[k, number],
            recv_sem=recv.at[k, arrival],
            device_id=device(y, tz, tx, core),
            device_id_type=MESH,
        )
        c.start()
        started.append(c)

    def forward(level):
        for i in range(SIDE):
            j = level - i
            if not 0 <= j < SIDE:
                continue
            for k in range(4):
                if level > 0:
                    rows = pl.ds(CUTS[k], CUTS[k + 1] - CUTS[k])
                    here = gathered.at[spot_of(k, i, j), rows]
                    pltpu.make_async_copy(here, here, recv.at[k, i * SIDE + j]).wait()
                if j == 0 and i < SIDE - 1:
                    copy(k, i, j, True)
                if j < SIDE - 1:
                    copy(k, i, j, False)

    def swap(n, a, b):
        c = pltpu.make_async_remote_copy(
            src_ref=a, dst_ref=b, send_sem=pair_send.at[n], recv_sem=pair_recv.at[n],
            device_id=sibling, device_id_type=MESH,
        )
        c.start()
        swaps.append(c)

    def targets_at(dz, dx):
        spot = (z + dz) % SIDE * SIDE + (x + dx) % SIDE

        def leaf_rows(leaf, _):
            rows = pl.ds(pl.multiple_of(leaf * HALF, HALF), HALF)
            both = payload[rows, :] if dz == dx == 0 else gathered[spot, rows, :]
            put_target(both, left, pl.multiple_of((leaf * SPOTS + spot) * LEAF, LEAF))
            return _

        lax.fori_loop(0, MINE, leaf_rows, 0)
        lists_here = payload[MINE * HALF :, :] if dz == dx == 0 else gathered[spot, MINE * HALF :, :]
        found[spot] = lists_here.astype(jnp.int32)
        for leaf in range(MINE):
            rows = pl.ds(pl.multiple_of((leaf * SPOTS + spot) * LEAF, LEAF), LEAF)
            c = pltpu.make_async_copy(left.at[rows], left_hbm.at[rows], left_sem.at[leaf, dz * SIDE + dx])
            c.start()
            handed.append(c)

    def column(points_ref, weights_ref, base):
        def one(n, _):
            at = pl.multiple_of(n * LEAF, LEAF)
            put_source(points_ref[:, pl.ds(at, LEAF)], right, norm, base + 2 * n)
            put_weights(weights_ref[pl.ds(at, LEAF), :], wcat, base + 2 * n)
            return _

        lax.fori_loop(0, LEAVES, one, 0)

    def spots_of(level):
        steps = (0, 1, 2, 3)

        def done(dz, dx):
            far = lambda d: max(d, (SIDE - d) % SIDE)
            return far(dz) + far(dx)

        return [(dz, dx) for dz in steps for dx in steps if done(dz, dx) == level]

    forward(0)
    loads[1].wait()
    loads[2].wait()
    swap(0, points, points2)
    swap(1, weights, weights2)
    targets_at(0, 0)
    for n in range(IDLE // BLOCK, BLOCKS):
        right[n] = jnp.zeros((4 * DIM, BLOCK), BF16)
        norm[n] = jnp.zeros((1, BLOCK), F32)
        wcat[n] = jnp.zeros((BLOCK, 2 * WCOL), BF16)
    column(points, weights, 0)
    forward(1)
    values[...] = jnp.zeros_like(values)
    coords[...] = jnp.zeros_like(coords)

    def skeleton(n, _):
        proj_load(n).wait()

        @pl.when(n + 1 < COLPTS // CHUNK)
        def next_load():
            proj_load(n + 1).start()

        at = pl.multiple_of(n * CHUNK, CHUNK)
        four = pl.ds(n * (CHUNK // BLOCK), CHUNK // BLOCK)
        wh, wl = wcat[four, :, 0:WCOL].reshape(CHUNK, WCOL), wcat[four, :, WCOL : 2 * WCOL].reshape(CHUNK, WCOL)
        ph, plow = split2(proj[n % 2])
        values[...] += mm(ph, wh) + mm(ph, wl) + mm(plow, wh)
        rows = lax.broadcasted_iota(jnp.int32, (CHUNK, SKEL), 0) + at
        pick = jnp.where(rows == index[...], 1.0, 0.0).astype(BF16)
        block = points[:, pl.ds(at, CHUNK)]
        first = block.astype(BF16)
        second, third = split2(block - first.astype(F32))
        coords[...] += mm(first, pick) + mm(second, pick) + mm(third, pick)
        return _

    lax.fori_loop(0, COLPTS // CHUNK, skeleton, 0)
    swap(2, coords, coords2)
    swap(3, values, values2)
    forward(2)
    put_source(coords[...], right, norm, 2 * COLPTS // BLOCK)
    put_weights(values[...], wcat, 2 * COLPTS // BLOCK)
    swaps[0].wait_recv()
    swaps[1].wait_recv()
    column(points2, weights2, COLPTS // BLOCK)
    forward(3)
    swaps[2].wait_recv()
    swaps[3].wait_recv()
    put_source(coords2[...], right, norm, (2 * COLPTS + SKEL) // BLOCK)
    put_weights(values2[...], wcat, (2 * COLPTS + SKEL) // BLOCK)
    handed.append(pltpu.make_async_copy(wcat, wcat_hbm, load_sem.at[5]))
    handed[-1].start()
    for level in (2, 3):
        for dz, dx in spots_of(level):
            targets_at(dz, dx)
    for level in (4, 5, 6):
        forward(level)
        for dz, dx in spots_of(level):
            targets_at(dz, dx)
    for c in started + swaps:
        c.wait_send()
    for c in handed:
        c.wait()


def gather(points, weights, proj, index, table):
    hbm = pl.BlockSpec(memory_space=pltpu.HBM)
    vmem = pl.BlockSpec(memory_space=VMEM)
    return pl.pallas_call(
        gather_kernel,
        out_shape=(
            pltpu.HBM((TARGETS * LEAF, 256), BF16),
            pltpu.VMEM((BLOCKS, 4 * DIM, BLOCK), BF16),
            pltpu.VMEM((BLOCKS, 1, BLOCK), F32),
            pltpu.HBM((BLOCKS, BLOCK, 2 * WCOL), BF16),
            jax.ShapeDtypeStruct((SPOTS, 8, 128), jnp.int32),
        ),
        in_specs=[hbm] * 3 + [vmem] * 2,
        out_specs=[hbm, vmem, vmem, hbm, vmem],
        scratch_shapes=[
            VMEM((TARGETS * LEAF, 256), BF16),
            VMEM((BLOCKS, BLOCK, 2 * WCOL), BF16),
            VMEM((PAYLOAD, 128), F32),
            VMEM((SPOTS, PAYLOAD, 128), F32),
            VMEM((DIM, MINE * LEAF), F32),
            VMEM((DIM, COLPTS), F32),
            VMEM((DIM, COLPTS), F32),
            VMEM((COLPTS, WCOL), F32),
            VMEM((COLPTS, WCOL), F32),
            VMEM((2, SKEL, CHUNK), F32),
            VMEM((DIM, SKEL), F32),
            VMEM((DIM, SKEL), F32),
            VMEM((SKEL, WCOL), F32),
            VMEM((SKEL, WCOL), F32),
            pltpu.SemaphoreType.DMA((4, 15)),
            pltpu.SemaphoreType.DMA((4, 16)),
            pltpu.SemaphoreType.DMA((4,)),
            pltpu.SemaphoreType.DMA((4,)),
            pltpu.SemaphoreType.DMA((6,)),
            pltpu.SemaphoreType.DMA((MINE, SPOTS)),
        ],
        compiler_params=pltpu.CompilerParams(
            collective_id=0, has_side_effects=True, vmem_limit_bytes=K1_VMEM
        ),
    )(points, weights, proj, index, table)


def produce(left, right, norm, at, block, width, high_ref, low_ref):
    blocks = range(width // BLOCK)
    columns = jnp.concatenate([right[block + n] for n in blocks], axis=1)
    norms = jnp.concatenate([norm[block + n] for n in blocks], axis=1)
    power = mm(left[pl.ds(at, LEAF), :], columns) + norms
    high_ref[:, :width], low_ref[:, :width] = split2(jnp.exp2(power))


def consume(wcat, out, at, block, width, high_ref, low_ref):
    rows = jnp.concatenate([wcat[block + n] for n in range(width // BLOCK)], axis=0)
    total = mm(high_ref[:, :width], rows)
    rest = mm(low_ref[:, :width], rows[:, :WCOL])
    out[pl.ds(at, LEAF), :] += total[:, :WCOL] + total[:, WCOL:] + rest


def near_start(source):
    return source * (LEAF // BLOCK)


def far_start(node):
    return 2 * COLPTS // BLOCK + node


def pair_kernel(
    spot_ref, table, left_hbm, right, norm, wcat_hbm, out, extra_hbm, slots,
    even, even_low, odd, odd_low, left, wcat, extra, near_pairs, far_pairs, near_extra, far_extra, sem,
):
    first = pl.ds(0, SPOTS * LEAF)
    later = pl.ds(SPOTS * LEAF, LATER * LEAF)
    loads = [
        pltpu.make_async_copy(wcat_hbm, wcat, sem.at[0]),
        pltpu.make_async_copy(left_hbm.at[later], left.at[later], sem.at[1]),
        pltpu.make_async_copy(left_hbm.at[first], left.at[first], sem.at[2]),
    ]
    for c in loads:
        c.start()

    def clear(ref, n):
        def zero(t, _):
            ref[pl.ds(pl.multiple_of(t * LEAF, LEAF), LEAF), :] = jnp.zeros((LEAF, WCOL), F32)
            return _

        lax.fori_loop(0, n, zero, 0)

    clear(out, SPOTS + 1)
    clear(extra, LATER + 1)
    spot = spot_ref[0]

    def used(t, slot):
        return table[t % SPOTS, t // SPOTS, slot]

    def note(t, counts):
        near, far = counts
        for slot in range(4):
            source = used(t, 4 * spot + slot)
            near_pairs[near] = t * 64 + source
            near = near + jnp.where(source >= 0, 1, 0)
        for slot in range(2):
            node = used(t, 64 + 2 * spot + slot)
            far_pairs[far] = t * 64 + node
            far = far + jnp.where(node >= 0, 1, 0)
        return near, far

    near_count, far_count = lax.fori_loop(0, SPOTS, note, (0, 0))

    def note_later(t, counts):
        near, far = counts
        slots[t, 0], slots[t, 1], slots[t, 2] = IDLE // LEAF, IDLE // LEAF, 2
        have = 0
        for slot in range(4):
            source = used(t + SPOTS, 4 * spot + slot)
            hit = source >= 0
            take = jnp.logical_and(hit, have < 2)
            slots[t, jnp.where(take, have, 7)] = source
            have = have + jnp.where(take, 1, 0)
            near_extra[near] = t * 64 + source
            near = near + jnp.where(jnp.logical_and(hit, jnp.logical_not(take)), 1, 0)
        have = 0
        for slot in range(2):
            node = used(t + SPOTS, 64 + 2 * spot + slot)
            hit = node >= 0
            take = jnp.logical_and(hit, have < 1)
            slots[t, jnp.where(take, 2, 7)] = node
            have = have + jnp.where(take, 1, 0)
            far_extra[far] = t * 64 + node
            far = far + jnp.where(jnp.logical_and(hit, jnp.logical_not(take)), 1, 0)
        return near, far

    near_more, far_more = lax.fori_loop(0, LATER, note_later, (0, 0))
    for n in range(3):
        near_pairs[near_count + n] = SPOTS * 64
        far_pairs[far_count + n] = SPOTS * 64
        near_extra[near_more + n] = LATER * 64
        far_extra[far_more + n] = LATER * 64

    def run(pair_list, count, start_of, width, ref, n_targets, base):
        def make(n, high_ref, low_ref):
            code = pair_list[n]
            t = code // 64
            at = pl.multiple_of((base + jnp.where(t < n_targets, t, 0)) * LEAF, LEAF)
            produce(left, right, norm, at, start_of(code % 64), width, high_ref, low_ref)

        def use(n, high_ref, low_ref):
            code = pair_list[n]
            at = pl.multiple_of((code // 64) * LEAF, LEAF)
            consume(wcat, ref, at, start_of(code % 64), width, high_ref, low_ref)

        make(0, even, even_low)

        def two(m, _):
            make(2 * m + 1, odd, odd_low)
            use(2 * m, even, even_low)
            make(2 * m + 2, even, even_low)
            use(2 * m + 1, odd, odd_low)
            return _

        lax.fori_loop(0, (count + 1) // 2, two, 0)

    loads[0].wait()
    loads[1].wait()
    run(near_extra, near_more, near_start, LEAF, extra, LATER, SPOTS)
    run(far_extra, far_more, far_start, SKEL, extra, LATER, SPOTS)
    handed = pltpu.make_async_copy(extra.at[pl.ds(0, LATER * LEAF)], extra_hbm, sem.at[3])
    handed.start()
    loads[2].wait()
    run(near_pairs, near_count, near_start, LEAF, out, SPOTS, 0)
    run(far_pairs, far_count, far_start, SKEL, out, SPOTS, 0)
    handed.wait()


def pairs(spot, table, left, right, norm, wcat):
    smem = pl.BlockSpec(memory_space=pltpu.SMEM)
    vmem = pl.BlockSpec(memory_space=VMEM)
    hbm = pl.BlockSpec(memory_space=pltpu.HBM)
    return pl.pallas_call(
        pair_kernel,
        out_shape=(
            pltpu.VMEM(((SPOTS + 1) * LEAF, WCOL), F32),
            pltpu.HBM((LATER * LEAF, WCOL), F32),
            jax.ShapeDtypeStruct((LATER, 8), jnp.int32),
        ),
        in_specs=[smem, smem, hbm, vmem, vmem, hbm],
        out_specs=(vmem, hbm, smem),
        scratch_shapes=[VMEM((LEAF, LEAF), BF16)] * 4
        + [
            VMEM((TARGETS * LEAF, 256), BF16),
            VMEM((BLOCKS, BLOCK, 2 * WCOL), BF16),
            VMEM(((LATER + 1) * LEAF, WCOL), F32),
            pltpu.SMEM((SPOTS * 4 + 3,), jnp.int32),
            pltpu.SMEM((SPOTS * 2 + 3,), jnp.int32),
            pltpu.SMEM((LATER * 4 + 3,), jnp.int32),
            pltpu.SMEM((LATER * 2 + 3,), jnp.int32),
            pltpu.SemaphoreType.DMA((4,)),
        ],
        compiler_params=pltpu.CompilerParams(vmem_limit_bytes=K2_VMEM),
    )(spot, table, left, right, norm, wcat)


QUARTER = LEAF // 4


def scatter_kernel(
    chosen, partial, extra_hbm, left_hbm, right, norm, wcat_hbm, out,
    slots, turn, sums, left, wcat, even, even_low, odd, odd_low, third, third_low,
    send, recv, turn_send, turn_recv, y_send, y_recv, load_sem,
):
    y, z, x, core = place()
    loads = [
        pltpu.make_async_copy(left_hbm.at[pl.ds(SPOTS * LEAF, LATER * LEAF)], left, load_sem.at[0]),
        pltpu.make_async_copy(wcat_hbm, wcat, load_sem.at[1]),
        pltpu.make_async_copy(extra_hbm, sums, load_sem.at[2]),
    ]
    for c in loads:
        c.start()
    near = [(1, 0), (SIDE - 1, 0), (0, 1), (0, SIDE - 1)]
    peers = [device(y, (z + a) % SIDE, (x + b) % SIDE, core) for a, b in near]
    above, below = device((y + 1) % SIDE, z, x, core), device((y + SIDE - 1) % SIDE, z, x, core)
    greet(peers + [above, below])
    started = []

    def own(k, leaf, first, second):
        az, ax = moved(k, z, x, first, second)
        place_of = az * SIDE + ax + (0 if leaf == 0 else (leaf - 1) * SPOTS)
        rows = pl.ds(pl.multiple_of(place_of * LEAF + k * QUARTER, QUARTER), QUARTER)
        return partial.at[rows] if leaf == 0 else sums.at[rows]

    def begin(make):
        make().start()
        started.append(make)

    def step_first(k, leaf, step, j, source):
        n = (leaf * 3 + step) * SIDE + j

        def make():
            tz, tx = moved(k, z, x, 1, 0)
            return pltpu.make_async_remote_copy(
                src_ref=source(), dst_ref=slots.at[k, n], send_sem=send.at[k, n], recv_sem=recv.at[k, n],
                device_id=device(y, tz, tx, core), device_id_type=MESH,
            )

        begin(make)

    def arrived_first(k, leaf, step, j):
        n = (leaf * 3 + step) * SIDE + j
        pltpu.make_async_copy(slots.at[k, n], slots.at[k, n], recv.at[k, n]).wait()
        slots[k, n] += own(k, leaf, 2 - step, 3 - j)[...]
        return n

    def step_second(k, leaf, step, source):
        n = leaf * 3 + step

        def make():
            tz, tx = moved(k, z, x, 0, 1)
            return pltpu.make_async_remote_copy(
                src_ref=source(), dst_ref=turn.at[k, n], send_sem=turn_send.at[k, n], recv_sem=turn_recv.at[k, n],
                device_id=device(y, tz, tx, core), device_id_type=MESH,
            )

        begin(make)

    def rows_of(plane, leaf, k):
        return pl.ds(pl.multiple_of((plane * MINE + leaf) * LEAF + k * QUARTER, QUARTER), QUARTER)

    def to_y(leaf, k, number, plane, up):
        n = (leaf * 4 + k) * 3 + number

        def make():
            rows = rows_of(plane, leaf, k)
            return pltpu.make_async_remote_copy(
                src_ref=out.at[rows], dst_ref=out.at[rows], send_sem=y_send.at[n], recv_sem=y_recv.at[n],
                device_id=above if up else below, device_id_type=MESH,
            )

        begin(make)

    def y_wait(leaf, k, number, plane):
        rows = rows_of(plane, leaf, k)
        n = (leaf * 4 + k) * 3 + number
        pltpu.make_async_copy(out.at[rows], out.at[rows], y_recv.at[n]).wait()

    def second_axis(k, leaf, j):
        n = arrived_first(k, leaf, 2, j)
        if j > 0:
            m = leaf * 3 + j - 1
            pltpu.make_async_copy(turn.at[k, m], turn.at[k, m], turn_recv.at[k, m]).wait()
        if j == 0:
            step_second(k, leaf, 0, lambda: slots.at[k, n])
        elif j < 3:
            turn[k, m] += slots[k, n]
            step_second(k, leaf, j, lambda: turn.at[k, m])
        else:
            out[rows_of(y, leaf, k), :] = turn[k, m] + slots[k, n]
            to_y(leaf, k, 0, y, True)
            to_y(leaf, k, 1, y, False)

    def second_hop(leaf, k):
        lower, upper = (y + SIDE - 1) % SIDE, (y + 1) % SIDE
        if k % 2 == 0:
            y_wait(leaf, k, 0, lower)
            to_y(leaf, k, 2, lower, True)
        else:
            y_wait(leaf, k, 1, upper)
            to_y(leaf, k, 2, upper, False)

    def last_arrivals(leaf, k):
        lower, upper, across = (y + SIDE - 1) % SIDE, (y + 1) % SIDE, (y + 2) % SIDE
        if k % 2 == 0:
            y_wait(leaf, k, 1, upper)
        else:
            y_wait(leaf, k, 0, lower)
        y_wait(leaf, k, 2, across)

    def start_leaf(leaf):
        for j in range(SIDE):
            for k in range(4):
                step_first(k, leaf, 0, j, functools.partial(own, k, leaf, 3, 3 - j))

    def part(leaf, n):
        j = n % SIDE
        for k in range(4):
            if leaf < MINE:
                m = arrived_first(k, leaf, n // SIDE, j)
                step_first(k, leaf, 1 + n // SIDE, j, lambda k=k, m=m: slots.at[k, m])
            if leaf > 0 and n < SIDE:
                second_axis(k, leaf - 1, j)

    def make(t, slot, width, start_of, high_ref, low_ref):
        at = pl.multiple_of(t * LEAF, LEAF)
        produce(left, right, norm, at, start_of(chosen[t, slot]), width, high_ref, low_ref)

    def use(t, slot, width, start_of, high_ref, low_ref):
        at = pl.multiple_of(t * LEAF, LEAF)
        consume(wcat, sums, at, start_of(chosen[t, slot]), width, high_ref, low_ref)

    def one_target(t):
        make(t, 1, LEAF, near_start, odd, odd_low)
        use(t, 0, LEAF, near_start, even, even_low)
        make(t, 2, SKEL, far_start, third, third_low)
        use(t, 1, LEAF, near_start, odd, odd_low)
        make((t + 1) % LATER, 0, LEAF, near_start, even, even_low)
        use(t, 2, SKEL, far_start, third, third_low)

    for leaf in range(MINE + 1):
        if leaf < MINE:
            start_leaf(leaf)
        if leaf == 0:
            for c in loads:
                c.wait()
            make(0, 0, LEAF, near_start, even, even_low)
        if leaf < MINE - 1:

            def step(n, _, leaf=leaf):
                def inner(m, carry):
                    one_target(leaf * SPOTS + 2 * n + m)
                    return carry

                lax.fori_loop(0, 2, inner, 0)
                for which in range(2 * SIDE):
                    pl.when(n == which)(functools.partial(part, leaf, which))
                return _

            lax.fori_loop(0, 2 * SIDE, step, 0)
        else:
            for n in range(2 * SIDE):
                part(leaf, n)
        if leaf > 0:
            for k in range(4):
                second_hop(leaf - 1, k)
    for leaf in range(MINE):
        for k in range(4):
            last_arrivals(leaf, k)
    for again in started:
        again().wait_send()


def scatter(chosen, partial, extra, left, right, norm, wcat):
    smem = pl.BlockSpec(memory_space=pltpu.SMEM)
    vmem = pl.BlockSpec(memory_space=VMEM)
    hbm = pl.BlockSpec(memory_space=pltpu.HBM)
    return pl.pallas_call(
        scatter_kernel,
        out_shape=jax.ShapeDtypeStruct((COLPTS, WCOL), F32),
        in_specs=[smem, vmem, hbm, hbm, vmem, vmem, hbm],
        out_specs=vmem,
        scratch_shapes=[
            VMEM((4, MINE * 3 * SIDE, QUARTER, WCOL), F32),
            VMEM((4, MINE * 3, QUARTER, WCOL), F32),
            VMEM((LATER * LEAF, WCOL), F32),
            VMEM((LATER * LEAF, 256), BF16),
            VMEM((BLOCKS, BLOCK, 2 * WCOL), BF16),
        ]
        + [VMEM((LEAF, LEAF), BF16)] * 4
        + [VMEM((LEAF, SKEL), BF16)] * 2
        + [
            pltpu.SemaphoreType.DMA((4, MINE * 3 * SIDE)),
            pltpu.SemaphoreType.DMA((4, MINE * 3 * SIDE)),
            pltpu.SemaphoreType.DMA((4, MINE * 3)),
            pltpu.SemaphoreType.DMA((4, MINE * 3)),
            pltpu.SemaphoreType.DMA((MINE * 4 * 3,)),
            pltpu.SemaphoreType.DMA((MINE * 4 * 3,)),
            pltpu.SemaphoreType.DMA((3,)),
        ],
        compiler_params=pltpu.CompilerParams(
            collective_id=1, has_side_effects=True, vmem_limit_bytes=K3_VMEM
        ),
    )(chosen, partial, extra, left, right, norm, wcat)


def lists(y, core, fetch_table, near_list, far_list):
    near = lax.dynamic_slice_in_dim(near_list, y * MINE, MINE, 0)
    far = lax.dynamic_slice_in_dim(far_list, y * MINE, MINE, 0)
    slots = jnp.arange(64, dtype=jnp.int32)
    nodes = jnp.arange(32, dtype=jnp.int32)
    near_used = jnp.any(near[:, :, None] == slots, axis=1)
    far_used = jnp.any(far[:, :, None] == nodes, axis=1)
    rows = (y * MINE + jnp.arange(MINE, dtype=jnp.int32)) // 4
    requests = fetch_table[:, 0].reshape(3, 64)
    local = jnp.sum(jnp.where(rows[:, None, None] == jnp.arange(3)[None, :, None], requests[None], 0), axis=1)
    side = (slots // 2 + core) % 2
    near_value = jnp.where(near_used, side * LEAVES + local, -1)
    far_value = jnp.where(far_used, (nodes + core) % 2, -1)
    table = jnp.concatenate([near_value, far_value, jnp.full((MINE, 32), -1, jnp.int32)], axis=1)
    return jnp.pad(table, ((0, 8 - MINE), (0, 0))).astype(F32)


def on_device(points, weights, proj, fetch_table, near_list, far_list, skel_idx):
    y, z, x, core = place()
    table = lists(y, core, fetch_table, near_list, far_list)
    fixed = pltpu.with_memory_space_constraint
    points, weights, proj = (fixed(a, pltpu.HBM) for a in (points, weights, proj))
    left, right, norm, wcat, found = gather(points, weights, proj, skel_idx, table)
    spot = (z * SIDE + x).reshape(1).astype(jnp.int32)
    left, wcat = fixed(left, pltpu.HBM), fixed(wcat, pltpu.HBM)
    right, norm = fixed(right, VMEM), fixed(norm, VMEM)
    partial, extra, chosen = pairs(spot, found, left, right, norm, wcat)
    return scatter(chosen, fixed(partial, VMEM), fixed(extra, pltpu.HBM), left, right, norm, wcat)


def solution(mesh):
    placed = (
        P(None, "dev"),
        P("dev", None),
        P(None, "dev"),
        P(None, "dev", None, None),
        P("dev", None),
        P("dev", None),
        P("dev", None),
    )
    return jax.shard_map(
        on_device, mesh=mesh, in_specs=placed, out_specs=P("dev", None), check_vma=False
    )
```

```python
import functools
import math

import jax
import jax.numpy as jnp
from jax import lax
from jax.experimental import pallas as pl
from jax.experimental.pallas import tpu as pltpu
from jax.sharding import PartitionSpec as P

F32, BF16 = jnp.float32, jnp.bfloat16
MESH = pl.DeviceIdType.MESH
VMEM = pltpu.VMEM
LOG2E = math.log2(math.e)
SIDE = 4
SPOTS = SIDE * SIDE
LEAF, DIM, WCOL, SKEL = 512, 64, 128, 256
LEAVES = 12
MINE = 3
COLPTS = LEAVES * LEAF
HALF = LEAF // 2
PAYLOAD = MINE * HALF + 8
TARGETS = SPOTS * MINE
IDLE = 2 * COLPTS + 2 * SKEL
SOURCES = IDLE + LEAF
BLOCK = 256
BLOCKS = SOURCES // BLOCK
LATER = (MINE - 1) * SPOTS
CHUNK = 1024
SCALE = LOG2E / 32.0
K1_VMEM, K2_VMEM, K3_VMEM = 44 << 20, 32 << 20, 38 << 20
CUTS = (0, 192, 384, 576, PAYLOAD)


def mm(a, b):
    return jnp.dot(a, b, preferred_element_type=F32)


def split2(v):
    high = v.astype(BF16)
    return high, (v - high.astype(F32)).astype(BF16)


def place():
    y, dev = lax.axis_index("grp"), lax.axis_index("dev")
    return y, dev // 8, (dev // 2) % SIDE, dev % 2


def device(y, z, x, core):
    return (y, (z * SIDE + x) * 2 + core)


def stream_axes(k):
    return k < 2, 1 if k % 2 == 0 else SIDE - 1


def moved(k, z, x, first, second):
    x_first, sign = stream_axes(k)
    along_x, along_z = (first, second) if x_first else (second, first)
    return (z + sign * along_z) % SIDE, (x + sign * along_x) % SIDE


def greet(peers):
    barrier = pltpu.get_barrier_semaphore()
    for peer in peers:
        pl.semaphore_signal(barrier, inc=1, device_id=peer, device_id_type=MESH)
    pl.semaphore_wait(barrier, len(peers))


def put_source(block, right, norm, first):
    high, low = split2(block * (2.0 * SCALE))
    total = -SCALE * jnp.sum(block * block, axis=0, keepdims=True)
    for n in range(block.shape[1] // BLOCK):
        cols = slice(n * BLOCK, (n + 1) * BLOCK)
        right[first + n, 0:DIM, :] = high[:, cols]
        right[first + n, DIM : 2 * DIM, :] = high[:, cols]
        right[first + n, 2 * DIM : 3 * DIM, :] = low[:, cols]
        right[first + n, 3 * DIM : 4 * DIM, :] = jnp.full((DIM, BLOCK), -1.0, BF16)
        norm[first + n] = total[:, cols]


def put_weights(block, wcat, first):
    high, low = split2(block)
    for n in range(block.shape[0] // BLOCK):
        rows = slice(n * BLOCK, (n + 1) * BLOCK)
        wcat[first + n, :, 0:WCOL] = high[rows]
        wcat[first + n, :, WCOL : 2 * WCOL] = low[rows]


def put_target(both, left, at):
    lane = lax.broadcasted_iota(jnp.int32, both.shape, 1)
    first_half = lane < DIM
    first_quarter = lane % DIM < DIM // 2
    high = both.astype(BF16).astype(F32)
    low = both - high
    high_r, low_r = pltpu.roll(high, DIM, 1), pltpu.roll(low, DIM, 1)
    square = both * both * SCALE
    down = square + pltpu.roll(square, 32, 1)
    up = square + pltpu.roll(square, 96, 1)
    up_high = up.astype(BF16).astype(F32)
    down_low = down - down.astype(BF16).astype(F32)
    sums = jnp.where(first_quarter, up_high, down_low)
    left[pl.ds(at, HALF), 0:128] = jnp.where(first_half, high, low_r).astype(BF16)
    left[pl.ds(at, HALF), 128:256] = jnp.where(first_half, high, pltpu.roll(sums, DIM, 1)).astype(BF16)
    left[pl.ds(at + HALF, HALF), 0:128] = jnp.where(first_half, high_r, low).astype(BF16)
    left[pl.ds(at + HALF, HALF), 128:256] = jnp.where(first_half, high_r, sums).astype(BF16)


def gather_kernel(
    points_hbm, weights_hbm, proj_hbm, index, table,
    left_hbm, right, norm, wcat_hbm, found,
    left, wcat, payload, gathered, own, points, points2, weights, weights2, proj, coords, coords2, values, values2,
    send, recv, pair_send, pair_recv, load_sem, left_sem,
):
    y, z, x, core = place()
    loads = [
        pltpu.make_async_copy(
            points_hbm.at[:, pl.ds(pl.multiple_of(y * (MINE * LEAF), LEAF), MINE * LEAF)], own, load_sem.at[0]
        ),
        pltpu.make_async_copy(points_hbm, points, load_sem.at[1]),
        pltpu.make_async_copy(weights_hbm, weights, load_sem.at[2]),
    ]

    def proj_load(n):
        at = pl.multiple_of(n * CHUNK, CHUNK)
        return pltpu.make_async_copy(proj_hbm.at[:, pl.ds(at, CHUNK)], proj.at[n % 2], load_sem.at[3 + n % 2])

    for c in loads:
        c.start()
    proj_load(0).start()
    near = [(1, 0), (SIDE - 1, 0), (0, 1), (0, SIDE - 1)]
    peers = [device(y, (z + a) % SIDE, (x + b) % SIDE, core) for a, b in near]
    sibling = device(y, z, x, 1 - core)
    greet(peers + [sibling])

    loads[0].wait()
    for leaf in range(MINE):
        block = own[:, leaf * LEAF : (leaf + 1) * LEAF]
        packed = jnp.concatenate([block[:, :HALF], block[:, HALF:]], axis=0)
        payload[leaf * HALF : (leaf + 1) * HALF, :] = packed.T
    payload[MINE * HALF :, :] = table[...]

    started, swaps, handed = [], [], []

    def spot_of(k, i, j):
        az, ax = moved(k, z, x, -i, -j)
        return az * SIDE + ax

    def copy(k, i, j, first):
        rows = pl.ds(CUTS[k], CUTS[k + 1] - CUTS[k])
        tz, tx = moved(k, z, x, 1 if first else 0, 0 if first else 1)
        arrival = (i + 1) * SIDE + j if first else i * SIDE + j + 1
        number = i if first else SIDE - 1 + i * (SIDE - 1) + j
        target = gathered.at[spot_of(k, i, j), rows]
        c = pltpu.make_async_remote_copy(
            src_ref=payload.at[rows] if i == 0 and j == 0 else target,
            dst_ref=target,
            send_sem=send.at[k, number],
            recv_sem=recv.at[k, arrival],
            device_id=device(y, tz, tx, core),
            device_id_type=MESH,
        )
        c.start()
        started.append(c)

    def forward(level):
        for i in range(SIDE):
            j = level - i
            if not 0 <= j < SIDE:
                continue
            for k in range(4):
                if level > 0:
                    rows = pl.ds(CUTS[k], CUTS[k + 1] - CUTS[k])
                    here = gathered.at[spot_of(k, i, j), rows]
                    pltpu.make_async_copy(here, here, recv.at[k, i * SIDE + j]).wait()
                if j == 0 and i < SIDE - 1:
                    copy(k, i, j, True)
                if j < SIDE - 1:
                    copy(k, i, j, False)

    def swap(n, a, b):
        c = pltpu.make_async_remote_copy(
            src_ref=a, dst_ref=b, send_sem=pair_send.at[n], recv_sem=pair_recv.at[n],
            device_id=sibling, device_id_type=MESH,
        )
        c.start()
        swaps.append(c)

    def targets_at(dz, dx):
        spot = (z + dz) % SIDE * SIDE + (x + dx) % SIDE

        def leaf_rows(leaf, _):
            rows = pl.ds(pl.multiple_of(leaf * HALF, HALF), HALF)
            both = payload[rows, :] if dz == dx == 0 else gathered[spot, rows, :]
            put_target(both, left, pl.multiple_of((leaf * SPOTS + spot) * LEAF, LEAF))
            return _

        lax.fori_loop(0, MINE, leaf_rows, 0)
        lists_here = payload[MINE * HALF :, :] if dz == dx == 0 else gathered[spot, MINE * HALF :, :]
        found[spot] = lists_here.astype(jnp.int32)
        for leaf in range(MINE):
            rows = pl.ds(pl.multiple_of((leaf * SPOTS + spot) * LEAF, LEAF), LEAF)
            c = pltpu.make_async_copy(left.at[rows], left_hbm.at[rows], left_sem.at[leaf, dz * SIDE + dx])
            c.start()
            handed.append(c)

    def column(points_ref, weights_ref, base):
        def one(n, _):
            at = pl.multiple_of(n * LEAF, LEAF)
            put_source(points_ref[:, pl.ds(at, LEAF)], right, norm, base + 2 * n)
            put_weights(weights_ref[pl.ds(at, LEAF), :], wcat, base + 2 * n)
            return _

        lax.fori_loop(0, LEAVES, one, 0)

    def spots_of(level):
        steps = (0, 1, 2, 3)

        def done(dz, dx):
            far = lambda d: max(d, (SIDE - d) % SIDE)
            return far(dz) + far(dx)

        return [(dz, dx) for dz in steps for dx in steps if done(dz, dx) == level]

    forward(0)
    loads[1].wait()
    loads[2].wait()
    swap(0, points, points2)
    swap(1, weights, weights2)
    targets_at(0, 0)
    for n in range(IDLE // BLOCK, BLOCKS):
        right[n] = jnp.zeros((4 * DIM, BLOCK), BF16)
        norm[n] = jnp.zeros((1, BLOCK), F32)
        wcat[n] = jnp.zeros((BLOCK, 2 * WCOL), BF16)
    column(points, weights, 0)
    forward(1)
    values[...] = jnp.zeros_like(values)
    coords[...] = jnp.zeros_like(coords)

    def skeleton(n, _):
        proj_load(n).wait()

        @pl.when(n + 1 < COLPTS // CHUNK)
        def next_load():
            proj_load(n + 1).start()

        at = pl.multiple_of(n * CHUNK, CHUNK)
        four = pl.ds(n * (CHUNK // BLOCK), CHUNK // BLOCK)
        wh, wl = wcat[four, :, 0:WCOL].reshape(CHUNK, WCOL), wcat[four, :, WCOL : 2 * WCOL].reshape(CHUNK, WCOL)
        ph, plow = split2(proj[n % 2])
        values[...] += mm(ph, wh) + mm(ph, wl) + mm(plow, wh)
        rows = lax.broadcasted_iota(jnp.int32, (CHUNK, SKEL), 0) + at
        pick = jnp.where(rows == index[...], 1.0, 0.0).astype(BF16)
        block = points[:, pl.ds(at, CHUNK)]
        first = block.astype(BF16)
        second, third = split2(block - first.astype(F32))
        coords[...] += mm(first, pick) + mm(second, pick) + mm(third, pick)
        return _

    lax.fori_loop(0, COLPTS // CHUNK, skeleton, 0)
    swap(2, coords, coords2)
    swap(3, values, values2)
    forward(2)
    put_source(coords[...], right, norm, 2 * COLPTS // BLOCK)
    put_weights(values[...], wcat, 2 * COLPTS // BLOCK)
    swaps[0].wait_recv()
    swaps[1].wait_recv()
    column(points2, weights2, COLPTS // BLOCK)
    forward(3)
    swaps[2].wait_recv()
    swaps[3].wait_recv()
    put_source(coords2[...], right, norm, (2 * COLPTS + SKEL) // BLOCK)
    put_weights(values2[...], wcat, (2 * COLPTS + SKEL) // BLOCK)
    handed.append(pltpu.make_async_copy(wcat, wcat_hbm, load_sem.at[5]))
    handed[-1].start()
    for level in (2, 3):
        for dz, dx in spots_of(level):
            targets_at(dz, dx)
    for level in (4, 5, 6):
        forward(level)
        for dz, dx in spots_of(level):
            targets_at(dz, dx)
    for c in started + swaps:
        c.wait_send()
    for c in handed:
        c.wait()


def gather(points, weights, proj, index, table):
    hbm = pl.BlockSpec(memory_space=pltpu.HBM)
    vmem = pl.BlockSpec(memory_space=VMEM)
    return pl.pallas_call(
        gather_kernel,
        out_shape=(
            pltpu.HBM((TARGETS * LEAF, 256), BF16),
            pltpu.VMEM((BLOCKS, 4 * DIM, BLOCK), BF16),
            pltpu.VMEM((BLOCKS, 1, BLOCK), F32),
            pltpu.HBM((BLOCKS, BLOCK, 2 * WCOL), BF16),
            jax.ShapeDtypeStruct((SPOTS, 8, 128), jnp.int32),
        ),
        in_specs=[hbm] * 3 + [vmem] * 2,
        out_specs=[hbm, vmem, vmem, hbm, vmem],
        scratch_shapes=[
            VMEM((TARGETS * LEAF, 256), BF16),
            VMEM((BLOCKS, BLOCK, 2 * WCOL), BF16),
            VMEM((PAYLOAD, 128), F32),
            VMEM((SPOTS, PAYLOAD, 128), F32),
            VMEM((DIM, MINE * LEAF), F32),
            VMEM((DIM, COLPTS), F32),
            VMEM((DIM, COLPTS), F32),
            VMEM((COLPTS, WCOL), F32),
            VMEM((COLPTS, WCOL), F32),
            VMEM((2, SKEL, CHUNK), F32),
            VMEM((DIM, SKEL), F32),
            VMEM((DIM, SKEL), F32),
            VMEM((SKEL, WCOL), F32),
            VMEM((SKEL, WCOL), F32),
            pltpu.SemaphoreType.DMA((4, 15)),
            pltpu.SemaphoreType.DMA((4, 16)),
            pltpu.SemaphoreType.DMA((4,)),
            pltpu.SemaphoreType.DMA((4,)),
            pltpu.SemaphoreType.DMA((6,)),
            pltpu.SemaphoreType.DMA((MINE, SPOTS)),
        ],
        compiler_params=pltpu.CompilerParams(
            collective_id=0, has_side_effects=True, vmem_limit_bytes=K1_VMEM
        ),
    )(points, weights, proj, index, table)


def produce(left, right, norm, at, block, width, high_ref, low_ref):
    blocks = range(width // BLOCK)
    columns = jnp.concatenate([right[block + n] for n in blocks], axis=1)
    norms = jnp.concatenate([norm[block + n] for n in blocks], axis=1)
    power = mm(left[pl.ds(at, LEAF), :], columns) + norms
    high_ref[:, :width], low_ref[:, :width] = split2(jnp.exp2(power))


def consume(wcat, out, at, block, width, high_ref, low_ref):
    rows = jnp.concatenate([wcat[block + n] for n in range(width // BLOCK)], axis=0)
    total = mm(high_ref[:, :width], rows)
    rest = mm(low_ref[:, :width], rows[:, :WCOL])
    out[pl.ds(at, LEAF), :] += total[:, :WCOL] + total[:, WCOL:] + rest


def near_start(source):
    return source * (LEAF // BLOCK)


def far_start(node):
    return 2 * COLPTS // BLOCK + node


def pair_kernel(
    spot_ref, table, left_hbm, right, norm, wcat_hbm, out, extra_hbm, slots,
    even, even_low, odd, odd_low, left, wcat, extra, near_pairs, far_pairs, near_extra, far_extra, sem,
):
    first = pl.ds(0, SPOTS * LEAF)
    later = pl.ds(SPOTS * LEAF, LATER * LEAF)
    loads = [
        pltpu.make_async_copy(wcat_hbm, wcat, sem.at[0]),
        pltpu.make_async_copy(left_hbm.at[later], left.at[later], sem.at[1]),
        pltpu.make_async_copy(left_hbm.at[first], left.at[first], sem.at[2]),
    ]
    for c in loads:
        c.start()

    def clear(ref, n):
        def zero(t, _):
            ref[pl.ds(pl.multiple_of(t * LEAF, LEAF), LEAF), :] = jnp.zeros((LEAF, WCOL), F32)
            return _

        lax.fori_loop(0, n, zero, 0)

    clear(out, SPOTS + 1)
    clear(extra, LATER + 1)
    spot = spot_ref[0]

    def used(t, slot):
        return table[t % SPOTS, t // SPOTS, slot]

    def note(t, counts):
        near, far = counts
        for slot in range(4):
            source = used(t, 4 * spot + slot)
            near_pairs[near] = t * 64 + source
            near = near + jnp.where(source >= 0, 1, 0)
        for slot in range(2):
            node = used(t, 64 + 2 * spot + slot)
            far_pairs[far] = t * 64 + node
            far = far + jnp.where(node >= 0, 1, 0)
        return near, far

    near_count, far_count = lax.fori_loop(0, SPOTS, note, (0, 0))

    def note_later(t, counts):
        near, far = counts
        slots[t, 0], slots[t, 1] = IDLE // LEAF, 2
        have = 0
        for slot in range(4):
            source = used(t + SPOTS, 4 * spot + slot)
            hit = source >= 0
            take = jnp.logical_and(hit, have < 1)
            slots[t, jnp.where(take, 0, 7)] = source
            have = have + jnp.where(take, 1, 0)
            near_extra[near] = t * 64 + source
            near = near + jnp.where(jnp.logical_and(hit, jnp.logical_not(take)), 1, 0)
        have = 0
        for slot in range(2):
            node = used(t + SPOTS, 64 + 2 * spot + slot)
            hit = node >= 0
            take = jnp.logical_and(hit, have < 1)
            slots[t, jnp.where(take, 1, 7)] = node
            have = have + jnp.where(take, 1, 0)
            far_extra[far] = t * 64 + node
            far = far + jnp.where(jnp.logical_and(hit, jnp.logical_not(take)), 1, 0)
        return near, far

    near_more, far_more = lax.fori_loop(0, LATER, note_later, (0, 0))
    for n in range(3):
        near_pairs[near_count + n] = SPOTS * 64
        far_pairs[far_count + n] = SPOTS * 64
        near_extra[near_more + n] = LATER * 64
        far_extra[far_more + n] = LATER * 64

    def run(pair_list, count, start_of, width, ref, n_targets, base):
        def make(n, high_ref, low_ref):
            code = pair_list[n]
            t = code // 64
            at = pl.multiple_of((base + jnp.where(t < n_targets, t, 0)) * LEAF, LEAF)
            produce(left, right, norm, at, start_of(code % 64), width, high_ref, low_ref)

        def use(n, high_ref, low_ref):
            code = pair_list[n]
            at = pl.multiple_of((code // 64) * LEAF, LEAF)
            consume(wcat, ref, at, start_of(code % 64), width, high_ref, low_ref)

        make(0, even, even_low)

        def two(m, _):
            make(2 * m + 1, odd, odd_low)
            use(2 * m, even, even_low)
            make(2 * m + 2, even, even_low)
            use(2 * m + 1, odd, odd_low)
            return _

        lax.fori_loop(0, (count + 1) // 2, two, 0)

    loads[0].wait()
    loads[1].wait()
    run(near_extra, near_more, near_start, LEAF, extra, LATER, SPOTS)
    run(far_extra, far_more, far_start, SKEL, extra, LATER, SPOTS)
    handed = pltpu.make_async_copy(extra.at[pl.ds(0, LATER * LEAF)], extra_hbm, sem.at[3])
    handed.start()
    loads[2].wait()
    run(near_pairs, near_count, near_start, LEAF, out, SPOTS, 0)
    run(far_pairs, far_count, far_start, SKEL, out, SPOTS, 0)
    handed.wait()


def pairs(spot, table, left, right, norm, wcat):
    smem = pl.BlockSpec(memory_space=pltpu.SMEM)
    vmem = pl.BlockSpec(memory_space=VMEM)
    hbm = pl.BlockSpec(memory_space=pltpu.HBM)
    return pl.pallas_call(
        pair_kernel,
        out_shape=(
            pltpu.VMEM(((SPOTS + 1) * LEAF, WCOL), F32),
            pltpu.HBM((LATER * LEAF, WCOL), F32),
            jax.ShapeDtypeStruct((LATER, 8), jnp.int32),
        ),
        in_specs=[smem, smem, hbm, vmem, vmem, hbm],
        out_specs=(vmem, hbm, smem),
        scratch_shapes=[VMEM((LEAF, LEAF), BF16)] * 4
        + [
            VMEM((TARGETS * LEAF, 256), BF16),
            VMEM((BLOCKS, BLOCK, 2 * WCOL), BF16),
            VMEM(((LATER + 1) * LEAF, WCOL), F32),
            pltpu.SMEM((SPOTS * 4 + 3,), jnp.int32),
            pltpu.SMEM((SPOTS * 2 + 3,), jnp.int32),
            pltpu.SMEM((LATER * 4 + 3,), jnp.int32),
            pltpu.SMEM((LATER * 2 + 3,), jnp.int32),
            pltpu.SemaphoreType.DMA((4,)),
        ],
        compiler_params=pltpu.CompilerParams(vmem_limit_bytes=K2_VMEM),
    )(spot, table, left, right, norm, wcat)


QUARTER = LEAF // 4


def scatter_kernel(
    chosen, partial, extra_hbm, left_hbm, right, norm, wcat_hbm, out,
    slots, turn, sums, left, wcat, even, even_low, odd, odd_low,
    send, recv, turn_send, turn_recv, y_send, y_recv, load_sem,
):
    y, z, x, core = place()
    loads = [
        pltpu.make_async_copy(left_hbm.at[pl.ds(SPOTS * LEAF, LATER * LEAF)], left, load_sem.at[0]),
        pltpu.make_async_copy(wcat_hbm, wcat, load_sem.at[1]),
        pltpu.make_async_copy(extra_hbm, sums, load_sem.at[2]),
    ]
    for c in loads:
        c.start()
    near = [(1, 0), (SIDE - 1, 0), (0, 1), (0, SIDE - 1)]
    peers = [device(y, (z + a) % SIDE, (x + b) % SIDE, core) for a, b in near]
    above, below = device((y + 1) % SIDE, z, x, core), device((y + SIDE - 1) % SIDE, z, x, core)
    greet(peers + [above, below])
    started = []

    def own(k, leaf, first, second):
        az, ax = moved(k, z, x, first, second)
        place_of = az * SIDE + ax + (0 if leaf == 0 else (leaf - 1) * SPOTS)
        rows = pl.ds(pl.multiple_of(place_of * LEAF + k * QUARTER, QUARTER), QUARTER)
        return partial.at[rows] if leaf == 0 else sums.at[rows]

    def begin(make):
        make().start()
        started.append(make)

    def step_first(k, leaf, step, j, source):
        n = (leaf * 3 + step) * SIDE + j

        def make():
            tz, tx = moved(k, z, x, 1, 0)
            return pltpu.make_async_remote_copy(
                src_ref=source(), dst_ref=slots.at[k, n], send_sem=send.at[k, n], recv_sem=recv.at[k, n],
                device_id=device(y, tz, tx, core), device_id_type=MESH,
            )

        begin(make)

    def arrived_first(k, leaf, step, j):
        n = (leaf * 3 + step) * SIDE + j
        pltpu.make_async_copy(slots.at[k, n], slots.at[k, n], recv.at[k, n]).wait()
        slots[k, n] += own(k, leaf, 2 - step, 3 - j)[...]
        return n

    def step_second(k, leaf, step, source):
        n = leaf * 3 + step

        def make():
            tz, tx = moved(k, z, x, 0, 1)
            return pltpu.make_async_remote_copy(
                src_ref=source(), dst_ref=turn.at[k, n], send_sem=turn_send.at[k, n], recv_sem=turn_recv.at[k, n],
                device_id=device(y, tz, tx, core), device_id_type=MESH,
            )

        begin(make)

    def rows_of(plane, leaf, k):
        return pl.ds(pl.multiple_of((plane * MINE + leaf) * LEAF + k * QUARTER, QUARTER), QUARTER)

    def to_y(leaf, k, number, plane, up):
        n = (leaf * 4 + k) * 3 + number

        def make():
            rows = rows_of(plane, leaf, k)
            return pltpu.make_async_remote_copy(
                src_ref=out.at[rows], dst_ref=out.at[rows], send_sem=y_send.at[n], recv_sem=y_recv.at[n],
                device_id=above if up else below, device_id_type=MESH,
            )

        begin(make)

    def y_wait(leaf, k, number, plane):
        rows = rows_of(plane, leaf, k)
        n = (leaf * 4 + k) * 3 + number
        pltpu.make_async_copy(out.at[rows], out.at[rows], y_recv.at[n]).wait()

    def second_axis(k, leaf, j):
        n = arrived_first(k, leaf, 2, j)
        if j > 0:
            m = leaf * 3 + j - 1
            pltpu.make_async_copy(turn.at[k, m], turn.at[k, m], turn_recv.at[k, m]).wait()
        if j == 0:
            step_second(k, leaf, 0, lambda: slots.at[k, n])
        elif j < 3:
            turn[k, m] += slots[k, n]
            step_second(k, leaf, j, lambda: turn.at[k, m])
        else:
            out[rows_of(y, leaf, k), :] = turn[k, m] + slots[k, n]
            to_y(leaf, k, 0, y, True)
            to_y(leaf, k, 1, y, False)

    def second_hop(leaf, k):
        lower, upper = (y + SIDE - 1) % SIDE, (y + 1) % SIDE
        if k % 2 == 0:
            y_wait(leaf, k, 0, lower)
            to_y(leaf, k, 2, lower, True)
        else:
            y_wait(leaf, k, 1, upper)
            to_y(leaf, k, 2, upper, False)

    def last_arrivals(leaf, k):
        lower, upper, across = (y + SIDE - 1) % SIDE, (y + 1) % SIDE, (y + 2) % SIDE
        if k % 2 == 0:
            y_wait(leaf, k, 1, upper)
        else:
            y_wait(leaf, k, 0, lower)
        y_wait(leaf, k, 2, across)

    def start_leaf(leaf):
        for j in range(SIDE):
            for k in range(4):
                step_first(k, leaf, 0, j, functools.partial(own, k, leaf, 3, 3 - j))

    def part(leaf, n):
        j = n % SIDE
        for k in range(4):
            if leaf < MINE:
                m = arrived_first(k, leaf, n // SIDE, j)
                step_first(k, leaf, 1 + n // SIDE, j, lambda k=k, m=m: slots.at[k, m])
            if leaf > 0 and n < SIDE:
                second_axis(k, leaf - 1, j)

    def make(t, slot, width, start_of, high_ref, low_ref):
        at = pl.multiple_of(t * LEAF, LEAF)
        produce(left, right, norm, at, start_of(chosen[t, slot]), width, high_ref, low_ref)

    def use(t, slot, width, start_of, high_ref, low_ref):
        at = pl.multiple_of(t * LEAF, LEAF)
        consume(wcat, sums, at, start_of(chosen[t, slot]), width, high_ref, low_ref)

    def one_target(t):
        make(t, 1, SKEL, far_start, odd, odd_low)
        use(t, 0, LEAF, near_start, even, even_low)
        make((t + 1) % LATER, 0, LEAF, near_start, even, even_low)
        use(t, 1, SKEL, far_start, odd, odd_low)

    for leaf in range(MINE + 1):
        if leaf < MINE:
            start_leaf(leaf)
        if leaf == 0:
            for c in loads:
                c.wait()
            make(0, 0, LEAF, near_start, even, even_low)
        if leaf < MINE - 1:

            def step(n, _, leaf=leaf):
                def inner(m, carry):
                    one_target(leaf * SPOTS + 2 * n + m)
                    return carry

                lax.fori_loop(0, 2, inner, 0)
                for which in range(2 * SIDE):
                    pl.when(n == which)(functools.partial(part, leaf, which))
                return _

            lax.fori_loop(0, 2 * SIDE, step, 0)
        else:
            for n in range(2 * SIDE):
                part(leaf, n)
        if leaf > 0:
            for k in range(4):
                second_hop(leaf - 1, k)
    for leaf in range(MINE):
        for k in range(4):
            last_arrivals(leaf, k)
    for again in started:
        again().wait_send()


def scatter(chosen, partial, extra, left, right, norm, wcat):
    smem = pl.BlockSpec(memory_space=pltpu.SMEM)
    vmem = pl.BlockSpec(memory_space=VMEM)
    hbm = pl.BlockSpec(memory_space=pltpu.HBM)
    return pl.pallas_call(
        scatter_kernel,
        out_shape=jax.ShapeDtypeStruct((COLPTS, WCOL), F32),
        in_specs=[smem, vmem, hbm, hbm, vmem, vmem, hbm],
        out_specs=vmem,
        scratch_shapes=[
            VMEM((4, MINE * 3 * SIDE, QUARTER, WCOL), F32),
            VMEM((4, MINE * 3, QUARTER, WCOL), F32),
            VMEM((LATER * LEAF, WCOL), F32),
            VMEM((LATER * LEAF, 256), BF16),
            VMEM((BLOCKS, BLOCK, 2 * WCOL), BF16),
        ]
        + [VMEM((LEAF, LEAF), BF16)] * 2
        + [VMEM((LEAF, SKEL), BF16)] * 2
        + [
            pltpu.SemaphoreType.DMA((4, MINE * 3 * SIDE)),
            pltpu.SemaphoreType.DMA((4, MINE * 3 * SIDE)),
            pltpu.SemaphoreType.DMA((4, MINE * 3)),
            pltpu.SemaphoreType.DMA((4, MINE * 3)),
            pltpu.SemaphoreType.DMA((MINE * 4 * 3,)),
            pltpu.SemaphoreType.DMA((MINE * 4 * 3,)),
            pltpu.SemaphoreType.DMA((3,)),
        ],
        compiler_params=pltpu.CompilerParams(
            collective_id=1, has_side_effects=True, vmem_limit_bytes=K3_VMEM
        ),
    )(chosen, partial, extra, left, right, norm, wcat)


def lists(y, core, fetch_table, near_list, far_list):
    near = lax.dynamic_slice_in_dim(near_list, y * MINE, MINE, 0)
    far = lax.dynamic_slice_in_dim(far_list, y * MINE, MINE, 0)
    slots = jnp.arange(64, dtype=jnp.int32)
    nodes = jnp.arange(32, dtype=jnp.int32)
    near_used = jnp.any(near[:, :, None] == slots, axis=1)
    far_used = jnp.any(far[:, :, None] == nodes, axis=1)
    rows = (y * MINE + jnp.arange(MINE, dtype=jnp.int32)) // 4
    requests = fetch_table[:, 0].reshape(3, 64)
    local = jnp.sum(jnp.where(rows[:, None, None] == jnp.arange(3)[None, :, None], requests[None], 0), axis=1)
    side = (slots // 2 + core) % 2
    near_value = jnp.where(near_used, side * LEAVES + local, -1)
    far_value = jnp.where(far_used, (nodes + core) % 2, -1)
    table = jnp.concatenate([near_value, far_value, jnp.full((MINE, 32), -1, jnp.int32)], axis=1)
    return jnp.pad(table, ((0, 8 - MINE), (0, 0))).astype(F32)


def on_device(points, weights, proj, fetch_table, near_list, far_list, skel_idx):
    y, z, x, core = place()
    table = lists(y, core, fetch_table, near_list, far_list)
    fixed = pltpu.with_memory_space_constraint
    points, weights, proj = (fixed(a, pltpu.HBM) for a in (points, weights, proj))
    left, right, norm, wcat, found = gather(points, weights, proj, skel_idx, table)
    spot = (z * SIDE + x).reshape(1).astype(jnp.int32)
    left, wcat = fixed(left, pltpu.HBM), fixed(wcat, pltpu.HBM)
    right, norm = fixed(right, VMEM), fixed(norm, VMEM)
    partial, extra, chosen = pairs(spot, found, left, right, norm, wcat)
    return scatter(chosen, fixed(partial, VMEM), fixed(extra, pltpu.HBM), left, right, norm, wcat)


def solution(mesh):
    placed = (
        P(None, "dev"),
        P("dev", None),
        P(None, "dev"),
        P(None, "dev", None, None),
        P("dev", None),
        P("dev", None),
        P("dev", None),
    )
    return jax.shard_map(
        on_device, mesh=mesh, in_specs=placed, out_specs=P("dev", None), check_vma=False
    )
```

```python
import functools
import math

import jax
import jax.numpy as jnp
from jax import lax
from jax.experimental import pallas as pl
from jax.experimental.pallas import tpu as pltpu
from jax.sharding import PartitionSpec as P

F32, BF16 = jnp.float32, jnp.bfloat16
MESH = pl.DeviceIdType.MESH
VMEM = pltpu.VMEM
LOG2E = math.log2(math.e)
SIDE = 4
SPOTS = SIDE * SIDE
LEAF, DIM, WCOL, SKEL = 512, 64, 128, 256
LEAVES = 12
MINE = 3
COLPTS = LEAVES * LEAF
HALF = LEAF // 2
PAYLOAD = MINE * HALF + 8
TARGETS = SPOTS * MINE
IDLE = 2 * COLPTS + 2 * SKEL
SOURCES = IDLE + LEAF
BLOCK = 256
BLOCKS = SOURCES // BLOCK
LATER = (MINE - 1) * SPOTS
CHUNK = 1024
SCALE = LOG2E / 32.0
K1_VMEM, K2_VMEM, K3_VMEM = 44 << 20, 32 << 20, 38 << 20
CUTS = (0, 192, 384, 576, PAYLOAD)


def mm(a, b):
    return jnp.dot(a, b, preferred_element_type=F32)


def split2(v):
    high = v.astype(BF16)
    return high, (v - high.astype(F32)).astype(BF16)


def place():
    y, dev = lax.axis_index("grp"), lax.axis_index("dev")
    return y, lax.div(dev, 8), lax.rem(lax.div(dev, 2), SIDE), lax.rem(dev, 2)


def shift(k, first, second):
    sign = 1 if k % 2 == 0 else -1
    along_x, along_z = (first, second) if k < 2 else (second, first)
    return sign * along_z % SIDE, sign * along_x % SIDE


class Around:
    def __init__(self):
        self.y, self.z, self.x, self.core = place()
        zs = [lax.rem(self.z + a, SIDE) for a in range(SIDE)]
        xs = [lax.rem(self.x + a, SIDE) for a in range(SIDE)]
        self.spots = {(a, b): zs[a] * SIDE + xs[b] for a in range(SIDE) for b in range(SIDE)}
        self.devices = {
            (a, b): (self.y, self.spots[a, b] * 2 + self.core) for a, b in ((1, 0), (3, 0), (0, 1), (0, 3))
        }
        self.sibling = (self.y, self.spots[0, 0] * 2 + 1 - self.core)

    def spot(self, k, first, second):
        return self.spots[shift(k, first, second)]

    def next(self, k, along_first):
        return self.devices[shift(k, 1, 0) if along_first else shift(k, 0, 1)]


def greet(peers):
    barrier = pltpu.get_barrier_semaphore()
    for peer in peers:
        pl.semaphore_signal(barrier, inc=1, device_id=peer, device_id_type=MESH)
    pl.semaphore_wait(barrier, len(peers))


def put_source(block, right, norm, first):
    high, low = split2(block * (2.0 * SCALE))
    total = -SCALE * jnp.sum(block * block, axis=0, keepdims=True)
    for n in range(block.shape[1] // BLOCK):
        cols = slice(n * BLOCK, (n + 1) * BLOCK)
        right[first + n, 0:DIM, :] = high[:, cols]
        right[first + n, DIM : 2 * DIM, :] = high[:, cols]
        right[first + n, 2 * DIM : 3 * DIM, :] = low[:, cols]
        right[first + n, 3 * DIM : 4 * DIM, :] = jnp.full((DIM, BLOCK), -1.0, BF16)
        norm[first + n] = total[:, cols]


def put_weights(block, wcat, first):
    high, low = split2(block)
    for n in range(block.shape[0] // BLOCK):
        rows = slice(n * BLOCK, (n + 1) * BLOCK)
        wcat[first + n, :, 0:WCOL] = high[rows]
        wcat[first + n, :, WCOL : 2 * WCOL] = low[rows]


def put_target(both, left, at):
    lane = lax.broadcasted_iota(jnp.int32, both.shape, 1)
    first_half = lane < DIM
    first_quarter = lane % DIM < DIM // 2
    high = both.astype(BF16).astype(F32)
    low = both - high
    high_r, low_r = pltpu.roll(high, DIM, 1), pltpu.roll(low, DIM, 1)
    square = both * both * SCALE
    down = square + pltpu.roll(square, 32, 1)
    up = square + pltpu.roll(square, 96, 1)
    up_high = up.astype(BF16).astype(F32)
    down_low = down - down.astype(BF16).astype(F32)
    sums = jnp.where(first_quarter, up_high, down_low)
    left[pl.ds(at, HALF), 0:128] = jnp.where(first_half, high, low_r).astype(BF16)
    left[pl.ds(at, HALF), 128:256] = jnp.where(first_half, high, pltpu.roll(sums, DIM, 1)).astype(BF16)
    left[pl.ds(at + HALF, HALF), 0:128] = jnp.where(first_half, high_r, low).astype(BF16)
    left[pl.ds(at + HALF, HALF), 128:256] = jnp.where(first_half, high_r, sums).astype(BF16)


def gather_kernel(
    points_hbm, weights_hbm, proj_hbm, index, table,
    left_hbm, right, norm, wcat_hbm, found,
    left, wcat, payload, gathered, own, points, points2, weights, weights2, proj, coords, coords2, values, values2,
    send, recv, pair_send, pair_recv, load_sem, left_sem,
):
    around = Around()
    y = around.y
    loads = [
        pltpu.make_async_copy(
            points_hbm.at[:, pl.ds(pl.multiple_of(y * (MINE * LEAF), LEAF), MINE * LEAF)], own, load_sem.at[0]
        ),
        pltpu.make_async_copy(points_hbm, points, load_sem.at[1]),
        pltpu.make_async_copy(weights_hbm, weights, load_sem.at[2]),
    ]

    def proj_load(n):
        at = pl.multiple_of(n * CHUNK, CHUNK)
        return pltpu.make_async_copy(proj_hbm.at[:, pl.ds(at, CHUNK)], proj.at[n % 2], load_sem.at[3 + n % 2])

    for c in loads:
        c.start()
    proj_load(0).start()
    greet(list(around.devices.values()) + [around.sibling])

    loads[0].wait()
    for leaf in range(MINE):
        block = own[:, leaf * LEAF : (leaf + 1) * LEAF]
        packed = jnp.concatenate([block[:, :HALF], block[:, HALF:]], axis=0)
        payload[leaf * HALF : (leaf + 1) * HALF, :] = packed.T
    payload[MINE * HALF :, :] = table[...]

    started, swaps, handed = [], [], []

    def spot_of(k, i, j):
        return around.spot(k, -i, -j)

    def copy(k, i, j, first):
        rows = pl.ds(CUTS[k], CUTS[k + 1] - CUTS[k])
        arrival = (i + 1) * SIDE + j if first else i * SIDE + j + 1
        number = i if first else SIDE - 1 + i * (SIDE - 1) + j
        target = gathered.at[spot_of(k, i, j), rows]
        c = pltpu.make_async_remote_copy(
            src_ref=payload.at[rows] if i == 0 and j == 0 else target,
            dst_ref=target,
            send_sem=send.at[k, number],
            recv_sem=recv.at[k, arrival],
            device_id=around.next(k, first),
            device_id_type=MESH,
        )
        c.start()
        started.append(c)

    def forward(level):
        for i in range(SIDE):
            j = level - i
            if not 0 <= j < SIDE:
                continue
            for k in range(4):
                if level > 0:
                    rows = pl.ds(CUTS[k], CUTS[k + 1] - CUTS[k])
                    here = gathered.at[spot_of(k, i, j), rows]
                    pltpu.make_async_copy(here, here, recv.at[k, i * SIDE + j]).wait()
                if j == 0 and i < SIDE - 1:
                    copy(k, i, j, True)
                if j < SIDE - 1:
                    copy(k, i, j, False)

    def swap(n, a, b):
        c = pltpu.make_async_remote_copy(
            src_ref=a, dst_ref=b, send_sem=pair_send.at[n], recv_sem=pair_recv.at[n],
            device_id=around.sibling, device_id_type=MESH,
        )
        c.start()
        swaps.append(c)

    def targets_at(dz, dx):
        spot = around.spots[dz, dx]

        def leaf_rows(leaf, _):
            rows = pl.ds(pl.multiple_of(leaf * HALF, HALF), HALF)
            both = payload[rows, :] if dz == dx == 0 else gathered[spot, rows, :]
            put_target(both, left, pl.multiple_of((leaf * SPOTS + spot) * LEAF, LEAF))
            return _

        lax.fori_loop(0, MINE, leaf_rows, 0)
        lists_here = payload[MINE * HALF :, :] if dz == dx == 0 else gathered[spot, MINE * HALF :, :]
        found[spot] = lists_here.astype(jnp.int32)
        for leaf in range(MINE):
            rows = pl.ds(pl.multiple_of((leaf * SPOTS + spot) * LEAF, LEAF), LEAF)
            c = pltpu.make_async_copy(left.at[rows], left_hbm.at[rows], left_sem.at[leaf, dz * SIDE + dx])
            c.start()
            handed.append(c)

    def column(points_ref, weights_ref, base):
        def one(n, _):
            at = pl.multiple_of(n * LEAF, LEAF)
            put_source(points_ref[:, pl.ds(at, LEAF)], right, norm, base + 2 * n)
            put_weights(weights_ref[pl.ds(at, LEAF), :], wcat, base + 2 * n)
            return _

        lax.fori_loop(0, LEAVES, one, 0)

    def spots_of(level):
        steps = (0, 1, 2, 3)

        def done(dz, dx):
            far = lambda d: max(d, (SIDE - d) % SIDE)
            return far(dz) + far(dx)

        return [(dz, dx) for dz in steps for dx in steps if done(dz, dx) == level]

    forward(0)
    loads[1].wait()
    loads[2].wait()
    swap(0, points, points2)
    swap(1, weights, weights2)
    targets_at(0, 0)
    for n in range(IDLE // BLOCK, BLOCKS):
        right[n] = jnp.zeros((4 * DIM, BLOCK), BF16)
        norm[n] = jnp.zeros((1, BLOCK), F32)
        wcat[n] = jnp.zeros((BLOCK, 2 * WCOL), BF16)
    column(points, weights, 0)
    forward(1)
    values[...] = jnp.zeros_like(values)
    coords[...] = jnp.zeros_like(coords)

    def skeleton(n, _):
        proj_load(n).wait()

        @pl.when(n + 1 < COLPTS // CHUNK)
        def next_load():
            proj_load(n + 1).start()

        at = pl.multiple_of(n * CHUNK, CHUNK)
        four = pl.ds(n * (CHUNK // BLOCK), CHUNK // BLOCK)
        wh, wl = wcat[four, :, 0:WCOL].reshape(CHUNK, WCOL), wcat[four, :, WCOL : 2 * WCOL].reshape(CHUNK, WCOL)
        ph, plow = split2(proj[n % 2])
        values[...] += mm(ph, wh) + mm(ph, wl) + mm(plow, wh)
        rows = lax.broadcasted_iota(jnp.int32, (CHUNK, SKEL), 0) + at
        pick = jnp.where(rows == index[...], 1.0, 0.0).astype(BF16)
        block = points[:, pl.ds(at, CHUNK)]
        first = block.astype(BF16)
        second, third = split2(block - first.astype(F32))
        coords[...] += mm(first, pick) + mm(second, pick) + mm(third, pick)
        return _

    lax.fori_loop(0, COLPTS // CHUNK, skeleton, 0)
    swap(2, coords, coords2)
    swap(3, values, values2)
    forward(2)
    put_source(coords[...], right, norm, 2 * COLPTS // BLOCK)
    put_weights(values[...], wcat, 2 * COLPTS // BLOCK)
    swaps[0].wait_recv()
    swaps[1].wait_recv()
    column(points2, weights2, COLPTS // BLOCK)
    forward(3)
    swaps[2].wait_recv()
    swaps[3].wait_recv()
    put_source(coords2[...], right, norm, (2 * COLPTS + SKEL) // BLOCK)
    put_weights(values2[...], wcat, (2 * COLPTS + SKEL) // BLOCK)
    handed.append(pltpu.make_async_copy(wcat, wcat_hbm, load_sem.at[5]))
    handed[-1].start()
    for level in (2, 3):
        for dz, dx in spots_of(level):
            targets_at(dz, dx)
    for level in (4, 5, 6):
        forward(level)
        for dz, dx in spots_of(level):
            targets_at(dz, dx)
    for c in started + swaps:
        c.wait_send()
    for c in handed:
        c.wait()


def gather(points, weights, proj, index, table):
    hbm = pl.BlockSpec(memory_space=pltpu.HBM)
    vmem = pl.BlockSpec(memory_space=VMEM)
    return pl.pallas_call(
        gather_kernel,
        out_shape=(
            pltpu.HBM((TARGETS * LEAF, 256), BF16),
            pltpu.VMEM((BLOCKS, 4 * DIM, BLOCK), BF16),
            pltpu.VMEM((BLOCKS, 1, BLOCK), F32),
            pltpu.HBM((BLOCKS, BLOCK, 2 * WCOL), BF16),
            jax.ShapeDtypeStruct((SPOTS, 8, 128), jnp.int32),
        ),
        in_specs=[hbm] * 3 + [vmem] * 2,
        out_specs=[hbm, vmem, vmem, hbm, vmem],
        scratch_shapes=[
            VMEM((TARGETS * LEAF, 256), BF16),
            VMEM((BLOCKS, BLOCK, 2 * WCOL), BF16),
            VMEM((PAYLOAD, 128), F32),
            VMEM((SPOTS, PAYLOAD, 128), F32),
            VMEM((DIM, MINE * LEAF), F32),
            VMEM((DIM, COLPTS), F32),
            VMEM((DIM, COLPTS), F32),
            VMEM((COLPTS, WCOL), F32),
            VMEM((COLPTS, WCOL), F32),
            VMEM((2, SKEL, CHUNK), F32),
            VMEM((DIM, SKEL), F32),
            VMEM((DIM, SKEL), F32),
            VMEM((SKEL, WCOL), F32),
            VMEM((SKEL, WCOL), F32),
            pltpu.SemaphoreType.DMA((4, 15)),
            pltpu.SemaphoreType.DMA((4, 16)),
            pltpu.SemaphoreType.DMA((4,)),
            pltpu.SemaphoreType.DMA((4,)),
            pltpu.SemaphoreType.DMA((6,)),
            pltpu.SemaphoreType.DMA((MINE, SPOTS)),
        ],
        compiler_params=pltpu.CompilerParams(
            collective_id=0, has_side_effects=True, vmem_limit_bytes=K1_VMEM
        ),
    )(points, weights, proj, index, table)


def produce(left, right, norm, at, block, width, high_ref, low_ref):
    blocks = range(width // BLOCK)
    columns = jnp.concatenate([right[block + n] for n in blocks], axis=1)
    norms = jnp.concatenate([norm[block + n] for n in blocks], axis=1)
    power = mm(left[pl.ds(at, LEAF), :], columns) + norms
    high_ref[:, :width], low_ref[:, :width] = split2(jnp.exp2(power))


def consume(wcat, out, at, block, width, high_ref, low_ref):
    rows = jnp.concatenate([wcat[block + n] for n in range(width // BLOCK)], axis=0)
    total = mm(high_ref[:, :width], rows)
    rest = mm(low_ref[:, :width], rows[:, :WCOL])
    out[pl.ds(at, LEAF), :] += total[:, :WCOL] + total[:, WCOL:] + rest


def near_start(source):
    return source * (LEAF // BLOCK)


def far_start(node):
    return 2 * COLPTS // BLOCK + node


def pair_kernel(
    spot_ref, table, left_hbm, right, norm, wcat_hbm, out, extra_hbm, slots,
    even, even_low, odd, odd_low, left, wcat, extra, near_pairs, far_pairs, near_extra, far_extra, sem,
):
    first = pl.ds(0, SPOTS * LEAF)
    later = pl.ds(SPOTS * LEAF, LATER * LEAF)
    loads = [
        pltpu.make_async_copy(wcat_hbm, wcat, sem.at[0]),
        pltpu.make_async_copy(left_hbm.at[later], left.at[later], sem.at[1]),
        pltpu.make_async_copy(left_hbm.at[first], left.at[first], sem.at[2]),
    ]
    for c in loads:
        c.start()

    def clear(ref, n):
        def zero(t, _):
            ref[pl.ds(pl.multiple_of(t * LEAF, LEAF), LEAF), :] = jnp.zeros((LEAF, WCOL), F32)
            return _

        lax.fori_loop(0, n, zero, 0)

    clear(out, SPOTS + 1)
    clear(extra, LATER + 1)
    spot = spot_ref[0]

    def used(t, slot):
        return table[t % SPOTS, t // SPOTS, slot]

    def note(t, counts):
        near, far = counts
        for slot in range(4):
            source = used(t, 4 * spot + slot)
            near_pairs[near] = t * 64 + source
            near = near + jnp.where(source >= 0, 1, 0)
        for slot in range(2):
            node = used(t, 64 + 2 * spot + slot)
            far_pairs[far] = t * 64 + node
            far = far + jnp.where(node >= 0, 1, 0)
        return near, far

    near_count, far_count = lax.fori_loop(0, SPOTS, note, (0, 0))

    def note_later(t, counts):
        near, far = counts
        slots[t, 0], slots[t, 1] = IDLE // LEAF, 2
        have = 0
        for slot in range(4):
            source = used(t + SPOTS, 4 * spot + slot)
            hit = source >= 0
            take = jnp.logical_and(hit, have < 1)
            slots[t, jnp.where(take, 0, 7)] = source
            have = have + jnp.where(take, 1, 0)
            near_extra[near] = t * 64 + source
            near = near + jnp.where(jnp.logical_and(hit, jnp.logical_not(take)), 1, 0)
        have = 0
        for slot in range(2):
            node = used(t + SPOTS, 64 + 2 * spot + slot)
            hit = node >= 0
            take = jnp.logical_and(hit, have < 1)
            slots[t, jnp.where(take, 1, 7)] = node
            have = have + jnp.where(take, 1, 0)
            far_extra[far] = t * 64 + node
            far = far + jnp.where(jnp.logical_and(hit, jnp.logical_not(take)), 1, 0)
        return near, far

    near_more, far_more = lax.fori_loop(0, LATER, note_later, (0, 0))
    for n in range(3):
        near_pairs[near_count + n] = SPOTS * 64
        far_pairs[far_count + n] = SPOTS * 64
        near_extra[near_more + n] = LATER * 64
        far_extra[far_more + n] = LATER * 64

    def run(pair_list, count, start_of, width, ref, n_targets, base):
        def make(n, high_ref, low_ref):
            code = pair_list[n]
            t = code // 64
            at = pl.multiple_of((base + jnp.where(t < n_targets, t, 0)) * LEAF, LEAF)
            produce(left, right, norm, at, start_of(code % 64), width, high_ref, low_ref)

        def use(n, high_ref, low_ref):
            code = pair_list[n]
            at = pl.multiple_of((code // 64) * LEAF, LEAF)
            consume(wcat, ref, at, start_of(code % 64), width, high_ref, low_ref)

        make(0, even, even_low)

        def two(m, _):
            make(2 * m + 1, odd, odd_low)
            use(2 * m, even, even_low)
            make(2 * m + 2, even, even_low)
            use(2 * m + 1, odd, odd_low)
            return _

        lax.fori_loop(0, (count + 1) // 2, two, 0)

    loads[0].wait()
    loads[1].wait()
    run(near_extra, near_more, near_start, LEAF, extra, LATER, SPOTS)
    run(far_extra, far_more, far_start, SKEL, extra, LATER, SPOTS)
    handed = pltpu.make_async_copy(extra.at[pl.ds(0, LATER * LEAF)], extra_hbm, sem.at[3])
    handed.start()
    loads[2].wait()
    run(near_pairs, near_count, near_start, LEAF, out, SPOTS, 0)
    run(far_pairs, far_count, far_start, SKEL, out, SPOTS, 0)
    handed.wait()


def pairs(spot, table, left, right, norm, wcat):
    smem = pl.BlockSpec(memory_space=pltpu.SMEM)
    vmem = pl.BlockSpec(memory_space=VMEM)
    hbm = pl.BlockSpec(memory_space=pltpu.HBM)
    return pl.pallas_call(
        pair_kernel,
        out_shape=(
            pltpu.VMEM(((SPOTS + 1) * LEAF, WCOL), F32),
            pltpu.HBM((LATER * LEAF, WCOL), F32),
            jax.ShapeDtypeStruct((LATER, 8), jnp.int32),
        ),
        in_specs=[smem, smem, hbm, vmem, vmem, hbm],
        out_specs=(vmem, hbm, smem),
        scratch_shapes=[VMEM((LEAF, LEAF), BF16)] * 4
        + [
            VMEM((TARGETS * LEAF, 256), BF16),
            VMEM((BLOCKS, BLOCK, 2 * WCOL), BF16),
            VMEM(((LATER + 1) * LEAF, WCOL), F32),
            pltpu.SMEM((SPOTS * 4 + 3,), jnp.int32),
            pltpu.SMEM((SPOTS * 2 + 3,), jnp.int32),
            pltpu.SMEM((LATER * 4 + 3,), jnp.int32),
            pltpu.SMEM((LATER * 2 + 3,), jnp.int32),
            pltpu.SemaphoreType.DMA((4,)),
        ],
        compiler_params=pltpu.CompilerParams(vmem_limit_bytes=K2_VMEM),
    )(spot, table, left, right, norm, wcat)


QUARTER = LEAF // 4


def scatter_kernel(
    chosen, partial, extra_hbm, left_hbm, right, norm, wcat_hbm, out,
    slots, turn, sums, left, wcat, even, even_low, odd, odd_low,
    send, recv, turn_send, turn_recv, y_send, y_recv, load_sem,
):
    around = Around()
    y = around.y
    loads = [
        pltpu.make_async_copy(left_hbm.at[pl.ds(SPOTS * LEAF, LATER * LEAF)], left, load_sem.at[0]),
        pltpu.make_async_copy(wcat_hbm, wcat, load_sem.at[1]),
        pltpu.make_async_copy(extra_hbm, sums, load_sem.at[2]),
    ]
    for c in loads:
        c.start()
    planes = [lax.rem(y + a, SIDE) for a in range(SIDE)]
    here = around.spots[0, 0] * 2 + around.core
    above, below = (planes[1], here), (planes[3], here)
    greet(list(around.devices.values()) + [above, below])
    started = []

    def own(k, leaf, first, second):
        place_of = around.spot(k, first, second) + (0 if leaf == 0 else (leaf - 1) * SPOTS)
        rows = pl.ds(pl.multiple_of(place_of * LEAF + k * QUARTER, QUARTER), QUARTER)
        return partial.at[rows] if leaf == 0 else sums.at[rows]

    def begin(make):
        make().start()
        started.append(make)

    def step_first(k, leaf, step, j, source):
        n = (leaf * 3 + step) * SIDE + j

        def make():
            return pltpu.make_async_remote_copy(
                src_ref=source(), dst_ref=slots.at[k, n], send_sem=send.at[k, n], recv_sem=recv.at[k, n],
                device_id=around.next(k, True), device_id_type=MESH,
            )

        begin(make)

    def arrived_first(k, leaf, step, j):
        n = (leaf * 3 + step) * SIDE + j
        pltpu.make_async_copy(slots.at[k, n], slots.at[k, n], recv.at[k, n]).wait()
        slots[k, n] += own(k, leaf, 2 - step, 3 - j)[...]
        return n

    def step_second(k, leaf, step, source):
        n = leaf * 3 + step

        def make():
            return pltpu.make_async_remote_copy(
                src_ref=source(), dst_ref=turn.at[k, n], send_sem=turn_send.at[k, n], recv_sem=turn_recv.at[k, n],
                device_id=around.next(k, False), device_id_type=MESH,
            )

        begin(make)

    def rows_of(plane, leaf, k):
        return pl.ds(pl.multiple_of((plane * MINE + leaf) * LEAF + k * QUARTER, QUARTER), QUARTER)

    def to_y(leaf, k, number, plane, up):
        n = (leaf * 4 + k) * 3 + number

        def make():
            rows = rows_of(plane, leaf, k)
            return pltpu.make_async_remote_copy(
                src_ref=out.at[rows], dst_ref=out.at[rows], send_sem=y_send.at[n], recv_sem=y_recv.at[n],
                device_id=above if up else below, device_id_type=MESH,
            )

        begin(make)

    def y_wait(leaf, k, number, plane):
        rows = rows_of(plane, leaf, k)
        n = (leaf * 4 + k) * 3 + number
        pltpu.make_async_copy(out.at[rows], out.at[rows], y_recv.at[n]).wait()

    def second_axis(k, leaf, j):
        n = arrived_first(k, leaf, 2, j)
        if j > 0:
            m = leaf * 3 + j - 1
            pltpu.make_async_copy(turn.at[k, m], turn.at[k, m], turn_recv.at[k, m]).wait()
        if j == 0:
            step_second(k, leaf, 0, lambda: slots.at[k, n])
        elif j < 3:
            turn[k, m] += slots[k, n]
            step_second(k, leaf, j, lambda: turn.at[k, m])
        else:
            out[rows_of(y, leaf, k), :] = turn[k, m] + slots[k, n]
            to_y(leaf, k, 0, y, True)
            to_y(leaf, k, 1, y, False)

    def second_hop(leaf, k):
        lower, upper = planes[3], planes[1]
        if k % 2 == 0:
            y_wait(leaf, k, 0, lower)
            to_y(leaf, k, 2, lower, True)
        else:
            y_wait(leaf, k, 1, upper)
            to_y(leaf, k, 2, upper, False)

    def last_arrivals(leaf, k):
        lower, upper, across = planes[3], planes[1], planes[2]
        if k % 2 == 0:
            y_wait(leaf, k, 1, upper)
        else:
            y_wait(leaf, k, 0, lower)
        y_wait(leaf, k, 2, across)

    def start_leaf(leaf):
        for j in range(SIDE):
            for k in range(4):
                step_first(k, leaf, 0, j, functools.partial(own, k, leaf, 3, 3 - j))

    def part(leaf, n):
        j = n % SIDE
        for k in range(4):
            if leaf < MINE:
                m = arrived_first(k, leaf, n // SIDE, j)
                step_first(k, leaf, 1 + n // SIDE, j, lambda k=k, m=m: slots.at[k, m])
            if leaf > 0 and n < SIDE:
                second_axis(k, leaf - 1, j)

    def make(t, slot, width, start_of, high_ref, low_ref):
        at = pl.multiple_of(t * LEAF, LEAF)
        produce(left, right, norm, at, start_of(chosen[t, slot]), width, high_ref, low_ref)

    def use(t, slot, width, start_of, high_ref, low_ref):
        at = pl.multiple_of(t * LEAF, LEAF)
        consume(wcat, sums, at, start_of(chosen[t, slot]), width, high_ref, low_ref)

    def one_target(t):
        make(t, 1, SKEL, far_start, odd, odd_low)
        use(t, 0, LEAF, near_start, even, even_low)
        make((t + 1) % LATER, 0, LEAF, near_start, even, even_low)
        use(t, 1, SKEL, far_start, odd, odd_low)

    for leaf in range(MINE + 1):
        if leaf < MINE:
            start_leaf(leaf)
        if leaf == 0:
            for c in loads:
                c.wait()
            make(0, 0, LEAF, near_start, even, even_low)
        if leaf < MINE - 1:

            def step(n, _, leaf=leaf):
                def inner(m, carry):
                    one_target(leaf * SPOTS + 2 * n + m)
                    return carry

                lax.fori_loop(0, 2, inner, 0)
                for which in range(2 * SIDE):
                    pl.when(n == which)(functools.partial(part, leaf, which))
                return _

            lax.fori_loop(0, 2 * SIDE, step, 0)
        else:
            for n in range(2 * SIDE):
                part(leaf, n)
        if leaf > 0:
            for k in range(4):
                second_hop(leaf - 1, k)
    for leaf in range(MINE):
        for k in range(4):
            last_arrivals(leaf, k)
    for again in started:
        again().wait_send()


def scatter(chosen, partial, extra, left, right, norm, wcat):
    smem = pl.BlockSpec(memory_space=pltpu.SMEM)
    vmem = pl.BlockSpec(memory_space=VMEM)
    hbm = pl.BlockSpec(memory_space=pltpu.HBM)
    return pl.pallas_call(
        scatter_kernel,
        out_shape=jax.ShapeDtypeStruct((COLPTS, WCOL), F32),
        in_specs=[smem, vmem, hbm, hbm, vmem, vmem, hbm],
        out_specs=vmem,
        scratch_shapes=[
            VMEM((4, MINE * 3 * SIDE, QUARTER, WCOL), F32),
            VMEM((4, MINE * 3, QUARTER, WCOL), F32),
            VMEM((LATER * LEAF, WCOL), F32),
            VMEM((LATER * LEAF, 256), BF16),
            VMEM((BLOCKS, BLOCK, 2 * WCOL), BF16),
        ]
        + [VMEM((LEAF, LEAF), BF16)] * 2
        + [VMEM((LEAF, SKEL), BF16)] * 2
        + [
            pltpu.SemaphoreType.DMA((4, MINE * 3 * SIDE)),
            pltpu.SemaphoreType.DMA((4, MINE * 3 * SIDE)),
            pltpu.SemaphoreType.DMA((4, MINE * 3)),
            pltpu.SemaphoreType.DMA((4, MINE * 3)),
            pltpu.SemaphoreType.DMA((MINE * 4 * 3,)),
            pltpu.SemaphoreType.DMA((MINE * 4 * 3,)),
            pltpu.SemaphoreType.DMA((3,)),
        ],
        compiler_params=pltpu.CompilerParams(
            collective_id=1, has_side_effects=True, vmem_limit_bytes=K3_VMEM
        ),
    )(chosen, partial, extra, left, right, norm, wcat)


def lists(y, core, fetch_table, near_list, far_list):
    near = lax.dynamic_slice_in_dim(near_list, y * MINE, MINE, 0)
    far = lax.dynamic_slice_in_dim(far_list, y * MINE, MINE, 0)
    slots = jnp.arange(64, dtype=jnp.int32)
    nodes = jnp.arange(32, dtype=jnp.int32)
    near_used = jnp.any(near[:, :, None] == slots, axis=1)
    far_used = jnp.any(far[:, :, None] == nodes, axis=1)
    rows = (y * MINE + jnp.arange(MINE, dtype=jnp.int32)) // 4
    requests = fetch_table[:, 0].reshape(3, 64)
    local = jnp.sum(jnp.where(rows[:, None, None] == jnp.arange(3)[None, :, None], requests[None], 0), axis=1)
    side = (slots // 2 + core) % 2
    near_value = jnp.where(near_used, side * LEAVES + local, -1)
    far_value = jnp.where(far_used, (nodes + core) % 2, -1)
    table = jnp.concatenate([near_value, far_value, jnp.full((MINE, 32), -1, jnp.int32)], axis=1)
    return jnp.pad(table, ((0, 8 - MINE), (0, 0))).astype(F32)


def on_device(points, weights, proj, fetch_table, near_list, far_list, skel_idx):
    y, z, x, core = place()
    table = lists(y, core, fetch_table, near_list, far_list)
    fixed = pltpu.with_memory_space_constraint
    points, weights, proj = (fixed(a, pltpu.HBM) for a in (points, weights, proj))
    left, right, norm, wcat, found = gather(points, weights, proj, skel_idx, table)
    spot = (z * SIDE + x).reshape(1).astype(jnp.int32)
    left, wcat = fixed(left, pltpu.HBM), fixed(wcat, pltpu.HBM)
    right, norm = fixed(right, VMEM), fixed(norm, VMEM)
    partial, extra, chosen = pairs(spot, found, left, right, norm, wcat)
    return scatter(chosen, fixed(partial, VMEM), fixed(extra, pltpu.HBM), left, right, norm, wcat)


def solution(mesh):
    placed = (
        P(None, "dev"),
        P("dev", None),
        P(None, "dev"),
        P(None, "dev", None, None),
        P("dev", None),
        P("dev", None),
        P("dev", None),
    )
    return jax.shard_map(
        on_device, mesh=mesh, in_specs=placed, out_specs=P("dev", None), check_vma=False
    )
```

```python
import functools
import math

import jax
import jax.numpy as jnp
from jax import lax
from jax.experimental import pallas as pl
from jax.experimental.pallas import tpu as pltpu
from jax.sharding import PartitionSpec as P

F32, BF16 = jnp.float32, jnp.bfloat16
MESH = pl.DeviceIdType.MESH
VMEM = pltpu.VMEM
LOG2E = math.log2(math.e)
SIDE = 4
SPOTS = SIDE * SIDE
LEAF, DIM, WCOL, SKEL = 512, 64, 128, 256
LEAVES = 12
MINE = 3
COLPTS = LEAVES * LEAF
HALF = LEAF // 2
PAYLOAD = MINE * HALF + 8
TARGETS = SPOTS * MINE
IDLE = 2 * COLPTS + 2 * SKEL
SOURCES = IDLE + LEAF
BLOCK = 256
BLOCKS = SOURCES // BLOCK
LATER = (MINE - 1) * SPOTS
CHUNK = 1024
SCALE = LOG2E / 32.0
K1_VMEM, K2_VMEM, K3_VMEM = 44 << 20, 32 << 20, 38 << 20
CUTS = (0, 192, 384, 576, PAYLOAD)


def mm(a, b):
    return jnp.dot(a, b, preferred_element_type=F32)


def split2(v):
    high = v.astype(BF16)
    return high, (v - high.astype(F32)).astype(BF16)


def place():
    y, dev = lax.axis_index("grp"), lax.axis_index("dev")
    return y, lax.div(dev, 8), lax.rem(lax.div(dev, 2), SIDE), lax.rem(dev, 2)


def shift(k, first, second):
    sign = 1 if k % 2 == 0 else -1
    along_x, along_z = (first, second) if k < 2 else (second, first)
    return sign * along_z % SIDE, sign * along_x % SIDE


class Around:
    def __init__(self):
        self.y, self.z, self.x, self.core = place()
        zs = [lax.rem(self.z + a, SIDE) for a in range(SIDE)]
        xs = [lax.rem(self.x + a, SIDE) for a in range(SIDE)]
        self.spots = {(a, b): zs[a] * SIDE + xs[b] for a in range(SIDE) for b in range(SIDE)}
        self.devices = {
            (a, b): (self.y, self.spots[a, b] * 2 + self.core) for a, b in ((1, 0), (3, 0), (0, 1), (0, 3))
        }
        self.sibling = (self.y, self.spots[0, 0] * 2 + 1 - self.core)

    def spot(self, k, first, second):
        return self.spots[shift(k, first, second)]

    def next(self, k, along_first):
        return self.devices[shift(k, 1, 0) if along_first else shift(k, 0, 1)]


def greet(peers):
    barrier = pltpu.get_barrier_semaphore()
    for peer in peers:
        pl.semaphore_signal(barrier, inc=1, device_id=peer, device_id_type=MESH)
    pl.semaphore_wait(barrier, len(peers))


def put_source(block, right, norm, first):
    high, low = split2(block * (2.0 * SCALE))
    total = -SCALE * jnp.sum(block * block, axis=0, keepdims=True)
    for n in range(block.shape[1] // BLOCK):
        cols = slice(n * BLOCK, (n + 1) * BLOCK)
        right[first + n, 0:DIM, :] = high[:, cols]
        right[first + n, DIM : 2 * DIM, :] = high[:, cols]
        right[first + n, 2 * DIM : 3 * DIM, :] = low[:, cols]
        right[first + n, 3 * DIM : 4 * DIM, :] = jnp.full((DIM, BLOCK), -1.0, BF16)
        norm[first + n] = total[:, cols]


def put_weights(block, wcat, first):
    high, low = split2(block)
    for n in range(block.shape[0] // BLOCK):
        rows = slice(n * BLOCK, (n + 1) * BLOCK)
        wcat[first + n, :, 0:WCOL] = high[rows]
        wcat[first + n, :, WCOL : 2 * WCOL] = low[rows]


def put_target(both, left, at):
    lane = lax.broadcasted_iota(jnp.int32, both.shape, 1)
    first_half = lane < DIM
    first_quarter = lane % DIM < DIM // 2
    high = both.astype(BF16).astype(F32)
    low = both - high
    high_r, low_r = pltpu.roll(high, DIM, 1), pltpu.roll(low, DIM, 1)
    square = both * both * SCALE
    down = square + pltpu.roll(square, 32, 1)
    up = square + pltpu.roll(square, 96, 1)
    up_high = up.astype(BF16).astype(F32)
    down_low = down - down.astype(BF16).astype(F32)
    sums = jnp.where(first_quarter, up_high, down_low)
    left[pl.ds(at, HALF), 0:128] = jnp.where(first_half, high, low_r).astype(BF16)
    left[pl.ds(at, HALF), 128:256] = jnp.where(first_half, high, pltpu.roll(sums, DIM, 1)).astype(BF16)
    left[pl.ds(at + HALF, HALF), 0:128] = jnp.where(first_half, high_r, low).astype(BF16)
    left[pl.ds(at + HALF, HALF), 128:256] = jnp.where(first_half, high_r, sums).astype(BF16)


def gather_kernel(
    points_hbm, weights_hbm, proj_hbm, index, table,
    left_hbm, right, norm, wcat_hbm, found,
    left, wcat, payload, gathered, own, points, points2, weights, weights2, proj, coords, coords2, values, values2,
    send, recv, pair_send, pair_recv, load_sem, left_sem,
):
    around = Around()
    y = around.y
    loads = [
        pltpu.make_async_copy(
            points_hbm.at[:, pl.ds(pl.multiple_of(y * (MINE * LEAF), LEAF), MINE * LEAF)], own, load_sem.at[0]
        ),
        pltpu.make_async_copy(points_hbm, points, load_sem.at[1]),
        pltpu.make_async_copy(weights_hbm, weights, load_sem.at[2]),
    ]

    def proj_load(n):
        at = pl.multiple_of(n * CHUNK, CHUNK)
        return pltpu.make_async_copy(proj_hbm.at[:, pl.ds(at, CHUNK)], proj.at[n % 2], load_sem.at[3 + n % 2])

    for c in loads:
        c.start()
    proj_load(0).start()
    greet(list(around.devices.values()) + [around.sibling])

    loads[0].wait()
    for leaf in range(MINE):
        block = own[:, leaf * LEAF : (leaf + 1) * LEAF]
        packed = jnp.concatenate([block[:, :HALF], block[:, HALF:]], axis=0)
        payload[leaf * HALF : (leaf + 1) * HALF, :] = packed.T
    payload[MINE * HALF :, :] = table[...]

    started, swaps, handed = [], [], []

    def spot_of(k, i, j):
        return around.spot(k, -i, -j)

    def copy(k, i, j, first):
        rows = pl.ds(CUTS[k], CUTS[k + 1] - CUTS[k])
        arrival = (i + 1) * SIDE + j if first else i * SIDE + j + 1
        number = i if first else SIDE - 1 + i * (SIDE - 1) + j
        target = gathered.at[spot_of(k, i, j), rows]
        c = pltpu.make_async_remote_copy(
            src_ref=payload.at[rows] if i == 0 and j == 0 else target,
            dst_ref=target,
            send_sem=send.at[k, number],
            recv_sem=recv.at[k, arrival],
            device_id=around.next(k, first),
            device_id_type=MESH,
        )
        c.start()
        started.append(c)

    def forward(level):
        for i in range(SIDE):
            j = level - i
            if not 0 <= j < SIDE:
                continue
            for k in range(4):
                if level > 0:
                    rows = pl.ds(CUTS[k], CUTS[k + 1] - CUTS[k])
                    here = gathered.at[spot_of(k, i, j), rows]
                    pltpu.make_async_copy(here, here, recv.at[k, i * SIDE + j]).wait()
                if j == 0 and i < SIDE - 1:
                    copy(k, i, j, True)
                if j < SIDE - 1:
                    copy(k, i, j, False)

    def swap(n, a, b):
        c = pltpu.make_async_remote_copy(
            src_ref=a, dst_ref=b, send_sem=pair_send.at[n], recv_sem=pair_recv.at[n],
            device_id=around.sibling, device_id_type=MESH,
        )
        c.start()
        swaps.append(c)

    def targets_at(dz, dx):
        spot = around.spots[dz, dx]

        def leaf_rows(leaf, _):
            rows = pl.ds(pl.multiple_of(leaf * HALF, HALF), HALF)
            both = payload[rows, :] if dz == dx == 0 else gathered[spot, rows, :]
            put_target(both, left, pl.multiple_of((leaf * SPOTS + spot) * LEAF, LEAF))
            return _

        lax.fori_loop(0, MINE, leaf_rows, 0)
        lists_here = payload[MINE * HALF :, :] if dz == dx == 0 else gathered[spot, MINE * HALF :, :]
        found[spot] = lists_here.astype(jnp.int32)
        for leaf in range(MINE):
            rows = pl.ds(pl.multiple_of((leaf * SPOTS + spot) * LEAF, LEAF), LEAF)
            c = pltpu.make_async_copy(left.at[rows], left_hbm.at[rows], left_sem.at[leaf, dz * SIDE + dx])
            c.start()
            handed.append(c)

    def column(points_ref, weights_ref, base):
        def one(n, _):
            at = pl.multiple_of(n * LEAF, LEAF)
            put_source(points_ref[:, pl.ds(at, LEAF)], right, norm, base + 2 * n)
            put_weights(weights_ref[pl.ds(at, LEAF), :], wcat, base + 2 * n)
            return _

        lax.fori_loop(0, LEAVES, one, 0)

    def spots_of(level):
        steps = (0, 1, 2, 3)

        def done(dz, dx):
            far = lambda d: max(d, (SIDE - d) % SIDE)
            return far(dz) + far(dx)

        return [(dz, dx) for dz in steps for dx in steps if done(dz, dx) == level]

    forward(0)
    loads[1].wait()
    loads[2].wait()
    swap(0, points, points2)
    swap(1, weights, weights2)
    targets_at(0, 0)
    for n in range(IDLE // BLOCK, BLOCKS):
        right[n] = jnp.zeros((4 * DIM, BLOCK), BF16)
        norm[n] = jnp.zeros((1, BLOCK), F32)
        wcat[n] = jnp.zeros((BLOCK, 2 * WCOL), BF16)
    column(points, weights, 0)
    forward(1)
    values[...] = jnp.zeros_like(values)
    coords[...] = jnp.zeros_like(coords)

    def skeleton(n, _):
        proj_load(n).wait()

        @pl.when(n + 1 < COLPTS // CHUNK)
        def next_load():
            proj_load(n + 1).start()

        at = pl.multiple_of(n * CHUNK, CHUNK)
        four = pl.ds(n * (CHUNK // BLOCK), CHUNK // BLOCK)
        wh, wl = wcat[four, :, 0:WCOL].reshape(CHUNK, WCOL), wcat[four, :, WCOL : 2 * WCOL].reshape(CHUNK, WCOL)
        ph, plow = split2(proj[n % 2])
        values[...] += mm(ph, wh) + mm(ph, wl) + mm(plow, wh)
        rows = lax.broadcasted_iota(jnp.int32, (CHUNK, SKEL), 0) + at
        pick = jnp.where(rows == index[...], 1.0, 0.0).astype(BF16)
        block = points[:, pl.ds(at, CHUNK)]
        first = block.astype(BF16)
        second, third = split2(block - first.astype(F32))
        coords[...] += mm(first, pick) + mm(second, pick) + mm(third, pick)
        return _

    lax.fori_loop(0, COLPTS // CHUNK, skeleton, 0)
    swap(2, coords, coords2)
    swap(3, values, values2)
    forward(2)
    put_source(coords[...], right, norm, 2 * COLPTS // BLOCK)
    put_weights(values[...], wcat, 2 * COLPTS // BLOCK)
    swaps[0].wait_recv()
    swaps[1].wait_recv()
    column(points2, weights2, COLPTS // BLOCK)
    forward(3)
    swaps[2].wait_recv()
    swaps[3].wait_recv()
    put_source(coords2[...], right, norm, (2 * COLPTS + SKEL) // BLOCK)
    put_weights(values2[...], wcat, (2 * COLPTS + SKEL) // BLOCK)
    handed.append(pltpu.make_async_copy(wcat, wcat_hbm, load_sem.at[5]))
    handed[-1].start()
    for level in (2, 3):
        for dz, dx in spots_of(level):
            targets_at(dz, dx)
    for level in (4, 5, 6):
        forward(level)
        for dz, dx in spots_of(level):
            targets_at(dz, dx)
    for c in started + swaps:
        c.wait_send()
    for c in handed:
        c.wait()


def gather(points, weights, proj, index, table):
    hbm = pl.BlockSpec(memory_space=pltpu.HBM)
    vmem = pl.BlockSpec(memory_space=VMEM)
    return pl.pallas_call(
        gather_kernel,
        out_shape=(
            pltpu.HBM((TARGETS * LEAF, 256), BF16),
            pltpu.VMEM((BLOCKS, 4 * DIM, BLOCK), BF16),
            pltpu.VMEM((BLOCKS, 1, BLOCK), F32),
            pltpu.HBM((BLOCKS, BLOCK, 2 * WCOL), BF16),
            jax.ShapeDtypeStruct((SPOTS, 8, 128), jnp.int32),
        ),
        in_specs=[hbm] * 3 + [vmem] * 2,
        out_specs=[hbm, vmem, vmem, hbm, vmem],
        scratch_shapes=[
            VMEM((TARGETS * LEAF, 256), BF16),
            VMEM((BLOCKS, BLOCK, 2 * WCOL), BF16),
            VMEM((PAYLOAD, 128), F32),
            VMEM((SPOTS, PAYLOAD, 128), F32),
            VMEM((DIM, MINE * LEAF), F32),
            VMEM((DIM, COLPTS), F32),
            VMEM((DIM, COLPTS), F32),
            VMEM((COLPTS, WCOL), F32),
            VMEM((COLPTS, WCOL), F32),
            VMEM((2, SKEL, CHUNK), F32),
            VMEM((DIM, SKEL), F32),
            VMEM((DIM, SKEL), F32),
            VMEM((SKEL, WCOL), F32),
            VMEM((SKEL, WCOL), F32),
            pltpu.SemaphoreType.DMA((4, 15)),
            pltpu.SemaphoreType.DMA((4, 16)),
            pltpu.SemaphoreType.DMA((4,)),
            pltpu.SemaphoreType.DMA((4,)),
            pltpu.SemaphoreType.DMA((6,)),
            pltpu.SemaphoreType.DMA((MINE, SPOTS)),
        ],
        compiler_params=pltpu.CompilerParams(
            collective_id=0, has_side_effects=True, vmem_limit_bytes=K1_VMEM
        ),
    )(points, weights, proj, index, table)


def produce(left, right, norm, at, block, width, high_ref, low_ref):
    blocks = range(width // BLOCK)
    columns = jnp.concatenate([right[block + n] for n in blocks], axis=1)
    norms = jnp.concatenate([norm[block + n] for n in blocks], axis=1)
    power = mm(left[pl.ds(at, LEAF), :], columns) + norms
    high_ref[:, :width], low_ref[:, :width] = split2(jnp.exp2(power))


def consume(wcat, out, at, block, width, high_ref, low_ref):
    rows = jnp.concatenate([wcat[block + n] for n in range(width // BLOCK)], axis=0)
    total = mm(high_ref[:, :width], rows)
    rest = mm(low_ref[:, :width], rows[:, :WCOL])
    out[pl.ds(at, LEAF), :] += total[:, :WCOL] + total[:, WCOL:] + rest


def near_start(source):
    return source * (LEAF // BLOCK)


def far_start(node):
    return 2 * COLPTS // BLOCK + node


def pair_kernel(
    spot_ref, table, left_hbm, right, norm, wcat_hbm, out, extra_hbm, slots,
    even, even_low, odd, odd_low, left, wcat, extra, near_pairs, far_pairs, near_extra, far_extra, packed, packed_smem, sem,
):
    first = pl.ds(0, SPOTS * LEAF)
    later = pl.ds(SPOTS * LEAF, LATER * LEAF)
    loads = [
        pltpu.make_async_copy(wcat_hbm, wcat, sem.at[0]),
        pltpu.make_async_copy(left_hbm.at[later], left.at[later], sem.at[1]),
        pltpu.make_async_copy(left_hbm.at[first], left.at[first], sem.at[2]),
    ]
    for c in loads:
        c.start()

    def clear(ref, n):
        def zero(t, _):
            ref[pl.ds(pl.multiple_of(t * LEAF, LEAF), LEAF), :] = jnp.zeros((LEAF, WCOL), F32)
            return _

        lax.fori_loop(0, n, zero, 0)

    spot = spot_ref[0]
    lane = lax.broadcasted_iota(jnp.int32, (8, 128), 1)
    lists_here = jnp.full((8, 128), -1, jnp.int32)
    for n in range(SPOTS):
        near = pltpu.roll(table[n], (8 * n - 4 * spot + 128) % 128, 1)
        far = pltpu.roll(table[n], (8 * n + 4 + 64 - 2 * spot) % 128, 1)
        at = lane - 8 * n
        lists_here = jnp.where(jnp.logical_and(at >= 0, at < 4), near, lists_here)
        lists_here = jnp.where(jnp.logical_and(at >= 4, at < 6), far, lists_here)
    packed[...] = lists_here
    to_smem = pltpu.make_async_copy(packed, packed_smem, sem.at[4])
    to_smem.start()
    clear(out, SPOTS + 1)
    clear(extra, LATER + 1)
    to_smem.wait()

    def used(t, slot):
        return packed_smem[t // SPOTS, 8 * (t % SPOTS) + slot]

    def note(t, counts):
        near, far = counts
        for slot in range(4):
            source = used(t, slot)
            near_pairs[near] = t * 64 + source
            near = near + jnp.where(source >= 0, 1, 0)
        for slot in range(2):
            node = used(t, 4 + slot)
            far_pairs[far] = t * 64 + node
            far = far + jnp.where(node >= 0, 1, 0)
        return near, far

    near_count, far_count = lax.fori_loop(0, SPOTS, note, (0, 0))

    def note_later(t, counts):
        near, far = counts
        slots[t, 0] = IDLE // LEAF
        have = 0
        for slot in range(4):
            source = used(t + SPOTS, slot)
            hit = source >= 0
            take = jnp.logical_and(hit, have < 1)
            slots[t, jnp.where(take, 0, 7)] = source
            have = have + jnp.where(take, 1, 0)
            near_extra[near] = t * 64 + source
            near = near + jnp.where(jnp.logical_and(hit, jnp.logical_not(take)), 1, 0)
        for slot in range(2):
            node = used(t + SPOTS, 4 + slot)
            far_extra[far] = t * 64 + node
            far = far + jnp.where(node >= 0, 1, 0)
        return near, far

    near_more, far_more = lax.fori_loop(0, LATER, note_later, (0, 0))
    for n in range(3):
        near_pairs[near_count + n] = SPOTS * 64
        far_pairs[far_count + n] = SPOTS * 64
        near_extra[near_more + n] = LATER * 64
        far_extra[far_more + n] = LATER * 64

    def run(pair_list, count, start_of, width, ref, n_targets, base):
        def make(n, high_ref, low_ref):
            code = pair_list[n]
            t = code // 64
            at = pl.multiple_of((base + jnp.where(t < n_targets, t, 0)) * LEAF, LEAF)
            produce(left, right, norm, at, start_of(code % 64), width, high_ref, low_ref)

        def use(n, high_ref, low_ref):
            code = pair_list[n]
            at = pl.multiple_of((code // 64) * LEAF, LEAF)
            consume(wcat, ref, at, start_of(code % 64), width, high_ref, low_ref)

        make(0, even, even_low)

        def two(m, _):
            make(2 * m + 1, odd, odd_low)
            use(2 * m, even, even_low)
            make(2 * m + 2, even, even_low)
            use(2 * m + 1, odd, odd_low)
            return _

        lax.fori_loop(0, (count + 1) // 2, two, 0)

    loads[0].wait()
    loads[1].wait()
    run(near_extra, near_more, near_start, LEAF, extra, LATER, SPOTS)
    run(far_extra, far_more, far_start, SKEL, extra, LATER, SPOTS)
    handed = pltpu.make_async_copy(extra.at[pl.ds(0, LATER * LEAF)], extra_hbm, sem.at[3])
    handed.start()
    loads[2].wait()
    run(near_pairs, near_count, near_start, LEAF, out, SPOTS, 0)
    run(far_pairs, far_count, far_start, SKEL, out, SPOTS, 0)
    handed.wait()


def pairs(spot, table, left, right, norm, wcat):
    smem = pl.BlockSpec(memory_space=pltpu.SMEM)
    vmem = pl.BlockSpec(memory_space=VMEM)
    hbm = pl.BlockSpec(memory_space=pltpu.HBM)
    return pl.pallas_call(
        pair_kernel,
        out_shape=(
            pltpu.VMEM(((SPOTS + 1) * LEAF, WCOL), F32),
            pltpu.HBM((LATER * LEAF, WCOL), F32),
            jax.ShapeDtypeStruct((LATER, 8), jnp.int32),
        ),
        in_specs=[smem, vmem, hbm, vmem, vmem, hbm],
        out_specs=(vmem, hbm, smem),
        scratch_shapes=[VMEM((LEAF, LEAF), BF16)] * 4
        + [
            VMEM((TARGETS * LEAF, 256), BF16),
            VMEM((BLOCKS, BLOCK, 2 * WCOL), BF16),
            VMEM(((LATER + 1) * LEAF, WCOL), F32),
            pltpu.SMEM((SPOTS * 4 + 3,), jnp.int32),
            pltpu.SMEM((SPOTS * 2 + 3,), jnp.int32),
            pltpu.SMEM((LATER * 4 + 3,), jnp.int32),
            pltpu.SMEM((LATER * 2 + 3,), jnp.int32),
            VMEM((8, 128), jnp.int32),
            pltpu.SMEM((8, 128), jnp.int32),
            pltpu.SemaphoreType.DMA((5,)),
        ],
        compiler_params=pltpu.CompilerParams(vmem_limit_bytes=K2_VMEM),
    )(spot, table, left, right, norm, wcat)


QUARTER = LEAF // 4


def scatter_kernel(
    chosen, partial, extra_hbm, left_hbm, right, norm, wcat_hbm, out,
    slots, turn, sums, left, wcat, even, even_low, odd, odd_low,
    send, recv, turn_send, turn_recv, y_send, y_recv, load_sem,
):
    around = Around()
    y = around.y
    loads = [
        pltpu.make_async_copy(left_hbm.at[pl.ds(SPOTS * LEAF, LATER * LEAF)], left, load_sem.at[0]),
        pltpu.make_async_copy(wcat_hbm, wcat, load_sem.at[1]),
        pltpu.make_async_copy(extra_hbm, sums, load_sem.at[2]),
    ]
    for c in loads:
        c.start()
    planes = [lax.rem(y + a, SIDE) for a in range(SIDE)]
    here = around.spots[0, 0] * 2 + around.core
    above, below = (planes[1], here), (planes[3], here)
    greet(list(around.devices.values()) + [above, below])
    started = []

    def own(k, leaf, first, second):
        place_of = around.spot(k, first, second) + (0 if leaf == 0 else (leaf - 1) * SPOTS)
        rows = pl.ds(pl.multiple_of(place_of * LEAF + k * QUARTER, QUARTER), QUARTER)
        return partial.at[rows] if leaf == 0 else sums.at[rows]

    def begin(make):
        make().start()
        started.append(make)

    def step_first(k, leaf, step, j, source):
        n = (leaf * 3 + step) * SIDE + j

        def make():
            return pltpu.make_async_remote_copy(
                src_ref=source(), dst_ref=slots.at[k, n], send_sem=send.at[k, n], recv_sem=recv.at[k, n],
                device_id=around.next(k, True), device_id_type=MESH,
            )

        begin(make)

    def arrived_first(k, leaf, step, j):
        n = (leaf * 3 + step) * SIDE + j
        pltpu.make_async_copy(slots.at[k, n], slots.at[k, n], recv.at[k, n]).wait()
        slots[k, n] += own(k, leaf, 2 - step, 3 - j)[...]
        return n

    def step_second(k, leaf, step, source):
        n = leaf * 3 + step

        def make():
            return pltpu.make_async_remote_copy(
                src_ref=source(), dst_ref=turn.at[k, n], send_sem=turn_send.at[k, n], recv_sem=turn_recv.at[k, n],
                device_id=around.next(k, False), device_id_type=MESH,
            )

        begin(make)

    def rows_of(plane, leaf, k):
        return pl.ds(pl.multiple_of((plane * MINE + leaf) * LEAF + k * QUARTER, QUARTER), QUARTER)

    def to_y(leaf, k, number, plane, up):
        n = (leaf * 4 + k) * 3 + number

        def make():
            rows = rows_of(plane, leaf, k)
            return pltpu.make_async_remote_copy(
                src_ref=out.at[rows], dst_ref=out.at[rows], send_sem=y_send.at[n], recv_sem=y_recv.at[n],
                device_id=above if up else below, device_id_type=MESH,
            )

        begin(make)

    def y_wait(leaf, k, number, plane):
        rows = rows_of(plane, leaf, k)
        n = (leaf * 4 + k) * 3 + number
        pltpu.make_async_copy(out.at[rows], out.at[rows], y_recv.at[n]).wait()

    def second_axis(k, leaf, j):
        n = arrived_first(k, leaf, 2, j)
        if j > 0:
            m = leaf * 3 + j - 1
            pltpu.make_async_copy(turn.at[k, m], turn.at[k, m], turn_recv.at[k, m]).wait()
        if j == 0:
            step_second(k, leaf, 0, lambda: slots.at[k, n])
        elif j < 3:
            turn[k, m] += slots[k, n]
            step_second(k, leaf, j, lambda: turn.at[k, m])
        else:
            out[rows_of(y, leaf, k), :] = turn[k, m] + slots[k, n]
            to_y(leaf, k, 0, y, True)
            to_y(leaf, k, 1, y, False)

    def second_hop(leaf, k):
        lower, upper = planes[3], planes[1]
        if k % 2 == 0:
            y_wait(leaf, k, 0, lower)
            to_y(leaf, k, 2, lower, True)
        else:
            y_wait(leaf, k, 1, upper)
            to_y(leaf, k, 2, upper, False)

    def last_arrivals(leaf, k):
        lower, upper, across = planes[3], planes[1], planes[2]
        if k % 2 == 0:
            y_wait(leaf, k, 1, upper)
        else:
            y_wait(leaf, k, 0, lower)
        y_wait(leaf, k, 2, across)

    def start_leaf(leaf):
        for j in range(SIDE):
            for k in range(4):
                step_first(k, leaf, 0, j, functools.partial(own, k, leaf, 3, 3 - j))

    def part(leaf, n):
        j = n % SIDE
        for k in range(4):
            if leaf < MINE:
                m = arrived_first(k, leaf, n // SIDE, j)
                step_first(k, leaf, 1 + n // SIDE, j, lambda k=k, m=m: slots.at[k, m])
            if leaf > 0 and n < SIDE:
                second_axis(k, leaf - 1, j)

    def make(t, high_ref, low_ref):
        at = pl.multiple_of(t * LEAF, LEAF)
        produce(left, right, norm, at, near_start(chosen[t, 0]), LEAF, high_ref, low_ref)

    def use(t, high_ref, low_ref):
        at = pl.multiple_of(t * LEAF, LEAF)
        consume(wcat, sums, at, near_start(chosen[t, 0]), LEAF, high_ref, low_ref)

    def two_targets(t):
        make(t + 1, odd, odd_low)
        use(t, even, even_low)
        make((t + 2) % LATER, even, even_low)
        use(t + 1, odd, odd_low)

    for leaf in range(MINE + 1):
        if leaf < MINE:
            start_leaf(leaf)
        if leaf == 0:
            for c in loads:
                c.wait()
            make(0, even, even_low)
        if leaf < MINE - 1:

            def step(n, _, leaf=leaf):
                two_targets(leaf * SPOTS + 2 * n)
                for which in range(2 * SIDE):
                    pl.when(n == which)(functools.partial(part, leaf, which))
                return _

            lax.fori_loop(0, 2 * SIDE, step, 0)
        else:
            for n in range(2 * SIDE):
                part(leaf, n)
        if leaf > 0:
            for k in range(4):
                second_hop(leaf - 1, k)
    for leaf in range(MINE):
        for k in range(4):
            last_arrivals(leaf, k)
    for again in started:
        again().wait_send()


def scatter(chosen, partial, extra, left, right, norm, wcat):
    smem = pl.BlockSpec(memory_space=pltpu.SMEM)
    vmem = pl.BlockSpec(memory_space=VMEM)
    hbm = pl.BlockSpec(memory_space=pltpu.HBM)
    return pl.pallas_call(
        scatter_kernel,
        out_shape=jax.ShapeDtypeStruct((COLPTS, WCOL), F32),
        in_specs=[smem, vmem, hbm, hbm, vmem, vmem, hbm],
        out_specs=vmem,
        scratch_shapes=[
            VMEM((4, MINE * 3 * SIDE, QUARTER, WCOL), F32),
            VMEM((4, MINE * 3, QUARTER, WCOL), F32),
            VMEM((LATER * LEAF, WCOL), F32),
            VMEM((LATER * LEAF, 256), BF16),
            VMEM((BLOCKS, BLOCK, 2 * WCOL), BF16),
        ]
        + [VMEM((LEAF, LEAF), BF16)] * 4
        + [
            pltpu.SemaphoreType.DMA((4, MINE * 3 * SIDE)),
            pltpu.SemaphoreType.DMA((4, MINE * 3 * SIDE)),
            pltpu.SemaphoreType.DMA((4, MINE * 3)),
            pltpu.SemaphoreType.DMA((4, MINE * 3)),
            pltpu.SemaphoreType.DMA((MINE * 4 * 3,)),
            pltpu.SemaphoreType.DMA((MINE * 4 * 3,)),
            pltpu.SemaphoreType.DMA((3,)),
        ],
        compiler_params=pltpu.CompilerParams(
            collective_id=1, has_side_effects=True, vmem_limit_bytes=K3_VMEM
        ),
    )(chosen, partial, extra, left, right, norm, wcat)


def lists(y, core, fetch_table, near_list, far_list):
    near = lax.dynamic_slice_in_dim(near_list, y * MINE, MINE, 0)
    far = lax.dynamic_slice_in_dim(far_list, y * MINE, MINE, 0)
    slots = jnp.arange(64, dtype=jnp.int32)
    nodes = jnp.arange(32, dtype=jnp.int32)
    near_used = jnp.any(near[:, :, None] == slots, axis=1)
    far_used = jnp.any(far[:, :, None] == nodes, axis=1)
    rows = (y * MINE + jnp.arange(MINE, dtype=jnp.int32)) // 4
    requests = fetch_table[:, 0].reshape(3, 64)
    local = jnp.sum(jnp.where(rows[:, None, None] == jnp.arange(3)[None, :, None], requests[None], 0), axis=1)
    side = (slots // 2 + core) % 2
    near_value = jnp.where(near_used, side * LEAVES + local, -1)
    far_value = jnp.where(far_used, (nodes + core) % 2, -1)
    table = jnp.concatenate([near_value, far_value, jnp.full((MINE, 32), -1, jnp.int32)], axis=1)
    return jnp.pad(table, ((0, 8 - MINE), (0, 0))).astype(F32)


def on_device(points, weights, proj, fetch_table, near_list, far_list, skel_idx):
    y, z, x, core = place()
    table = lists(y, core, fetch_table, near_list, far_list)
    fixed = pltpu.with_memory_space_constraint
    points, weights, proj = (fixed(a, pltpu.HBM) for a in (points, weights, proj))
    left, right, norm, wcat, found = gather(points, weights, proj, skel_idx, table)
    spot = (z * SIDE + x).reshape(1).astype(jnp.int32)
    left, wcat = fixed(left, pltpu.HBM), fixed(wcat, pltpu.HBM)
    right, norm = fixed(right, VMEM), fixed(norm, VMEM)
    partial, extra, chosen = pairs(spot, found, left, right, norm, wcat)
    return scatter(chosen, fixed(partial, VMEM), fixed(extra, pltpu.HBM), left, right, norm, wcat)


def solution(mesh):
    placed = (
        P(None, "dev"),
        P("dev", None),
        P(None, "dev"),
        P(None, "dev", None, None),
        P("dev", None),
        P("dev", None),
        P("dev", None),
    )
    return jax.shard_map(
        on_device, mesh=mesh, in_specs=placed, out_specs=P("dev", None), check_vma=False
    )
```

```python
import functools
import math

import jax
import jax.numpy as jnp
from jax import lax
from jax.experimental import pallas as pl
from jax.experimental.pallas import tpu as pltpu
from jax.sharding import PartitionSpec as P

F32, BF16 = jnp.float32, jnp.bfloat16
MESH = pl.DeviceIdType.MESH
VMEM = pltpu.VMEM
LOG2E = math.log2(math.e)
SIDE = 4
SPOTS = SIDE * SIDE
LEAF, DIM, WCOL, SKEL = 512, 64, 128, 256
LEAVES = 12
MINE = 3
COLPTS = LEAVES * LEAF
HALF = LEAF // 2
PAYLOAD = MINE * HALF + 8
TARGETS = SPOTS * MINE
IDLE = 2 * COLPTS + 2 * SKEL
SOURCES = IDLE + LEAF
BLOCK = 256
BLOCKS = SOURCES // BLOCK
LATER = (MINE - 1) * SPOTS
CHUNK = 1024
SCALE = LOG2E / 32.0
K1_VMEM, K2_VMEM, K3_VMEM = 44 << 20, 32 << 20, 38 << 20
CUTS = (0, 192, 384, 576, PAYLOAD)


def mm(a, b):
    return jnp.dot(a, b, preferred_element_type=F32)


def split2(v):
    high = v.astype(BF16)
    return high, (v - high.astype(F32)).astype(BF16)


def place():
    y, dev = lax.axis_index("grp"), lax.axis_index("dev")
    return y, lax.div(dev, 8), lax.rem(lax.div(dev, 2), SIDE), lax.rem(dev, 2)


def shift(k, first, second):
    sign = 1 if k % 2 == 0 else -1
    along_x, along_z = (first, second) if k < 2 else (second, first)
    return sign * along_z % SIDE, sign * along_x % SIDE


class Around:
    def __init__(self):
        self.y, self.z, self.x, self.core = place()
        zs = [lax.rem(self.z + a, SIDE) for a in range(SIDE)]
        xs = [lax.rem(self.x + a, SIDE) for a in range(SIDE)]
        self.spots = {(a, b): zs[a] * SIDE + xs[b] for a in range(SIDE) for b in range(SIDE)}
        self.devices = {
            (a, b): (self.y, self.spots[a, b] * 2 + self.core) for a, b in ((1, 0), (3, 0), (0, 1), (0, 3))
        }
        self.sibling = (self.y, self.spots[0, 0] * 2 + 1 - self.core)

    def spot(self, k, first, second):
        return self.spots[shift(k, first, second)]

    def next(self, k, along_first):
        return self.devices[shift(k, 1, 0) if along_first else shift(k, 0, 1)]


def greet(peers):
    barrier = pltpu.get_barrier_semaphore()
    for peer in peers:
        pl.semaphore_signal(barrier, inc=1, device_id=peer, device_id_type=MESH)
    pl.semaphore_wait(barrier, len(peers))


def put_source(block, right, norm, first):
    high, low = split2(block * (2.0 * SCALE))
    total = -SCALE * jnp.sum(block * block, axis=0, keepdims=True)
    for n in range(block.shape[1] // BLOCK):
        cols = slice(n * BLOCK, (n + 1) * BLOCK)
        right[first + n, 0:DIM, :] = high[:, cols]
        right[first + n, DIM : 2 * DIM, :] = high[:, cols]
        right[first + n, 2 * DIM : 3 * DIM, :] = low[:, cols]
        right[first + n, 3 * DIM : 4 * DIM, :] = jnp.full((DIM, BLOCK), -1.0, BF16)
        norm[first + n] = total[:, cols]


def put_weights(block, wcat, first):
    high, low = split2(block)
    for n in range(block.shape[0] // BLOCK):
        rows = slice(n * BLOCK, (n + 1) * BLOCK)
        wcat[first + n, :, 0:WCOL] = high[rows]
        wcat[first + n, :, WCOL : 2 * WCOL] = low[rows]


def put_target(both, left, at):
    lane = lax.broadcasted_iota(jnp.int32, both.shape, 1)
    first_half = lane < DIM
    first_quarter = lane % DIM < DIM // 2
    high = both.astype(BF16).astype(F32)
    low = both - high
    high_r, low_r = pltpu.roll(high, DIM, 1), pltpu.roll(low, DIM, 1)
    square = both * both * SCALE
    down = square + pltpu.roll(square, 32, 1)
    up = square + pltpu.roll(square, 96, 1)
    up_high = up.astype(BF16).astype(F32)
    down_low = down - down.astype(BF16).astype(F32)
    sums = jnp.where(first_quarter, up_high, down_low)
    left[pl.ds(at, HALF), 0:128] = jnp.where(first_half, high, low_r).astype(BF16)
    left[pl.ds(at, HALF), 128:256] = jnp.where(first_half, high, pltpu.roll(sums, DIM, 1)).astype(BF16)
    left[pl.ds(at + HALF, HALF), 0:128] = jnp.where(first_half, high_r, low).astype(BF16)
    left[pl.ds(at + HALF, HALF), 128:256] = jnp.where(first_half, high_r, sums).astype(BF16)


def gather_kernel(
    points_hbm, weights_hbm, proj_hbm, index, table,
    left_hbm, right, norm, wcat_hbm, found,
    left, wcat, payload, gathered, own, points, points2, weights, weights2, proj, coords, coords2, values, values2,
    send, recv, pair_send, pair_recv, load_sem, left_sem,
):
    around = Around()
    y = around.y
    loads = [
        pltpu.make_async_copy(
            points_hbm.at[:, pl.ds(pl.multiple_of(y * (MINE * LEAF), LEAF), MINE * LEAF)], own, load_sem.at[0]
        ),
        pltpu.make_async_copy(points_hbm, points, load_sem.at[1]),
        pltpu.make_async_copy(weights_hbm, weights, load_sem.at[2]),
    ]

    def proj_load(n):
        at = pl.multiple_of(n * CHUNK, CHUNK)
        return pltpu.make_async_copy(proj_hbm.at[:, pl.ds(at, CHUNK)], proj.at[n % 2], load_sem.at[3 + n % 2])

    for c in loads:
        c.start()
    proj_load(0).start()
    greet(list(around.devices.values()) + [around.sibling])

    loads[0].wait()
    for leaf in range(MINE):
        block = own[:, leaf * LEAF : (leaf + 1) * LEAF]
        packed = jnp.concatenate([block[:, :HALF], block[:, HALF:]], axis=0)
        payload[leaf * HALF : (leaf + 1) * HALF, :] = packed.T
    payload[MINE * HALF :, :] = table[...]

    started, swaps, handed = [], [], []

    def spot_of(k, i, j):
        return around.spot(k, -i, -j)

    def copy(k, i, j, first):
        rows = pl.ds(CUTS[k], CUTS[k + 1] - CUTS[k])
        arrival = (i + 1) * SIDE + j if first else i * SIDE + j + 1
        number = i if first else SIDE - 1 + i * (SIDE - 1) + j
        target = gathered.at[spot_of(k, i, j), rows]
        c = pltpu.make_async_remote_copy(
            src_ref=payload.at[rows] if i == 0 and j == 0 else target,
            dst_ref=target,
            send_sem=send.at[k, number],
            recv_sem=recv.at[k, arrival],
            device_id=around.next(k, first),
            device_id_type=MESH,
        )
        c.start()
        started.append(c)

    def forward(level):
        for i in range(SIDE):
            j = level - i
            if not 0 <= j < SIDE:
                continue
            for k in range(4):
                if level > 0:
                    rows = pl.ds(CUTS[k], CUTS[k + 1] - CUTS[k])
                    here = gathered.at[spot_of(k, i, j), rows]
                    pltpu.make_async_copy(here, here, recv.at[k, i * SIDE + j]).wait()
                if j == 0 and i < SIDE - 1:
                    copy(k, i, j, True)
                if j < SIDE - 1:
                    copy(k, i, j, False)

    def swap(n, a, b):
        c = pltpu.make_async_remote_copy(
            src_ref=a, dst_ref=b, send_sem=pair_send.at[n], recv_sem=pair_recv.at[n],
            device_id=around.sibling, device_id_type=MESH,
        )
        c.start()
        swaps.append(c)

    def targets_at(dz, dx):
        spot = around.spots[dz, dx]

        def leaf_rows(leaf, _):
            rows = pl.ds(pl.multiple_of(leaf * HALF, HALF), HALF)
            both = payload[rows, :] if dz == dx == 0 else gathered[spot, rows, :]
            put_target(both, left, pl.multiple_of((leaf * SPOTS + spot) * LEAF, LEAF))
            return _

        lax.fori_loop(0, MINE, leaf_rows, 0)
        lists_here = payload[MINE * HALF :, :] if dz == dx == 0 else gathered[spot, MINE * HALF :, :]
        found[spot] = lists_here.astype(jnp.int32)
        for leaf in range(MINE):
            rows = pl.ds(pl.multiple_of((leaf * SPOTS + spot) * LEAF, LEAF), LEAF)
            c = pltpu.make_async_copy(left.at[rows], left_hbm.at[rows], left_sem.at[leaf, dz * SIDE + dx])
            c.start()
            handed.append(c)

    def column(points_ref, weights_ref, base):
        def one(n, _):
            at = pl.multiple_of(n * LEAF, LEAF)
            put_source(points_ref[:, pl.ds(at, LEAF)], right, norm, base + 2 * n)
            put_weights(weights_ref[pl.ds(at, LEAF), :], wcat, base + 2 * n)
            return _

        lax.fori_loop(0, LEAVES, one, 0)

    def spots_of(level):
        steps = (0, 1, 2, 3)

        def done(dz, dx):
            far = lambda d: max(d, (SIDE - d) % SIDE)
            return far(dz) + far(dx)

        return [(dz, dx) for dz in steps for dx in steps if done(dz, dx) == level]

    forward(0)
    loads[1].wait()
    loads[2].wait()
    swap(0, points, points2)
    swap(1, weights, weights2)
    targets_at(0, 0)
    for n in range(IDLE // BLOCK, BLOCKS):
        right[n] = jnp.zeros((4 * DIM, BLOCK), BF16)
        norm[n] = jnp.zeros((1, BLOCK), F32)
        wcat[n] = jnp.zeros((BLOCK, 2 * WCOL), BF16)
    column(points, weights, 0)
    forward(1)
    values[...] = jnp.zeros_like(values)
    coords[...] = jnp.zeros_like(coords)

    def skeleton(n, _):
        proj_load(n).wait()

        @pl.when(n + 1 < COLPTS // CHUNK)
        def next_load():
            proj_load(n + 1).start()

        at = pl.multiple_of(n * CHUNK, CHUNK)
        four = pl.ds(n * (CHUNK // BLOCK), CHUNK // BLOCK)
        wh, wl = wcat[four, :, 0:WCOL].reshape(CHUNK, WCOL), wcat[four, :, WCOL : 2 * WCOL].reshape(CHUNK, WCOL)
        ph, plow = split2(proj[n % 2])
        values[...] += mm(ph, wh) + mm(ph, wl) + mm(plow, wh)
        rows = lax.broadcasted_iota(jnp.int32, (CHUNK, SKEL), 0) + at
        pick = jnp.where(rows == index[...], 1.0, 0.0).astype(BF16)
        block = points[:, pl.ds(at, CHUNK)]
        first = block.astype(BF16)
        second, third = split2(block - first.astype(F32))
        coords[...] += mm(first, pick) + mm(second, pick) + mm(third, pick)
        return _

    lax.fori_loop(0, COLPTS // CHUNK, skeleton, 0)
    swap(2, coords, coords2)
    swap(3, values, values2)
    forward(2)
    put_source(coords[...], right, norm, 2 * COLPTS // BLOCK)
    put_weights(values[...], wcat, 2 * COLPTS // BLOCK)
    swaps[0].wait_recv()
    swaps[1].wait_recv()
    column(points2, weights2, COLPTS // BLOCK)
    forward(3)
    swaps[2].wait_recv()
    swaps[3].wait_recv()
    put_source(coords2[...], right, norm, (2 * COLPTS + SKEL) // BLOCK)
    put_weights(values2[...], wcat, (2 * COLPTS + SKEL) // BLOCK)
    handed.append(pltpu.make_async_copy(wcat, wcat_hbm, load_sem.at[5]))
    handed[-1].start()
    for level in (2, 3):
        for dz, dx in spots_of(level):
            targets_at(dz, dx)
    for level in (4, 5, 6):
        forward(level)
        for dz, dx in spots_of(level):
            targets_at(dz, dx)
    for c in started + swaps:
        c.wait_send()
    for c in handed:
        c.wait()


def gather(points, weights, proj, index, table):
    hbm = pl.BlockSpec(memory_space=pltpu.HBM)
    vmem = pl.BlockSpec(memory_space=VMEM)
    return pl.pallas_call(
        gather_kernel,
        out_shape=(
            pltpu.HBM((TARGETS * LEAF, 256), BF16),
            pltpu.VMEM((BLOCKS, 4 * DIM, BLOCK), BF16),
            pltpu.VMEM((BLOCKS, 1, BLOCK), F32),
            pltpu.HBM((BLOCKS, BLOCK, 2 * WCOL), BF16),
            jax.ShapeDtypeStruct((SPOTS, 8, 128), jnp.int32),
        ),
        in_specs=[hbm] * 3 + [vmem] * 2,
        out_specs=[hbm, vmem, vmem, hbm, vmem],
        scratch_shapes=[
            VMEM((TARGETS * LEAF, 256), BF16),
            VMEM((BLOCKS, BLOCK, 2 * WCOL), BF16),
            VMEM((PAYLOAD, 128), F32),
            VMEM((SPOTS, PAYLOAD, 128), F32),
            VMEM((DIM, MINE * LEAF), F32),
            VMEM((DIM, COLPTS), F32),
            VMEM((DIM, COLPTS), F32),
            VMEM((COLPTS, WCOL), F32),
            VMEM((COLPTS, WCOL), F32),
            VMEM((2, SKEL, CHUNK), F32),
            VMEM((DIM, SKEL), F32),
            VMEM((DIM, SKEL), F32),
            VMEM((SKEL, WCOL), F32),
            VMEM((SKEL, WCOL), F32),
            pltpu.SemaphoreType.DMA((4, 15)),
            pltpu.SemaphoreType.DMA((4, 16)),
            pltpu.SemaphoreType.DMA((4,)),
            pltpu.SemaphoreType.DMA((4,)),
            pltpu.SemaphoreType.DMA((6,)),
            pltpu.SemaphoreType.DMA((MINE, SPOTS)),
        ],
        compiler_params=pltpu.CompilerParams(
            collective_id=0, has_side_effects=True, vmem_limit_bytes=K1_VMEM
        ),
    )(points, weights, proj, index, table)


def produce(left, right, norm, at, block, width, high_ref, low_ref):
    blocks = range(width // BLOCK)
    columns = jnp.concatenate([right[block + n] for n in blocks], axis=1)
    norms = jnp.concatenate([norm[block + n] for n in blocks], axis=1)
    power = mm(left[pl.ds(at, LEAF), :], columns) + norms
    high_ref[:, :width], low_ref[:, :width] = split2(jnp.exp2(power))


def consume(wcat, out, at, block, width, high_ref, low_ref):
    rows = jnp.concatenate([wcat[block + n] for n in range(width // BLOCK)], axis=0)
    total = mm(high_ref[:, :width], rows)
    rest = mm(low_ref[:, :width], rows[:, :WCOL])
    out[pl.ds(at, LEAF), :] += total[:, :WCOL] + total[:, WCOL:] + rest


def near_start(source):
    return source * (LEAF // BLOCK)


def far_start(node):
    return 2 * COLPTS // BLOCK + node


def pair_kernel(
    spot_ref, table, left_hbm, right, norm, wcat_hbm, out, extra_hbm, slots,
    even, even_low, odd, odd_low, left, wcat, extra, near_pairs, far_pairs, near_extra, far_extra, packed, packed_smem, sem,
):
    first = pl.ds(0, SPOTS * LEAF)
    later = pl.ds(SPOTS * LEAF, LATER * LEAF)
    loads = [
        pltpu.make_async_copy(wcat_hbm, wcat, sem.at[0]),
        pltpu.make_async_copy(left_hbm.at[later], left.at[later], sem.at[1]),
        pltpu.make_async_copy(left_hbm.at[first], left.at[first], sem.at[2]),
    ]
    for c in loads:
        c.start()

    def clear(ref, n):
        def zero(t, _):
            ref[pl.ds(pl.multiple_of(t * LEAF, LEAF), LEAF), :] = jnp.zeros((LEAF, WCOL), F32)
            return _

        lax.fori_loop(0, n, zero, 0)

    spot = spot_ref[0]
    lane = lax.broadcasted_iota(jnp.int32, (8, 128), 1)
    lists_here = jnp.full((8, 128), -1, jnp.int32)
    for n in range(SPOTS):
        near = pltpu.roll(table[n], (8 * n - 4 * spot + 128) % 128, 1)
        far = pltpu.roll(table[n], (8 * n + 4 + 64 - 2 * spot) % 128, 1)
        at = lane - 8 * n
        lists_here = jnp.where(jnp.logical_and(at >= 0, at < 4), near, lists_here)
        lists_here = jnp.where(jnp.logical_and(at >= 4, at < 6), far, lists_here)
    packed[...] = lists_here
    to_smem = pltpu.make_async_copy(packed, packed_smem, sem.at[4])
    to_smem.start()
    clear(out, SPOTS + 1)
    clear(extra, LATER + 1)
    to_smem.wait()

    def used(t, slot):
        return packed_smem[t // SPOTS, 8 * (t % SPOTS) + slot]

    def note(t, counts):
        near, far = counts
        for slot in range(4):
            source = used(t, slot)
            near_pairs[near] = t * 64 + source
            near = near + jnp.where(source >= 0, 1, 0)
        for slot in range(2):
            node = used(t, 4 + slot)
            far_pairs[far] = t * 64 + node
            far = far + jnp.where(node >= 0, 1, 0)
        return near, far

    near_count, far_count = lax.fori_loop(0, SPOTS, note, (0, 0))

    def note_later(t, counts):
        near, far = counts
        slots[t, 0] = IDLE // LEAF
        have = 0
        for slot in range(4):
            source = used(t + SPOTS, slot)
            hit = source >= 0
            take = jnp.logical_and(hit, have < 1)
            slots[t, jnp.where(take, 0, 7)] = source
            have = have + jnp.where(take, 1, 0)
            near_extra[near] = t * 64 + source
            near = near + jnp.where(jnp.logical_and(hit, jnp.logical_not(take)), 1, 0)
        for slot in range(2):
            node = used(t + SPOTS, 4 + slot)
            far_extra[far] = t * 64 + node
            far = far + jnp.where(node >= 0, 1, 0)
        return near, far

    near_more, far_more = lax.fori_loop(0, LATER, note_later, (0, 0))
    for n in range(3):
        near_pairs[near_count + n] = SPOTS * 64
        far_pairs[far_count + n] = SPOTS * 64
        near_extra[near_more + n] = LATER * 64
        far_extra[far_more + n] = LATER * 64

    def run(pair_list, count, start_of, width, ref, n_targets, base):
        def make(n, high_ref, low_ref):
            code = pair_list[n]
            t = code // 64
            at = pl.multiple_of((base + jnp.where(t < n_targets, t, 0)) * LEAF, LEAF)
            produce(left, right, norm, at, start_of(code % 64), width, high_ref, low_ref)

        def use(n, high_ref, low_ref):
            code = pair_list[n]
            at = pl.multiple_of((code // 64) * LEAF, LEAF)
            consume(wcat, ref, at, start_of(code % 64), width, high_ref, low_ref)

        make(0, even, even_low)

        def two(m, _):
            make(2 * m + 1, odd, odd_low)
            use(2 * m, even, even_low)
            make(2 * m + 2, even, even_low)
            use(2 * m + 1, odd, odd_low)
            return _

        lax.fori_loop(0, (count + 1) // 2, two, 0)

    loads[0].wait()
    loads[1].wait()
    run(near_extra, near_more, near_start, LEAF, extra, LATER, SPOTS)
    run(far_extra, far_more, far_start, SKEL, extra, LATER, SPOTS)
    handed = pltpu.make_async_copy(extra.at[pl.ds(0, LATER * LEAF)], extra_hbm, sem.at[3])
    handed.start()
    loads[2].wait()
    run(near_pairs, near_count, near_start, LEAF, out, SPOTS, 0)
    run(far_pairs, far_count, far_start, SKEL, out, SPOTS, 0)
    handed.wait()


def pairs(spot, table, left, right, norm, wcat):
    smem = pl.BlockSpec(memory_space=pltpu.SMEM)
    vmem = pl.BlockSpec(memory_space=VMEM)
    hbm = pl.BlockSpec(memory_space=pltpu.HBM)
    return pl.pallas_call(
        pair_kernel,
        out_shape=(
            pltpu.VMEM(((SPOTS + 1) * LEAF, WCOL), F32),
            pltpu.HBM((LATER * LEAF, WCOL), F32),
            jax.ShapeDtypeStruct((LATER, 8), jnp.int32),
        ),
        in_specs=[smem, vmem, hbm, vmem, vmem, hbm],
        out_specs=(vmem, hbm, smem),
        scratch_shapes=[VMEM((LEAF, LEAF), BF16)] * 4
        + [
            VMEM((TARGETS * LEAF, 256), BF16),
            VMEM((BLOCKS, BLOCK, 2 * WCOL), BF16),
            VMEM(((LATER + 1) * LEAF, WCOL), F32),
            pltpu.SMEM((SPOTS * 4 + 3,), jnp.int32),
            pltpu.SMEM((SPOTS * 2 + 3,), jnp.int32),
            pltpu.SMEM((LATER * 4 + 3,), jnp.int32),
            pltpu.SMEM((LATER * 2 + 3,), jnp.int32),
            VMEM((8, 128), jnp.int32),
            pltpu.SMEM((8, 128), jnp.int32),
            pltpu.SemaphoreType.DMA((5,)),
        ],
        compiler_params=pltpu.CompilerParams(vmem_limit_bytes=K2_VMEM),
    )(spot, table, left, right, norm, wcat)


QUARTER = LEAF // 4


def scatter_kernel(
    chosen, partial, extra_hbm, left_hbm, right, norm, wcat_hbm, out,
    slots, turn, sums, left, wcat, even, even_low, odd, odd_low,
    send, recv, turn_send, turn_recv, y_send, y_recv, load_sem,
):
    around = Around()
    y = around.y
    loads = [
        pltpu.make_async_copy(left_hbm.at[pl.ds(SPOTS * LEAF, LATER * LEAF)], left, load_sem.at[0]),
        pltpu.make_async_copy(wcat_hbm, wcat, load_sem.at[1]),
        pltpu.make_async_copy(extra_hbm, sums, load_sem.at[2]),
    ]
    for c in loads:
        c.start()
    planes = [lax.rem(y + a, SIDE) for a in range(SIDE)]
    here = around.spots[0, 0] * 2 + around.core
    above, below = (planes[1], here), (planes[3], here)
    greet(list(around.devices.values()) + [above, below])
    started = []

    def own(k, leaf, first, second):
        place_of = around.spot(k, first, second) + (0 if leaf == 0 else (leaf - 1) * SPOTS)
        rows = pl.ds(pl.multiple_of(place_of * LEAF + k * QUARTER, QUARTER), QUARTER)
        return partial.at[rows] if leaf == 0 else sums.at[rows]

    def begin(make):
        make().start()
        started.append(make)

    def step_first(k, leaf, step, j, source):
        n = (leaf * 3 + step) * SIDE + j

        def make():
            return pltpu.make_async_remote_copy(
                src_ref=source(), dst_ref=slots.at[k, n], send_sem=send.at[k, n], recv_sem=recv.at[k, n],
                device_id=around.next(k, True), device_id_type=MESH,
            )

        begin(make)

    def arrived_first(k, leaf, step, j):
        n = (leaf * 3 + step) * SIDE + j
        pltpu.make_async_copy(slots.at[k, n], slots.at[k, n], recv.at[k, n]).wait()
        slots[k, n] += own(k, leaf, 2 - step, 3 - j)[...]
        return n

    def step_second(k, leaf, step, source):
        n = leaf * 3 + step

        def make():
            return pltpu.make_async_remote_copy(
                src_ref=source(), dst_ref=turn.at[k, n], send_sem=turn_send.at[k, n], recv_sem=turn_recv.at[k, n],
                device_id=around.next(k, False), device_id_type=MESH,
            )

        begin(make)

    def rows_of(plane, leaf, k):
        return pl.ds(pl.multiple_of((plane * MINE + leaf) * LEAF + k * QUARTER, QUARTER), QUARTER)

    def to_y(leaf, k, number, plane, up):
        n = (leaf * 4 + k) * 3 + number

        def make():
            rows = rows_of(plane, leaf, k)
            return pltpu.make_async_remote_copy(
                src_ref=out.at[rows], dst_ref=out.at[rows], send_sem=y_send.at[n], recv_sem=y_recv.at[n],
                device_id=above if up else below, device_id_type=MESH,
            )

        begin(make)

    def y_wait(leaf, k, number, plane):
        rows = rows_of(plane, leaf, k)
        n = (leaf * 4 + k) * 3 + number
        pltpu.make_async_copy(out.at[rows], out.at[rows], y_recv.at[n]).wait()

    def second_axis(k, leaf, j):
        n = arrived_first(k, leaf, 2, j)
        if j > 0:
            m = leaf * 3 + j - 1
            pltpu.make_async_copy(turn.at[k, m], turn.at[k, m], turn_recv.at[k, m]).wait()
        if j == 0:
            step_second(k, leaf, 0, lambda: slots.at[k, n])
        elif j < 3:
            turn[k, m] += slots[k, n]
            step_second(k, leaf, j, lambda: turn.at[k, m])
        else:
            out[rows_of(y, leaf, k), :] = turn[k, m] + slots[k, n]
            to_y(leaf, k, 0, y, True)
            to_y(leaf, k, 1, y, False)

    def second_hop(leaf, k):
        lower, upper = planes[3], planes[1]
        if k % 2 == 0:
            y_wait(leaf, k, 0, lower)
            to_y(leaf, k, 2, lower, True)
        else:
            y_wait(leaf, k, 1, upper)
            to_y(leaf, k, 2, upper, False)

    def last_arrivals(leaf, k):
        lower, upper, across = planes[3], planes[1], planes[2]
        if k % 2 == 0:
            y_wait(leaf, k, 1, upper)
        else:
            y_wait(leaf, k, 0, lower)
        y_wait(leaf, k, 2, across)

    def start_leaf(leaf):
        for j in range(SIDE):
            for k in range(4):
                step_first(k, leaf, 0, j, functools.partial(own, k, leaf, 3, 3 - j))

    def part(leaf, n):
        j = n % SIDE
        for k in range(4):
            if leaf < MINE:
                m = arrived_first(k, leaf, n // SIDE, j)
                step_first(k, leaf, 1 + n // SIDE, j, lambda k=k, m=m: slots.at[k, m])
            if leaf > 0 and n < SIDE:
                second_axis(k, leaf - 1, j)

    def make(t, high_ref, low_ref):
        at = pl.multiple_of(t * LEAF, LEAF)
        produce(left, right, norm, at, near_start(chosen[t, 0]), LEAF, high_ref, low_ref)

    def use(t, high_ref, low_ref):
        at = pl.multiple_of(t * LEAF, LEAF)
        consume(wcat, sums, at, near_start(chosen[t, 0]), LEAF, high_ref, low_ref)

    def two_targets(t):
        make(t + 1, odd, odd_low)
        use(t, even, even_low)
        make((t + 2) % LATER, even, even_low)
        use(t + 1, odd, odd_low)

    for leaf in range(MINE + 1):
        if leaf < MINE:
            start_leaf(leaf)
        begun = 0
        if leaf == 0:
            begun = 2
            for n in range(begun):
                part(leaf, n)
            for c in loads:
                c.wait()
            make(0, even, even_low)
        if leaf < MINE - 1:

            def step(n, _, leaf=leaf, begun=begun):
                two_targets(leaf * SPOTS + 2 * n)
                for which in range(begun, 2 * SIDE):
                    pl.when(n == which)(functools.partial(part, leaf, which))
                return _

            lax.fori_loop(0, 2 * SIDE, step, 0)
        else:
            for n in range(2 * SIDE):
                part(leaf, n)
        if leaf > 0:
            for k in range(4):
                second_hop(leaf - 1, k)
    for leaf in range(MINE):
        for k in range(4):
            last_arrivals(leaf, k)
    for again in started:
        again().wait_send()


def scatter(chosen, partial, extra, left, right, norm, wcat):
    smem = pl.BlockSpec(memory_space=pltpu.SMEM)
    vmem = pl.BlockSpec(memory_space=VMEM)
    hbm = pl.BlockSpec(memory_space=pltpu.HBM)
    return pl.pallas_call(
        scatter_kernel,
        out_shape=jax.ShapeDtypeStruct((COLPTS, WCOL), F32),
        in_specs=[smem, vmem, hbm, hbm, vmem, vmem, hbm],
        out_specs=vmem,
        scratch_shapes=[
            VMEM((4, MINE * 3 * SIDE, QUARTER, WCOL), F32),
            VMEM((4, MINE * 3, QUARTER, WCOL), F32),
            VMEM((LATER * LEAF, WCOL), F32),
            VMEM((LATER * LEAF, 256), BF16),
            VMEM((BLOCKS, BLOCK, 2 * WCOL), BF16),
        ]
        + [VMEM((LEAF, LEAF), BF16)] * 4
        + [
            pltpu.SemaphoreType.DMA((4, MINE * 3 * SIDE)),
            pltpu.SemaphoreType.DMA((4, MINE * 3 * SIDE)),
            pltpu.SemaphoreType.DMA((4, MINE * 3)),
            pltpu.SemaphoreType.DMA((4, MINE * 3)),
            pltpu.SemaphoreType.DMA((MINE * 4 * 3,)),
            pltpu.SemaphoreType.DMA((MINE * 4 * 3,)),
            pltpu.SemaphoreType.DMA((3,)),
        ],
        compiler_params=pltpu.CompilerParams(
            collective_id=1, has_side_effects=True, vmem_limit_bytes=K3_VMEM
        ),
    )(chosen, partial, extra, left, right, norm, wcat)


def lists(y, core, fetch_table, near_list, far_list):
    near = lax.dynamic_slice_in_dim(near_list, y * MINE, MINE, 0)
    far = lax.dynamic_slice_in_dim(far_list, y * MINE, MINE, 0)
    slots = jnp.arange(64, dtype=jnp.int32)
    nodes = jnp.arange(32, dtype=jnp.int32)
    near_used = jnp.any(near[:, :, None] == slots, axis=1)
    far_used = jnp.any(far[:, :, None] == nodes, axis=1)
    rows = (y * MINE + jnp.arange(MINE, dtype=jnp.int32)) // 4
    requests = fetch_table[:, 0].reshape(3, 64)
    local = jnp.sum(jnp.where(rows[:, None, None] == jnp.arange(3)[None, :, None], requests[None], 0), axis=1)
    side = (slots // 2 + core) % 2
    near_value = jnp.where(near_used, side * LEAVES + local, -1)
    far_value = jnp.where(far_used, (nodes + core) % 2, -1)
    table = jnp.concatenate([near_value, far_value, jnp.full((MINE, 32), -1, jnp.int32)], axis=1)
    return jnp.pad(table, ((0, 8 - MINE), (0, 0))).astype(F32)


def on_device(points, weights, proj, fetch_table, near_list, far_list, skel_idx):
    y, z, x, core = place()
    table = lists(y, core, fetch_table, near_list, far_list)
    fixed = pltpu.with_memory_space_constraint
    points, weights, proj = (fixed(a, pltpu.HBM) for a in (points, weights, proj))
    left, right, norm, wcat, found = gather(points, weights, proj, skel_idx, table)
    spot = (z * SIDE + x).reshape(1).astype(jnp.int32)
    left, wcat = fixed(left, pltpu.HBM), fixed(wcat, pltpu.HBM)
    right, norm = fixed(right, VMEM), fixed(norm, VMEM)
    partial, extra, chosen = pairs(spot, found, left, right, norm, wcat)
    return scatter(chosen, fixed(partial, VMEM), fixed(extra, pltpu.HBM), left, right, norm, wcat)


def solution(mesh):
    placed = (
        P(None, "dev"),
        P("dev", None),
        P(None, "dev"),
        P(None, "dev", None, None),
        P("dev", None),
        P("dev", None),
        P("dev", None),
    )
    return jax.shard_map(
        on_device, mesh=mesh, in_specs=placed, out_specs=P("dev", None), check_vma=False
    )
```

```python
import functools
import math

import jax
import jax.numpy as jnp
from jax import lax
from jax.experimental import pallas as pl
from jax.experimental.pallas import tpu as pltpu
from jax.sharding import PartitionSpec as P

F32, BF16 = jnp.float32, jnp.bfloat16
MESH = pl.DeviceIdType.MESH
VMEM = pltpu.VMEM
LOG2E = math.log2(math.e)
SIDE = 4
SPOTS = SIDE * SIDE
LEAF, DIM, WCOL, SKEL = 512, 64, 128, 256
LEAVES = 12
MINE = 3
COLPTS = LEAVES * LEAF
HALF = LEAF // 2
PAYLOAD = MINE * HALF + 8
TARGETS = SPOTS * MINE
IDLE = 2 * COLPTS + 2 * SKEL
SOURCES = IDLE + LEAF
BLOCK = 256
BLOCKS = SOURCES // BLOCK
LATER = (MINE - 1) * SPOTS
CHUNK = 1024
SCALE = LOG2E / 32.0
K1_VMEM, K2_VMEM, K3_VMEM = 44 << 20, 32 << 20, 38 << 20
CUTS = (0, 192, 384, 576, PAYLOAD)


def mm(a, b):
    return jnp.dot(a, b, preferred_element_type=F32)


def split2(v):
    high = v.astype(BF16)
    return high, (v - high.astype(F32)).astype(BF16)


def place():
    y, dev = lax.axis_index("grp"), lax.axis_index("dev")
    return y, lax.div(dev, 8), lax.rem(lax.div(dev, 2), SIDE), lax.rem(dev, 2)


def shift(k, first, second):
    sign = 1 if k % 2 == 0 else -1
    along_x, along_z = (first, second) if k < 2 else (second, first)
    return sign * along_z % SIDE, sign * along_x % SIDE


class Around:
    def __init__(self):
        self.y, self.z, self.x, self.core = place()
        zs = [lax.rem(self.z + a, SIDE) for a in range(SIDE)]
        xs = [lax.rem(self.x + a, SIDE) for a in range(SIDE)]
        self.spots = {(a, b): zs[a] * SIDE + xs[b] for a in range(SIDE) for b in range(SIDE)}
        self.devices = {
            (a, b): (self.y, self.spots[a, b] * 2 + self.core) for a, b in ((1, 0), (3, 0), (0, 1), (0, 3))
        }
        self.sibling = (self.y, self.spots[0, 0] * 2 + 1 - self.core)

    def spot(self, k, first, second):
        return self.spots[shift(k, first, second)]

    def next(self, k, along_first):
        return self.devices[shift(k, 1, 0) if along_first else shift(k, 0, 1)]


def greet(peers):
    barrier = pltpu.get_barrier_semaphore()
    for peer in peers:
        pl.semaphore_signal(barrier, inc=1, device_id=peer, device_id_type=MESH)
    pl.semaphore_wait(barrier, len(peers))


def put_source(block, right, norm, first):
    high, low = split2(block * (2.0 * SCALE))
    total = -SCALE * jnp.sum(block * block, axis=0, keepdims=True)
    for n in range(block.shape[1] // BLOCK):
        cols = slice(n * BLOCK, (n + 1) * BLOCK)
        right[first + n, 0:DIM, :] = high[:, cols]
        right[first + n, DIM : 2 * DIM, :] = high[:, cols]
        right[first + n, 2 * DIM : 3 * DIM, :] = low[:, cols]
        right[first + n, 3 * DIM : 4 * DIM, :] = jnp.full((DIM, BLOCK), -1.0, BF16)
        norm[first + n] = total[:, cols]


def put_weights(block, wcat, first):
    high, low = split2(block)
    for n in range(block.shape[0] // BLOCK):
        rows = slice(n * BLOCK, (n + 1) * BLOCK)
        wcat[first + n, :, 0:WCOL] = high[rows]
        wcat[first + n, :, WCOL : 2 * WCOL] = low[rows]


def put_target(both, left, at):
    lane = lax.broadcasted_iota(jnp.int32, both.shape, 1)
    first_half = lane < DIM
    first_quarter = lane % DIM < DIM // 2
    high = both.astype(BF16).astype(F32)
    low = both - high
    high_r, low_r = pltpu.roll(high, DIM, 1), pltpu.roll(low, DIM, 1)
    square = both * both * SCALE
    down = square + pltpu.roll(square, 32, 1)
    up = square + pltpu.roll(square, 96, 1)
    up_high = up.astype(BF16).astype(F32)
    down_low = down - down.astype(BF16).astype(F32)
    sums = jnp.where(first_quarter, up_high, down_low)
    left[pl.ds(at, HALF), 0:128] = jnp.where(first_half, high, low_r).astype(BF16)
    left[pl.ds(at, HALF), 128:256] = jnp.where(first_half, high, pltpu.roll(sums, DIM, 1)).astype(BF16)
    left[pl.ds(at + HALF, HALF), 0:128] = jnp.where(first_half, high_r, low).astype(BF16)
    left[pl.ds(at + HALF, HALF), 128:256] = jnp.where(first_half, high_r, sums).astype(BF16)


def gather_kernel(
    points_hbm, weights_hbm, proj_hbm, index, table,
    left_hbm, right, norm, wcat_hbm, found,
    left, wcat, payload, gathered, own, points, points2, weights, weights2, proj, coords, coords2, values, values2,
    send, recv, pair_send, pair_recv, load_sem, left_sem,
):
    around = Around()
    y = around.y
    loads = [
        pltpu.make_async_copy(
            points_hbm.at[:, pl.ds(pl.multiple_of(y * (MINE * LEAF), LEAF), MINE * LEAF)], own, load_sem.at[0]
        ),
        pltpu.make_async_copy(points_hbm, points, load_sem.at[1]),
        pltpu.make_async_copy(weights_hbm, weights, load_sem.at[2]),
    ]

    def proj_load(n):
        at = pl.multiple_of(n * CHUNK, CHUNK)
        return pltpu.make_async_copy(proj_hbm.at[:, pl.ds(at, CHUNK)], proj.at[n % 2], load_sem.at[3 + n % 2])

    for c in loads:
        c.start()
    proj_load(0).start()
    greet(list(around.devices.values()) + [around.sibling])

    loads[0].wait()
    for leaf in range(MINE):
        block = own[:, leaf * LEAF : (leaf + 1) * LEAF]
        packed = jnp.concatenate([block[:, :HALF], block[:, HALF:]], axis=0)
        payload[leaf * HALF : (leaf + 1) * HALF, :] = packed.T
    payload[MINE * HALF :, :] = table[...]

    started, swaps, handed = [], [], []

    def spot_of(k, i, j):
        return around.spot(k, -i, -j)

    def copy(k, i, j, first):
        rows = pl.ds(CUTS[k], CUTS[k + 1] - CUTS[k])
        arrival = (i + 1) * SIDE + j if first else i * SIDE + j + 1
        number = i if first else SIDE - 1 + i * (SIDE - 1) + j
        target = gathered.at[spot_of(k, i, j), rows]
        c = pltpu.make_async_remote_copy(
            src_ref=payload.at[rows] if i == 0 and j == 0 else target,
            dst_ref=target,
            send_sem=send.at[k, number],
            recv_sem=recv.at[k, arrival],
            device_id=around.next(k, first),
            device_id_type=MESH,
        )
        c.start()
        started.append(c)

    def forward(level):
        for i in range(SIDE):
            j = level - i
            if not 0 <= j < SIDE:
                continue
            for k in range(4):
                if level > 0:
                    rows = pl.ds(CUTS[k], CUTS[k + 1] - CUTS[k])
                    here = gathered.at[spot_of(k, i, j), rows]
                    pltpu.make_async_copy(here, here, recv.at[k, i * SIDE + j]).wait()
                if j == 0 and i < SIDE - 1:
                    copy(k, i, j, True)
                if j < SIDE - 1:
                    copy(k, i, j, False)

    def swap(n, a, b):
        c = pltpu.make_async_remote_copy(
            src_ref=a, dst_ref=b, send_sem=pair_send.at[n], recv_sem=pair_recv.at[n],
            device_id=around.sibling, device_id_type=MESH,
        )
        c.start()
        swaps.append(c)

    def targets_at(dz, dx):
        spot = around.spots[dz, dx]

        def leaf_rows(leaf, _):
            rows = pl.ds(pl.multiple_of(leaf * HALF, HALF), HALF)
            both = payload[rows, :] if dz == dx == 0 else gathered[spot, rows, :]
            put_target(both, left, pl.multiple_of((leaf * SPOTS + spot) * LEAF, LEAF))
            return _

        lax.fori_loop(0, MINE, leaf_rows, 0)
        lists_here = payload[MINE * HALF :, :] if dz == dx == 0 else gathered[spot, MINE * HALF :, :]
        found[spot] = lists_here.astype(jnp.int32)
        for leaf in range(MINE):
            rows = pl.ds(pl.multiple_of((leaf * SPOTS + spot) * LEAF, LEAF), LEAF)
            c = pltpu.make_async_copy(left.at[rows], left_hbm.at[rows], left_sem.at[leaf, dz * SIDE + dx])
            c.start()
            handed.append(c)

    def column(points_ref, weights_ref, base):
        def one(n, _):
            at = pl.multiple_of(n * LEAF, LEAF)
            put_source(points_ref[:, pl.ds(at, LEAF)], right, norm, base + 2 * n)
            put_weights(weights_ref[pl.ds(at, LEAF), :], wcat, base + 2 * n)
            return _

        lax.fori_loop(0, LEAVES, one, 0)

    def spots_of(level):
        steps = (0, 1, 2, 3)

        def done(dz, dx):
            far = lambda d: max(d, (SIDE - d) % SIDE)
            return far(dz) + far(dx)

        return [(dz, dx) for dz in steps for dx in steps if done(dz, dx) == level]

    forward(0)
    loads[1].wait()
    loads[2].wait()
    swap(0, points, points2)
    swap(1, weights, weights2)
    targets_at(0, 0)
    for n in range(IDLE // BLOCK, BLOCKS):
        right[n] = jnp.zeros((4 * DIM, BLOCK), BF16)
        norm[n] = jnp.zeros((1, BLOCK), F32)
        wcat[n] = jnp.zeros((BLOCK, 2 * WCOL), BF16)
    column(points, weights, 0)
    forward(1)
    values[...] = jnp.zeros_like(values)
    coords[...] = jnp.zeros_like(coords)

    def skeleton(n, _):
        proj_load(n).wait()

        @pl.when(n + 1 < COLPTS // CHUNK)
        def next_load():
            proj_load(n + 1).start()

        at = pl.multiple_of(n * CHUNK, CHUNK)
        four = pl.ds(n * (CHUNK // BLOCK), CHUNK // BLOCK)
        wh, wl = wcat[four, :, 0:WCOL].reshape(CHUNK, WCOL), wcat[four, :, WCOL : 2 * WCOL].reshape(CHUNK, WCOL)
        ph, plow = split2(proj[n % 2])
        values[...] += mm(ph, wh) + mm(ph, wl) + mm(plow, wh)
        rows = lax.broadcasted_iota(jnp.int32, (CHUNK, SKEL), 0) + at
        pick = jnp.where(rows == index[...], 1.0, 0.0).astype(BF16)
        block = points[:, pl.ds(at, CHUNK)]
        first = block.astype(BF16)
        second, third = split2(block - first.astype(F32))
        coords[...] += mm(first, pick) + mm(second, pick) + mm(third, pick)
        return _

    lax.fori_loop(0, COLPTS // CHUNK // 2, skeleton, 0)
    forward(2)
    lax.fori_loop(COLPTS // CHUNK // 2, COLPTS // CHUNK, skeleton, 0)
    swap(2, coords, coords2)
    swap(3, values, values2)
    put_source(coords[...], right, norm, 2 * COLPTS // BLOCK)
    put_weights(values[...], wcat, 2 * COLPTS // BLOCK)
    swaps[0].wait_recv()
    swaps[1].wait_recv()
    column(points2, weights2, COLPTS // BLOCK)
    forward(3)
    swaps[2].wait_recv()
    swaps[3].wait_recv()
    put_source(coords2[...], right, norm, (2 * COLPTS + SKEL) // BLOCK)
    put_weights(values2[...], wcat, (2 * COLPTS + SKEL) // BLOCK)
    handed.append(pltpu.make_async_copy(wcat, wcat_hbm, load_sem.at[5]))
    handed[-1].start()
    for level in (2, 3):
        for dz, dx in spots_of(level):
            targets_at(dz, dx)
    for level in (4, 5, 6):
        forward(level)
        for dz, dx in spots_of(level):
            targets_at(dz, dx)
    for c in started + swaps:
        c.wait_send()
    for c in handed:
        c.wait()


def gather(points, weights, proj, index, table):
    hbm = pl.BlockSpec(memory_space=pltpu.HBM)
    vmem = pl.BlockSpec(memory_space=VMEM)
    return pl.pallas_call(
        gather_kernel,
        out_shape=(
            pltpu.HBM((TARGETS * LEAF, 256), BF16),
            pltpu.VMEM((BLOCKS, 4 * DIM, BLOCK), BF16),
            pltpu.VMEM((BLOCKS, 1, BLOCK), F32),
            pltpu.HBM((BLOCKS, BLOCK, 2 * WCOL), BF16),
            jax.ShapeDtypeStruct((SPOTS, 8, 128), jnp.int32),
        ),
        in_specs=[hbm] * 3 + [vmem] * 2,
        out_specs=[hbm, vmem, vmem, hbm, vmem],
        scratch_shapes=[
            VMEM((TARGETS * LEAF, 256), BF16),
            VMEM((BLOCKS, BLOCK, 2 * WCOL), BF16),
            VMEM((PAYLOAD, 128), F32),
            VMEM((SPOTS, PAYLOAD, 128), F32),
            VMEM((DIM, MINE * LEAF), F32),
            VMEM((DIM, COLPTS), F32),
            VMEM((DIM, COLPTS), F32),
            VMEM((COLPTS, WCOL), F32),
            VMEM((COLPTS, WCOL), F32),
            VMEM((2, SKEL, CHUNK), F32),
            VMEM((DIM, SKEL), F32),
            VMEM((DIM, SKEL), F32),
            VMEM((SKEL, WCOL), F32),
            VMEM((SKEL, WCOL), F32),
            pltpu.SemaphoreType.DMA((4, 15)),
            pltpu.SemaphoreType.DMA((4, 16)),
            pltpu.SemaphoreType.DMA((4,)),
            pltpu.SemaphoreType.DMA((4,)),
            pltpu.SemaphoreType.DMA((6,)),
            pltpu.SemaphoreType.DMA((MINE, SPOTS)),
        ],
        compiler_params=pltpu.CompilerParams(
            collective_id=0, has_side_effects=True, vmem_limit_bytes=K1_VMEM
        ),
    )(points, weights, proj, index, table)


def produce(left, right, norm, at, block, width, high_ref, low_ref):
    blocks = range(width // BLOCK)
    columns = jnp.concatenate([right[block + n] for n in blocks], axis=1)
    norms = jnp.concatenate([norm[block + n] for n in blocks], axis=1)
    power = mm(left[pl.ds(at, LEAF), :], columns) + norms
    high_ref[:, :width], low_ref[:, :width] = split2(jnp.exp2(power))


def consume(wcat, out, at, block, width, high_ref, low_ref):
    rows = jnp.concatenate([wcat[block + n] for n in range(width // BLOCK)], axis=0)
    total = mm(high_ref[:, :width], rows)
    rest = mm(low_ref[:, :width], rows[:, :WCOL])
    out[pl.ds(at, LEAF), :] += total[:, :WCOL] + total[:, WCOL:] + rest


def near_start(source):
    return source * (LEAF // BLOCK)


def far_start(node):
    return 2 * COLPTS // BLOCK + node


def pair_kernel(
    spot_ref, table, left_hbm, right, norm, wcat_hbm, out, extra_hbm, slots,
    even, even_low, odd, odd_low, left, wcat, extra, near_pairs, far_pairs, near_extra, far_extra, packed, packed_smem, sem,
):
    first = pl.ds(0, SPOTS * LEAF)
    later = pl.ds(SPOTS * LEAF, LATER * LEAF)
    loads = [
        pltpu.make_async_copy(wcat_hbm, wcat, sem.at[0]),
        pltpu.make_async_copy(left_hbm.at[later], left.at[later], sem.at[1]),
        pltpu.make_async_copy(left_hbm.at[first], left.at[first], sem.at[2]),
    ]
    for c in loads:
        c.start()

    def clear(ref, n):
        def zero(t, _):
            ref[pl.ds(pl.multiple_of(t * LEAF, LEAF), LEAF), :] = jnp.zeros((LEAF, WCOL), F32)
            return _

        lax.fori_loop(0, n, zero, 0)

    spot = spot_ref[0]
    lane = lax.broadcasted_iota(jnp.int32, (8, 128), 1)
    lists_here = jnp.full((8, 128), -1, jnp.int32)
    for n in range(SPOTS):
        near = pltpu.roll(table[n], (8 * n - 4 * spot + 128) % 128, 1)
        far = pltpu.roll(table[n], (8 * n + 4 + 64 - 2 * spot) % 128, 1)
        at = lane - 8 * n
        lists_here = jnp.where(jnp.logical_and(at >= 0, at < 4), near, lists_here)
        lists_here = jnp.where(jnp.logical_and(at >= 4, at < 6), far, lists_here)
    packed[...] = lists_here
    to_smem = pltpu.make_async_copy(packed, packed_smem, sem.at[4])
    to_smem.start()
    clear(out, SPOTS + 1)
    clear(extra, LATER + 1)
    to_smem.wait()

    def used(t, slot):
        return packed_smem[t // SPOTS, 8 * (t % SPOTS) + slot]

    def note(t, counts):
        near, far = counts
        for slot in range(4):
            source = used(t, slot)
            near_pairs[near] = t * 64 + source
            near = near + jnp.where(source >= 0, 1, 0)
        for slot in range(2):
            node = used(t, 4 + slot)
            far_pairs[far] = t * 64 + node
            far = far + jnp.where(node >= 0, 1, 0)
        return near, far

    near_count, far_count = lax.fori_loop(0, SPOTS, note, (0, 0))

    def note_later(t, counts):
        near, far = counts
        slots[t, 0] = IDLE // LEAF
        have = 0
        for slot in range(4):
            source = used(t + SPOTS, slot)
            hit = source >= 0
            take = jnp.logical_and(hit, have < 1)
            slots[t, jnp.where(take, 0, 7)] = source
            have = have + jnp.where(take, 1, 0)
            near_extra[near] = t * 64 + source
            near = near + jnp.where(jnp.logical_and(hit, jnp.logical_not(take)), 1, 0)
        for slot in range(2):
            node = used(t + SPOTS, 4 + slot)
            far_extra[far] = t * 64 + node
            far = far + jnp.where(node >= 0, 1, 0)
        return near, far

    near_more, far_more = lax.fori_loop(0, LATER, note_later, (0, 0))
    for n in range(3):
        near_pairs[near_count + n] = SPOTS * 64
        far_pairs[far_count + n] = SPOTS * 64
        near_extra[near_more + n] = LATER * 64
        far_extra[far_more + n] = LATER * 64

    def run(pair_list, count, start_of, width, ref, n_targets, base):
        def make(n, high_ref, low_ref):
            code = pair_list[n]
            t = code // 64
            at = pl.multiple_of((base + jnp.where(t < n_targets, t, 0)) * LEAF, LEAF)
            produce(left, right, norm, at, start_of(code % 64), width, high_ref, low_ref)

        def use(n, high_ref, low_ref):
            code = pair_list[n]
            at = pl.multiple_of((code // 64) * LEAF, LEAF)
            consume(wcat, ref, at, start_of(code % 64), width, high_ref, low_ref)

        make(0, even, even_low)

        def two(m, _):
            make(2 * m + 1, odd, odd_low)
            use(2 * m, even, even_low)
            make(2 * m + 2, even, even_low)
            use(2 * m + 1, odd, odd_low)
            return _

        lax.fori_loop(0, (count + 1) // 2, two, 0)

    loads[0].wait()
    loads[1].wait()
    run(near_extra, near_more, near_start, LEAF, extra, LATER, SPOTS)
    run(far_extra, far_more, far_start, SKEL, extra, LATER, SPOTS)
    handed = pltpu.make_async_copy(extra.at[pl.ds(0, LATER * LEAF)], extra_hbm, sem.at[3])
    handed.start()
    loads[2].wait()
    run(near_pairs, near_count, near_start, LEAF, out, SPOTS, 0)
    run(far_pairs, far_count, far_start, SKEL, out, SPOTS, 0)
    handed.wait()


def pairs(spot, table, left, right, norm, wcat):
    smem = pl.BlockSpec(memory_space=pltpu.SMEM)
    vmem = pl.BlockSpec(memory_space=VMEM)
    hbm = pl.BlockSpec(memory_space=pltpu.HBM)
    return pl.pallas_call(
        pair_kernel,
        out_shape=(
            pltpu.VMEM(((SPOTS + 1) * LEAF, WCOL), F32),
            pltpu.HBM((LATER * LEAF, WCOL), F32),
            jax.ShapeDtypeStruct((LATER, 8), jnp.int32),
        ),
        in_specs=[smem, vmem, hbm, vmem, vmem, hbm],
        out_specs=(vmem, hbm, smem),
        scratch_shapes=[VMEM((LEAF, LEAF), BF16)] * 4
        + [
            VMEM((TARGETS * LEAF, 256), BF16),
            VMEM((BLOCKS, BLOCK, 2 * WCOL), BF16),
            VMEM(((LATER + 1) * LEAF, WCOL), F32),
            pltpu.SMEM((SPOTS * 4 + 3,), jnp.int32),
            pltpu.SMEM((SPOTS * 2 + 3,), jnp.int32),
            pltpu.SMEM((LATER * 4 + 3,), jnp.int32),
            pltpu.SMEM((LATER * 2 + 3,), jnp.int32),
            VMEM((8, 128), jnp.int32),
            pltpu.SMEM((8, 128), jnp.int32),
            pltpu.SemaphoreType.DMA((5,)),
        ],
        compiler_params=pltpu.CompilerParams(vmem_limit_bytes=K2_VMEM),
    )(spot, table, left, right, norm, wcat)


QUARTER = LEAF // 4


def scatter_kernel(
    chosen, partial, extra_hbm, left_hbm, right, norm, wcat_hbm, out,
    slots, turn, sums, left, wcat, even, even_low, odd, odd_low,
    send, recv, turn_send, turn_recv, y_send, y_recv, load_sem,
):
    around = Around()
    y = around.y
    loads = [
        pltpu.make_async_copy(left_hbm.at[pl.ds(SPOTS * LEAF, LATER * LEAF)], left, load_sem.at[0]),
        pltpu.make_async_copy(wcat_hbm, wcat, load_sem.at[1]),
        pltpu.make_async_copy(extra_hbm, sums, load_sem.at[2]),
    ]
    for c in loads:
        c.start()
    planes = [lax.rem(y + a, SIDE) for a in range(SIDE)]
    here = around.spots[0, 0] * 2 + around.core
    above, below = (planes[1], here), (planes[3], here)
    greet(list(around.devices.values()) + [above, below])
    started = []

    def own(k, leaf, first, second):
        place_of = around.spot(k, first, second) + (0 if leaf == 0 else (leaf - 1) * SPOTS)
        rows = pl.ds(pl.multiple_of(place_of * LEAF + k * QUARTER, QUARTER), QUARTER)
        return partial.at[rows] if leaf == 0 else sums.at[rows]

    def begin(make):
        make().start()
        started.append(make)

    def step_first(k, leaf, step, j, source):
        n = (leaf * 3 + step) * SIDE + j

        def make():
            return pltpu.make_async_remote_copy(
                src_ref=source(), dst_ref=slots.at[k, n], send_sem=send.at[k, n], recv_sem=recv.at[k, n],
                device_id=around.next(k, True), device_id_type=MESH,
            )

        begin(make)

    def arrived_first(k, leaf, step, j):
        n = (leaf * 3 + step) * SIDE + j
        pltpu.make_async_copy(slots.at[k, n], slots.at[k, n], recv.at[k, n]).wait()
        slots[k, n] += own(k, leaf, 2 - step, 3 - j)[...]
        return n

    def step_second(k, leaf, step, source):
        n = leaf * 3 + step

        def make():
            return pltpu.make_async_remote_copy(
                src_ref=source(), dst_ref=turn.at[k, n], send_sem=turn_send.at[k, n], recv_sem=turn_recv.at[k, n],
                device_id=around.next(k, False), device_id_type=MESH,
            )

        begin(make)

    def rows_of(plane, leaf, k):
        return pl.ds(pl.multiple_of((plane * MINE + leaf) * LEAF + k * QUARTER, QUARTER), QUARTER)

    def to_y(leaf, k, number, plane, up):
        n = (leaf * 4 + k) * 3 + number

        def make():
            rows = rows_of(plane, leaf, k)
            return pltpu.make_async_remote_copy(
                src_ref=out.at[rows], dst_ref=out.at[rows], send_sem=y_send.at[n], recv_sem=y_recv.at[n],
                device_id=above if up else below, device_id_type=MESH,
            )

        begin(make)

    def y_wait(leaf, k, number, plane):
        rows = rows_of(plane, leaf, k)
        n = (leaf * 4 + k) * 3 + number
        pltpu.make_async_copy(out.at[rows], out.at[rows], y_recv.at[n]).wait()

    def second_axis(k, leaf, j):
        n = arrived_first(k, leaf, 2, j)
        if j > 0:
            m = leaf * 3 + j - 1
            pltpu.make_async_copy(turn.at[k, m], turn.at[k, m], turn_recv.at[k, m]).wait()
        if j == 0:
            step_second(k, leaf, 0, lambda: slots.at[k, n])
        elif j < 3:
            turn[k, m] += slots[k, n]
            step_second(k, leaf, j, lambda: turn.at[k, m])
        else:
            out[rows_of(y, leaf, k), :] = turn[k, m] + slots[k, n]
            to_y(leaf, k, 0, y, True)
            to_y(leaf, k, 1, y, False)

    def second_hop(leaf, k):
        lower, upper = planes[3], planes[1]
        if k % 2 == 0:
            y_wait(leaf, k, 0, lower)
            to_y(leaf, k, 2, lower, True)
        else:
            y_wait(leaf, k, 1, upper)
            to_y(leaf, k, 2, upper, False)

    def last_arrivals(leaf, k):
        lower, upper, across = planes[3], planes[1], planes[2]
        if k % 2 == 0:
            y_wait(leaf, k, 1, upper)
        else:
            y_wait(leaf, k, 0, lower)
        y_wait(leaf, k, 2, across)

    def start_leaf(leaf):
        for j in range(SIDE):
            for k in range(4):
                step_first(k, leaf, 0, j, functools.partial(own, k, leaf, 3, 3 - j))

    def part(leaf, n):
        j = n % SIDE
        for k in range(4):
            if leaf < MINE:
                m = arrived_first(k, leaf, n // SIDE, j)
                step_first(k, leaf, 1 + n // SIDE, j, lambda k=k, m=m: slots.at[k, m])
            if leaf > 0 and n < SIDE:
                second_axis(k, leaf - 1, j)

    def make(t, high_ref, low_ref):
        at = pl.multiple_of(t * LEAF, LEAF)
        produce(left, right, norm, at, near_start(chosen[t, 0]), LEAF, high_ref, low_ref)

    def use(t, high_ref, low_ref):
        at = pl.multiple_of(t * LEAF, LEAF)
        consume(wcat, sums, at, near_start(chosen[t, 0]), LEAF, high_ref, low_ref)

    def two_targets(t):
        make(t + 1, odd, odd_low)
        use(t, even, even_low)
        make((t + 2) % LATER, even, even_low)
        use(t + 1, odd, odd_low)

    for leaf in range(MINE + 1):
        if leaf < MINE:
            start_leaf(leaf)
        if leaf == 0:
            for c in loads:
                c.wait()
            make(0, even, even_low)
        if leaf < MINE - 1:

            def step(n, _, leaf=leaf):
                two_targets(leaf * SPOTS + 2 * n)
                for which in range(2 * SIDE):
                    pl.when(n == which)(functools.partial(part, leaf, which))
                return _

            lax.fori_loop(0, 2 * SIDE, step, 0)
        else:
            for n in range(2 * SIDE):
                part(leaf, n)
        if leaf > 0:
            for k in range(4):
                second_hop(leaf - 1, k)
    for leaf in range(MINE):
        for k in range(4):
            last_arrivals(leaf, k)
    for again in started:
        again().wait_send()


def scatter(chosen, partial, extra, left, right, norm, wcat):
    smem = pl.BlockSpec(memory_space=pltpu.SMEM)
    vmem = pl.BlockSpec(memory_space=VMEM)
    hbm = pl.BlockSpec(memory_space=pltpu.HBM)
    return pl.pallas_call(
        scatter_kernel,
        out_shape=jax.ShapeDtypeStruct((COLPTS, WCOL), F32),
        in_specs=[smem, vmem, hbm, hbm, vmem, vmem, hbm],
        out_specs=vmem,
        scratch_shapes=[
            VMEM((4, MINE * 3 * SIDE, QUARTER, WCOL), F32),
            VMEM((4, MINE * 3, QUARTER, WCOL), F32),
            VMEM((LATER * LEAF, WCOL), F32),
            VMEM((LATER * LEAF, 256), BF16),
            VMEM((BLOCKS, BLOCK, 2 * WCOL), BF16),
        ]
        + [VMEM((LEAF, LEAF), BF16)] * 4
        + [
            pltpu.SemaphoreType.DMA((4, MINE * 3 * SIDE)),
            pltpu.SemaphoreType.DMA((4, MINE * 3 * SIDE)),
            pltpu.SemaphoreType.DMA((4, MINE * 3)),
            pltpu.SemaphoreType.DMA((4, MINE * 3)),
            pltpu.SemaphoreType.DMA((MINE * 4 * 3,)),
            pltpu.SemaphoreType.DMA((MINE * 4 * 3,)),
            pltpu.SemaphoreType.DMA((3,)),
        ],
        compiler_params=pltpu.CompilerParams(
            collective_id=1, has_side_effects=True, vmem_limit_bytes=K3_VMEM
        ),
    )(chosen, partial, extra, left, right, norm, wcat)


def lists(y, core, fetch_table, near_list, far_list):
    near = lax.dynamic_slice_in_dim(near_list, y * MINE, MINE, 0)
    far = lax.dynamic_slice_in_dim(far_list, y * MINE, MINE, 0)
    slots = jnp.arange(64, dtype=jnp.int32)
    nodes = jnp.arange(32, dtype=jnp.int32)
    near_used = jnp.any(near[:, :, None] == slots, axis=1)
    far_used = jnp.any(far[:, :, None] == nodes, axis=1)
    rows = (y * MINE + jnp.arange(MINE, dtype=jnp.int32)) // 4
    requests = fetch_table[:, 0].reshape(3, 64)
    local = jnp.sum(jnp.where(rows[:, None, None] == jnp.arange(3)[None, :, None], requests[None], 0), axis=1)
    side = (slots // 2 + core) % 2
    near_value = jnp.where(near_used, side * LEAVES + local, -1)
    far_value = jnp.where(far_used, (nodes + core) % 2, -1)
    table = jnp.concatenate([near_value, far_value, jnp.full((MINE, 32), -1, jnp.int32)], axis=1)
    return jnp.pad(table, ((0, 8 - MINE), (0, 0))).astype(F32)


def on_device(points, weights, proj, fetch_table, near_list, far_list, skel_idx):
    y, z, x, core = place()
    table = lists(y, core, fetch_table, near_list, far_list)
    fixed = pltpu.with_memory_space_constraint
    points, weights, proj = (fixed(a, pltpu.HBM) for a in (points, weights, proj))
    left, right, norm, wcat, found = gather(points, weights, proj, skel_idx, table)
    spot = (z * SIDE + x).reshape(1).astype(jnp.int32)
    left, wcat = fixed(left, pltpu.HBM), fixed(wcat, pltpu.HBM)
    right, norm = fixed(right, VMEM), fixed(norm, VMEM)
    partial, extra, chosen = pairs(spot, found, left, right, norm, wcat)
    return scatter(chosen, fixed(partial, VMEM), fixed(extra, pltpu.HBM), left, right, norm, wcat)


def solution(mesh):
    placed = (
        P(None, "dev"),
        P("dev", None),
        P(None, "dev"),
        P(None, "dev", None, None),
        P("dev", None),
        P("dev", None),
        P("dev", None),
    )
    return jax.shard_map(
        on_device, mesh=mesh, in_specs=placed, out_specs=P("dev", None), check_vma=False
    )
```
